128 devices in a mesh: wide: 16 (over y, x), narrow: 8 (over z, core).
Axes of the slice: x: 4, y: 4, z: 4, core: 2. Of those that a mesh axis runs over, the one named last changes fastest.
Arguments:
- tokens: int32 [4, 384], replicated, may hold values from 0 to 32
- segments: int32 [4, 384], replicated, may hold values from 0 to 5
- targets: int32 [4, 384, 384], P(None, 'wide', 'narrow'), may hold values from 0 to 63
- embed: float32 [33, 1024], P(None, ('wide', 'narrow')), may hold values from -6 to 6
- w_ab: float32 [1024, 64], P(('wide', 'narrow')), may hold values from -0.1875 to 0.1875
- w_outer: float32 [1024, 128], P(('wide', 'narrow')), may hold values from -0.1875 to 0.1875
- w_tri: float32 [128, 640], P(('wide', 'narrow')), may hold values from -0.5 to 0.5
- w_mix: float32 [128, 128], P(('wide', 'narrow')), may hold values from -0.5 to 0.5
- w_dist: float32 [128, 64], P(('wide', 'narrow')), may hold values from -0.5 to 0.5
- gains: float32 [2, 128], P(None, ('wide', 'narrow')), may hold values from 0.5 to 1.5
- m_embed: float32 [33, 1024], P(None, ('wide', 'narrow')), may hold values from -2.861023e-06 to 2.861023e-06
- m_ab: float32 [1024, 64], P(('wide', 'narrow')), may hold values from -2.861023e-06 to 2.861023e-06
- m_outer: float32 [1024, 128], P(('wide', 'narrow')), may hold values from -2.861023e-06 to 2.861023e-06
- m_tri: float32 [128, 640], P(('wide', 'narrow')), may hold values from -2.861023e-06 to 2.861023e-06
- m_mix: float32 [128, 128], P(('wide', 'narrow')), may hold values from -2.861023e-06 to 2.861023e-06
- m_dist: float32 [128, 64], P(('wide', 'narrow')), may hold values from -2.861023e-06 to 2.861023e-06
- m_gains: float32 [2, 128], P(None, ('wide', 'narrow')), may hold values from -1.5258789e-05 to 1.5258789e-05
- v_embed: float32 [33, 1024], P(None, ('wide', 'narrow')), may hold values from 4e-17 to 3.2e-16
- v_ab: float32 [1024, 64], P(('wide', 'narrow')), may hold values from 1.5e-15 to 1.2e-14
- v_outer: float32 [1024, 128], P(('wide', 'narrow')), may hold values from 1.5e-15 to 1.2e-14
- v_tri: float32 [128, 640], P(('wide', 'narrow')), may hold values from 1.5e-15 to 1.2e-14
- v_mix: float32 [128, 128], P(('wide', 'narrow')), may hold values from 1.5e-15 to 1.2e-14
- v_dist: float32 [128, 64], P(('wide', 'narrow')), may hold values from 1.5e-15 to 1.2e-14
- v_gains: float32 [2, 128], P(None, ('wide', 'narrow')), may hold values from 3e-14 to 2.4e-13
Outputs:
- loss_sum: float32 [], replicated
- pair_count: float32 [], replicated
- grad_norm: float32 [], replicated
- new_embed: float32 [33, 1024], P(None, ('wide', 'narrow'))
- new_ab: float32 [1024, 64], P(('wide', 'narrow'))
- new_outer: float32 [1024, 128], P(('wide', 'narrow'))
- new_tri: float32 [128, 640], P(('wide', 'narrow'))
- new_mix: float32 [128, 128], P(('wide', 'narrow'))
- new_dist: float32 [128, 64], P(('wide', 'narrow'))
- new_gains: float32 [2, 128], P(None, ('wide', 'narrow'))
- out_m_embed: float32 [33, 1024], P(None, ('wide', 'narrow'))
- out_m_ab: float32 [1024, 64], P(('wide', 'narrow'))
- out_m_outer: float32 [1024, 128], P(('wide', 'narrow'))
- out_m_tri: float32 [128, 640], P(('wide', 'narrow'))
- out_m_mix: float32 [128, 128], P(('wide', 'narrow'))
- out_m_dist: float32 [128, 64], P(('wide', 'narrow'))
- out_m_gains: float32 [2, 128], P(None, ('wide', 'narrow'))
- out_v_embed: float32 [33, 1024], P(None, ('wide', 'narrow'))
- out_v_ab: float32 [1024, 64], P(('wide', 'narrow'))
- out_v_outer: float32 [1024, 128], P(('wide', 'narrow'))
- out_v_tri: float32 [128, 640], P(('wide', 'narrow'))
- out_v_mix: float32 [128, 128], P(('wide', 'narrow'))
- out_v_dist: float32 [128, 64], P(('wide', 'narrow'))
- out_v_gains: float32 [2, 128], P(None, ('wide', 'narrow'))
The draws below stay inside these ranges and needn't reach their ends.
Inputs may be any that keep to these rules, and one draw needn't show every extreme that they name: `segments`: residues of one protein may stand anywhere in the crop.
All inputs are finite; a program needn't handle non-finite values.
Results may differ from the reference program's by a relative error of at most 0.0059.
Values may be sent and summed in bfloat16 or wider, within the bound.
A program may use at most 128 MiB of HBM per device.

```python
import math
import jax
import jax.numpy as jnp
from jax import lax

C_S = 1024
C_Z = 128
C_TRI = 128
C_OP = 32
BINS = 64
VOCAB = 33
L = 384
SEG_COUNT = 6
CROPS = 4


def plant(values, stream_key, least, top_value):
    spot = [jax.random.randint(jax.random.fold_in(stream_key, axis), (), 0, length) for axis, length in enumerate(values.shape)]
    widest = values.shape.index(max(values.shape))
    next_to = spot[:widest] + [(spot[widest] + 1) % values.shape[widest]] + spot[widest + 1:]
    return values.at[tuple(spot)].set(least).at[tuple(next_to)].set(top_value)


def levels(key, dims, pieces, least, high):
    loudness, own = 1.0, jax.random.fold_in(key, 6)
    for dim, parts in pieces:
        heights = jnp.exp(jax.random.uniform(jax.random.fold_in(own, dim), (parts,), jnp.float32, least / len(pieces), high / len(pieces)))
        loudness = loudness * jnp.repeat(heights, dims[dim] // parts).reshape([-1 if axis == dim else 1 for axis in range(len(dims))])
    return loudness


def centred(key, extent, deviation, reach, cuts=(), kind=jnp.bfloat16):
    level = levels(key, extent, cuts, -0.22, 0.18) if cuts else 1.0
    array = jax.random.normal(key, extent, jnp.float32) * deviation * level
    return jnp.minimum(jnp.maximum(array, -reach), reach).astype(kind)


def setup_inputs(seed: int = 0) -> dict:
    seeds = jax.random.split(jax.random.key(seed), 25)
    tokens = plant(jax.random.randint(seeds[0], (CROPS, L), 0, VOCAB), jax.random.fold_in(seeds[0], 1), 0, VOCAB - 1).astype(jnp.int32)
    segments = plant(jax.random.randint(seeds[1], (CROPS, L), 0, SEG_COUNT), jax.random.fold_in(seeds[1], 1), 0, SEG_COUNT - 1).astype(jnp.int32)
    targets = plant(jax.random.randint(seeds[2], (CROPS, L, L), 0, BINS), jax.random.fold_in(seeds[2], 1), 0, BINS - 1).astype(jnp.int32)
    embed = centred(seeds[3], (VOCAB, C_S), 1.0, 6.0, ((1, 128),), jnp.float32)
    w_ab = centred(seeds[4], (C_S, 2 * C_OP), C_S ** -0.5, 0.1875, ((0, 128),), jnp.float32)
    w_outer = centred(seeds[5], (C_OP * C_OP, C_Z), (C_OP * C_OP) ** -0.5, 0.1875, ((0, 128),), jnp.float32)
    w_tri = centred(seeds[6], (C_Z, 4 * C_TRI + C_Z), C_Z ** -0.5, 0.5, ((0, 128),), jnp.float32)
    w_mix = centred(seeds[7], (C_TRI, C_Z), C_TRI ** -0.5, 0.5, ((0, 128),), jnp.float32)
    w_dist = centred(seeds[8], (C_Z, BINS), C_Z ** -0.5, 0.5, ((0, 128),), jnp.float32)
    gains = jnp.clip(1.0 + 0.1 * jax.random.normal(seeds[9], (2, C_Z), jnp.float32), 0.5, 1.5)
    m_embed = centred(seeds[10], (VOCAB, C_S), (2e-7), 2.86102294921875e-06, ((1, 128),), jnp.float32)
    m_ab = centred(seeds[11], (C_S, 2 * C_OP), (2e-7), 2.86102294921875e-06, ((0, 128),), jnp.float32)
    m_outer = centred(seeds[12], (C_OP * C_OP, C_Z), (2e-7), 2.86102294921875e-06, ((0, 128),), jnp.float32)
    m_tri = centred(seeds[13], (C_Z, 4 * C_TRI + C_Z), (2e-7), 2.86102294921875e-06, ((0, 128),), jnp.float32)
    m_mix = centred(seeds[14], (C_TRI, C_Z), (2e-7), 2.86102294921875e-06, ((0, 128),), jnp.float32)
    m_dist = centred(seeds[15], (C_Z, BINS), (2e-7), 2.86102294921875e-06, ((0, 128),), jnp.float32)
    m_gains = centred(seeds[16], (2, C_Z), (1e-6), 1.52587890625e-05, ((1, 128),), jnp.float32)
    v_embed = jnp.clip(jnp.exp(math.log(3.199999948080509e-16) - 2.0794415 * jax.random.uniform(seeds[17], (VOCAB, C_S), jnp.float32) ** levels(seeds[17], (VOCAB, C_S), ((1, 128),), -0.2, 0.2)), 3.999999935100636e-17, 3.199999948080509e-16)
    v_ab = jnp.clip(jnp.exp(math.log(1.1999999620013451e-14) - 2.0794415 * jax.random.uniform(seeds[18], (C_S, 2 * C_OP), jnp.float32) ** levels(seeds[18], (C_S, 2 * C_OP), ((0, 128),), -0.2, 0.2)), 1.4999999525016814e-15, 1.1999999620013451e-14)
    v_outer = jnp.clip(jnp.exp(math.log(1.1999999620013451e-14) - 2.0794415 * jax.random.uniform(seeds[19], (C_OP * C_OP, C_Z), jnp.float32) ** levels(seeds[19], (C_OP * C_OP, C_Z), ((0, 128),), -0.2, 0.2)), 1.4999999525016814e-15, 1.1999999620013451e-14)
    v_tri = jnp.clip(jnp.exp(math.log(1.1999999620013451e-14) - 2.0794415 * jax.random.uniform(seeds[20], (C_Z, 4 * C_TRI + C_Z), jnp.float32) ** levels(seeds[20], (C_Z, 4 * C_TRI + C_Z), ((0, 128),), -0.2, 0.2)), 1.4999999525016814e-15, 1.1999999620013451e-14)
    v_mix = jnp.clip(jnp.exp(math.log(1.1999999620013451e-14) - 2.0794415 * jax.random.uniform(seeds[21], (C_TRI, C_Z), jnp.float32) ** levels(seeds[21], (C_TRI, C_Z), ((0, 128),), -0.2, 0.2)), 1.4999999525016814e-15, 1.1999999620013451e-14)
    v_dist = jnp.clip(jnp.exp(math.log(1.1999999620013451e-14) - 2.0794415 * jax.random.uniform(seeds[22], (C_Z, BINS), jnp.float32) ** levels(seeds[22], (C_Z, BINS), ((0, 128),), -0.2, 0.2)), 1.4999999525016814e-15, 1.1999999620013451e-14)
    v_gains = jnp.clip(jnp.exp(math.log(2.399999957884008e-13) - 2.0794415 * jax.random.uniform(seeds[23], (2, C_Z), jnp.float32) ** levels(seeds[23], (2, C_Z), ((1, 128),), -0.2, 0.2)), 2.99999994735501e-14, 2.399999957884008e-13)
    return {"tokens": tokens, "segments": segments, "targets": targets, "embed": embed, "w_ab": w_ab, "w_outer": w_outer, "w_tri": w_tri, "w_mix": w_mix, "w_dist": w_dist, "gains": gains, "m_embed": m_embed, "m_ab": m_ab, "m_outer": m_outer, "m_tri": m_tri, "m_mix": m_mix, "m_dist": m_dist, "m_gains": m_gains, "v_embed": v_embed, "v_ab": v_ab, "v_outer": v_outer, "v_tri": v_tri, "v_mix": v_mix, "v_dist": v_dist, "v_gains": v_gains}


@jax.custom_vjp
def low(v):
    return lax.optimization_barrier(v.astype(jnp.bfloat16)).astype(jnp.float32)

@jax.custom_vjp
def low_back(v):
    return v

def low_keep(v):
    return (low(v), None)

def low_pass(kept, grad):
    return (grad,)

def back_keep(v):
    return (v, None)

def back_low(kept, grad):
    return (low(grad),)
low.defvjp(low_keep, low_pass)
low_back.defvjp(back_keep, back_low)
norm_eps = 1e-05
clip_level = 0.001
beta_one = 0.9
beta_two = 0.999
adam_eps = 1e-10
decay_rate = 0.01
step_count = 10.0
rates = (0.5, 0.016, 0.016, 0.044, 0.044, 0.044, 0.5)

def layer_norm(values, gain):
    center = values - lax.optimization_barrier(jnp.mean(values, -1, keepdims=True))
    spread = lax.optimization_barrier(jnp.mean(center * center, -1, keepdims=True))
    return center * lax.rsqrt(spread + norm_eps) * gain

def crop_loss(params, tok, seg, tgt, count):
    embed, w_ab, w_outer, w_tri, w_mix, w_dist, gains = params
    highest = lax.Precision.HIGHEST
    one_hot = (tok[:, None] == jnp.arange(VOCAB)[None, :]).astype(jnp.float32)
    seq = jnp.dot(one_hot, embed, precision=highest)
    factors = low(jnp.dot(seq, w_ab, precision=highest))
    left = factors[:, :C_OP]
    right = factors[:, C_OP:]
    inner = low(jnp.dot(left, w_outer.reshape(C_OP, C_OP * C_Z), precision=highest)).reshape(L, C_OP, C_Z)
    mask = (seg[:, None] == seg[None, :]).astype(jnp.float32)
    mask3 = mask[..., None]
    pair = jnp.einsum('jq,iqc->ijc', right, inner, precision=highest) * mask3
    normed = low(layer_norm(pair, gains[0]))
    projected = low_back(jnp.einsum('ijc,cd->ijd', normed, w_tri, precision=highest))
    gate_left = projected[..., :C_TRI]
    value_left = projected[..., C_TRI:2 * C_TRI]
    gate_right = projected[..., 2 * C_TRI:3 * C_TRI]
    value_right = projected[..., 3 * C_TRI:4 * C_TRI]
    gate_out = projected[..., 4 * C_TRI:]
    left_edge = low(mask3 * jax.nn.sigmoid(gate_left) * value_left)
    right_edge = low(mask3 * jax.nn.sigmoid(gate_right) * value_right)
    product = low_back(jnp.einsum('ikc,jkc->ijc', left_edge, right_edge, precision=highest))
    mixed = low(layer_norm(product, gains[1]))
    branch = low_back(jnp.einsum('ijc,cd->ijd', mixed, w_mix, precision=highest))
    update = pair + jax.nn.sigmoid(gate_out) * branch
    logits = low_back(jnp.einsum('ijc,ck->ijk', low(update), w_dist, precision=highest))
    log_prob = jax.nn.log_softmax(logits, -1)
    picked = jnp.take_along_axis(log_prob, tgt[..., None], -1)[..., 0]
    return -jnp.sum(mask * picked) / count

def reference(tokens, segments, targets, embed, w_ab, w_outer, w_tri, w_mix, w_dist, gains, m_embed, m_ab, m_outer, m_tri, m_mix, m_dist, m_gains, v_embed, v_ab, v_outer, v_tri, v_mix, v_dist, v_gains):
    masters = (embed, w_ab, w_outer, w_tri, w_mix, w_dist, gains)
    firsts = (m_embed, m_ab, m_outer, m_tri, m_mix, m_dist, m_gains)
    seconds = (v_embed, v_ab, v_outer, v_tri, v_mix, v_dist, v_gains)
    same = (segments[:, :, None] == segments[:, None, :]).astype(jnp.float32)
    count = jnp.sum(same)

    def objective(weights):
        params = tuple((low(w) for w in weights))

        def one_crop(inputs):
            return crop_loss(params, inputs[0], inputs[1], inputs[2], count)
        return jnp.sum(lax.map(jax.checkpoint(one_crop), (tokens, segments, targets)))
    loss, pull = jax.vjp(objective, masters)
    grads = pull(jnp.ones((), jnp.float32))[0]
    loss_sum = loss * count
    grad_norm = jnp.sqrt(sum((jnp.sum(g * g) for g in grads)))
    scale = jnp.minimum(1.0, clip_level / grad_norm)
    news, moms, vels = ([], [], [])
    for weight, first, second, grad, rate in zip(masters, firsts, seconds, grads, rates):
        clipped = grad * scale
        first_new = beta_one * first + (1.0 - beta_one) * clipped
        second_new = beta_two * second + (1.0 - beta_two) * clipped * clipped
        ratio = first_new / (1.0 - beta_one ** step_count) / (jnp.sqrt(second_new / (1.0 - beta_two ** step_count)) + adam_eps)
        news.append(weight - rate * (ratio + decay_rate * weight))
        moms.append(first_new)
        vels.append(second_new)
    return (loss_sum, count, grad_norm, news[0], news[1], news[2], news[3], news[4], news[5], news[6], moms[0], moms[1], moms[2], moms[3], moms[4], moms[5], moms[6], vels[0], vels[1], vels[2], vels[3], vels[4], vels[5], vels[6])
```

```python
import functools

import jax
import jax.numpy as jnp
from jax import lax
from jax.experimental import pallas as pl
from jax.experimental.pallas import tpu as pltpu
from jax.sharding import PartitionSpec as P

norm_eps = 1e-05
clip_level = 0.001
beta_one = 0.9
beta_two = 0.999
adam_eps = 1e-10
decay_rate = 0.01
step_count = 10.0
rates = (0.5, 0.016, 0.016, 0.044, 0.044, 0.044, 0.5)

f32 = jnp.float32
bf16 = jnp.bfloat16
MESH = pl.DeviceIdType.MESH
VMEM = pltpu.VMEM
LIMIT = 56 * 1024 * 1024

vocab = 33
tokens_padded = 40
table = tokens_padded * tokens_padded
own_rows = 12
bins = 64
narrow_size = 8
wide_size = 16
length = 384


def dot(a, b, axis_a, axis_b, precision=None):
    return lax.dot_general(
        a, b, (((axis_a,), (axis_b,)), ((), ())), precision=precision, preferred_element_type=f32
    )


def rounded(values):
    return values.astype(bf16).astype(f32)


def greet(wide, narrow):
    barrier = pltpu.get_barrier_semaphore()
    for k in range(1, narrow_size):
        peer = lax.rem(narrow + k, narrow_size)
        pl.semaphore_signal(barrier, inc=1, device_id=(wide, peer), device_id_type=MESH)
    for k in range(1, wide_size):
        peer = lax.rem(wide + k, wide_size)
        pl.semaphore_signal(barrier, inc=1, device_id=(peer, narrow), device_id_type=MESH)
    pl.semaphore_wait(barrier, narrow_size + wide_size - 2)


def gather_kernel(
    tgt, emb, ab, outer, tri, mix, dist, gain,
    g_out, t_out, tgt_out,
    pack, tstage, stage, taken, part, taken_t, source, source_t, taken_w,
    send_a, recv_a, send_t, recv_t, send_b, recv_b, send_u, recv_u,
):
    wide = lax.axis_index("wide")
    narrow = lax.axis_index("narrow")
    greet(wide, narrow)
    pack[...] = jnp.zeros_like(pack)
    pack[0:8, :] = outer[...]
    for m in range(5):
        pack[8 + m : 9 + m, :] = tri[:, 128 * m : 128 * m + 128]
    pack[13:14, :] = mix[...]
    pack[14:15, 0:64] = dist[...]
    pack[14:15, 64:66] = gain[...]
    low = pack[...].astype(bf16)
    tstage[...] = jnp.zeros_like(tstage)
    for m in range(narrow_size):
        start = 8 * (m % 2)
        tstage[m, :, 0:48] = tgt[m // 2, start : start + 16, :].astype(f32)
        stage[m, 0:16, :] = low
        stage[m, 16:32, :] = tstage[m].astype(bf16)
    part[...] = jnp.zeros_like(part)
    part[0:vocab, 0:64] = dot(emb[...].astype(bf16), ab[...].astype(bf16), 0, 0)

    copies = []
    for k in range(1, narrow_size):
        peer = lax.rem(narrow + k, narrow_size)
        copies.append(
            pltpu.make_async_remote_copy(
                src_ref=stage.at[peer], dst_ref=taken.at[narrow],
                send_sem=send_a.at[k], recv_sem=recv_a.at[k],
                device_id=(wide, peer), device_id_type=MESH,
            )
        )
        copies.append(
            pltpu.make_async_remote_copy(
                src_ref=part, dst_ref=taken_t.at[narrow],
                send_sem=send_t.at[k], recv_sem=recv_t.at[k],
                device_id=(wide, peer), device_id_type=MESH,
            )
        )
    for copy in copies:
        copy.start()
    taken[narrow] = stage[narrow]
    taken_t[narrow] = part[...]
    for copy in copies:
        copy.wait()
    total = taken_t[0]
    for m in range(1, narrow_size):
        total = total + taken_t[m]
    source_t[...] = total
    for m in range(narrow_size):
        source[16 * m : 16 * m + 16, :] = taken[m, 0:16, :]
        tgt_out[m] = taken[m, 16:32, :]

    place = pl.ds(pl.multiple_of(wide * 128, 128), 128)
    copies = []
    for k in range(1, wide_size):
        peer = lax.rem(wide + k, wide_size)
        copies.append(
            pltpu.make_async_remote_copy(
                src_ref=source_t, dst_ref=taken_w.at[wide],
                send_sem=send_u.at[k], recv_sem=recv_u.at[k],
                device_id=(peer, narrow), device_id_type=MESH,
            )
        )
        copies.append(
            pltpu.make_async_remote_copy(
                src_ref=source, dst_ref=g_out.at[place],
                send_sem=send_b.at[k], recv_sem=recv_b.at[k],
                device_id=(peer, narrow), device_id_type=MESH,
            )
        )
    for copy in copies:
        copy.start()
    g_out[place, :] = source[...]
    taken_w[wide] = source_t[...]
    for copy in copies:
        copy.wait()
    total = taken_w[0]
    for m in range(1, wide_size):
        total = total + taken_w[m]
    t_out[...] = total


def class_kernel(
    tok_s, seg_s, tok_v, seg_v, tgt, gathered, factors,
    grads_out, d_out,
    weights, tg, u, z, xhat, rstd, zn, sa, pa, sb, pb, ta, tb, sgo,
    hist, many, wa, zi, so, x, dx, dgo, dz1, ga, gb, go, gz, dp, dz, du, grads,
):
    wide = lax.axis_index("wide")
    narrow = lax.axis_index("narrow")
    crop = narrow // 2
    half = lax.rem(narrow, 2)
    row0 = wide * 24 + half * own_rows
    rows = tokens_padded

    weights[...] = gathered[...].astype(f32)
    factor = factors[...].astype(bf16)
    a = factor[:, 0:32]
    b = factor[:, 32:64]
    w_outer = jnp.concatenate(
        [weights[pl.ds(16 * (q // 8) + q % 8, 32, stride=64), :] for q in range(32)], axis=1
    ).astype(bf16)
    w_tri = jnp.concatenate(
        [weights[pl.ds(8 + m, 128, stride=16), :] for m in range(5)], axis=1
    ).astype(bf16)
    w_mix = weights[pl.ds(13, 128, stride=16), :].astype(bf16)
    tail_t = weights[pl.ds(14, 128, stride=16), :].T
    dist_t = tail_t[0:bins, :].astype(bf16)
    gain_in = tail_t[64:65, :]
    gain_mid = tail_t[65:66, :]

    u_q = rounded(dot(a, w_outer, 1, 0))
    for q in range(32):
        u[pl.ds(q, rows, stride=32), :] = u_q[:, 128 * q : 128 * q + 128]
    u_cat = jnp.concatenate([u[32 * t : 32 * t + 32, :] for t in range(rows)], axis=1).astype(bf16)
    z_cat = dot(b, u_cat, 1, 0)
    for t in range(rows):
        z[rows * t : rows * t + rows, :] = z_cat[:, 128 * t : 128 * t + 128]

    chunk = 160

    def forward(step, carry):
        at = pl.ds(pl.multiple_of(step * chunk, chunk), chunk)
        values = z[at, :]
        center = values - jnp.mean(values, -1, keepdims=True)
        inverse = lax.rsqrt(jnp.mean(center * center, -1, keepdims=True) + norm_eps)
        scaled = center * inverse
        normed = (scaled * gain_in).astype(bf16)
        xhat[at, :] = scaled
        rstd[at, :] = jnp.broadcast_to(inverse, scaled.shape)
        zn[at, :] = normed
        projected = dot(normed, w_tri, 1, 0)
        gate = jax.nn.sigmoid(projected[:, 0:128])
        value = projected[:, 128:256]
        sa[at, :] = gate
        pa[at, :] = value
        ta[at, :] = rounded(gate * value)
        gate = jax.nn.sigmoid(projected[:, 256:384])
        value = projected[:, 384:512]
        sb[at, :] = gate
        pb[at, :] = value
        tb[at, :] = rounded(gate * value)
        sgo[at, :] = jax.nn.sigmoid(projected[:, 512:640])
        return carry

    lax.fori_loop(0, table // chunk, forward, 0)

    count = jnp.zeros((4, 1), f32)
    for s in range(6):
        members = jnp.sum((seg_v[...] == s).astype(f32), axis=1, keepdims=True)
        count = count + members * members
    count = jnp.sum(count, axis=0, keepdims=True)

    for m in range(narrow_size):
        tg[:, 48 * m : 48 * m + 48] = tgt[m].astype(f32)[:, 0:48]
    tok_row = tok_v[pl.ds(crop, 1), :]
    seg_row = seg_v[pl.ds(crop, 1), :]
    hot = (lax.broadcasted_iota(jnp.int32, (rows, length), 0) == tok_row).astype(f32).astype(bf16)
    bin_of = lax.broadcasted_iota(jnp.int32, (bins, length), 0).astype(f32)
    starts = []
    for i in range(own_rows):
        kind = tok_s[crop, row0 + i]
        start = pl.ds(pl.multiple_of(kind * rows, 8), rows)
        starts.append(start)
        here = slice(rows * i, rows * i + rows)
        wanted = jnp.where(seg_row == seg_s[crop, row0 + i], tg[pl.ds(4 * half + i, 1), :], -1.0)
        counts = dot(hot, (bin_of == wanted).astype(f32).astype(bf16), 1, 1)
        number = jnp.sum(counts, -1, keepdims=True)
        hist[here, :] = counts
        many[here, :] = jnp.broadcast_to(number, (rows, 128))
        wa[here, :] = number * ta[start, :]
        zi[here, :] = z[start, :]
        so[here, :] = sgo[start, :]

    for group in range(own_rows // 4):
        own = range(4 * group, 4 * group + 4)

        def product(v, sums, own=own):
            edge = tb[pl.ds(v, rows, stride=rows), :]
            return tuple(
                total + wa[pl.ds(rows * i + v, 1), :] * edge for total, i in zip(sums, own)
            )

        sums = lax.fori_loop(0, vocab, product, (jnp.zeros((rows, 128), f32),) * 4)
        for total, i in zip(sums, own):
            x[rows * i : rows * i + rows, :] = total

    values = x[...]
    center = values - jnp.mean(values, -1, keepdims=True)
    inverse = lax.rsqrt(jnp.mean(center * center, -1, keepdims=True) + norm_eps)
    scaled = center * inverse
    mixed = (scaled * gain_mid).astype(bf16)
    branch = dot(mixed, w_mix, 1, 0)
    gate_out = so[...]
    update = (zi[...] + gate_out * branch).astype(bf16)
    logits = dot(update, dist_t, 1, 1)
    top = jnp.max(logits, -1, keepdims=True)
    powers = jnp.exp(logits - top)
    power_sum = jnp.sum(powers, -1, keepdims=True)
    counts = hist[...]
    number = many[:, 0:bins]
    loss = jnp.sum(many[:, 0:1] * (jnp.log(power_sum) + top), axis=0, keepdims=True) - jnp.sum(
        jnp.sum(counts * logits, axis=1, keepdims=True), axis=0, keepdims=True
    )
    grad_logits = ((number * (powers / power_sum) - counts) / count).astype(bf16)
    grad_dist_t = dot(grad_logits, update, 0, 0)
    grad_update = dot(grad_logits, dist_t, 1, 0)
    grad_branch = (grad_update * gate_out).astype(bf16)
    dz1[...] = grad_update
    dgo[...] = grad_update * branch * gate_out * (1.0 - gate_out)
    grad_mix = dot(mixed, grad_branch, 0, 0)
    grad_mixed = dot(grad_branch, w_mix, 1, 1)
    grad_gain_mid = jnp.sum(grad_mixed * scaled, axis=0, keepdims=True)
    grad_hat = grad_mixed * gain_mid
    dx[...] = inverse * (
        grad_hat
        - jnp.mean(grad_hat, -1, keepdims=True)
        - scaled * jnp.mean(grad_hat * scaled, -1, keepdims=True)
    )

    for ref in (ga, gb, go, gz):
        ref[...] = jnp.zeros_like(ref)
    for group in range(own_rows // 4):
        own = range(4 * group, 4 * group + 4)
        weighted = [wa[rows * i : rows * i + rows, :] for i in own]

        def edges(t, sums, own=own, weighted=weighted):
            at = pl.ds(pl.multiple_of(t * rows, 8), rows)
            edge = tb[at, :]
            right = gb[at, :]
            news = []
            for total, i, left in zip(sums, own, weighted):
                grad = dx[pl.ds(rows * i + t, 1), :]
                news.append(total + grad * edge)
                right = right + grad * left
            gb[at, :] = right
            return tuple(news)

        sums = lax.fori_loop(0, vocab, edges, (jnp.zeros((rows, 128), f32),) * 4)
        for total, i in zip(sums, own):
            here = slice(rows * i, rows * i + rows)
            ga[starts[i], :] += total * many[here, :]
            go[starts[i], :] += dgo[here, :]
            gz[starts[i], :] += dz1[here, :]

    def backward(step, grad_gain):
        at = pl.ds(pl.multiple_of(step * chunk, chunk), chunk)
        gate = sa[at, :]
        grad = ga[at, :] * gate
        dp[at, 0:128] = (grad * pa[at, :] * (1.0 - gate)).astype(bf16)
        dp[at, 128:256] = grad.astype(bf16)
        gate = sb[at, :]
        grad = gb[at, :] * gate
        dp[at, 256:384] = (grad * pb[at, :] * (1.0 - gate)).astype(bf16)
        dp[at, 384:512] = grad.astype(bf16)
        dp[at, 512:640] = go[at, :].astype(bf16)
        grad_normed = dot(dp[at, :], w_tri, 1, 1)
        scaled = xhat[at, :]
        grad_gain = grad_gain + jnp.sum(grad_normed * scaled, axis=0, keepdims=True)
        grad_hat = grad_normed * gain_in
        dz[at, :] = gz[at, :] + rstd[at, :] * (
            grad_hat
            - jnp.mean(grad_hat, -1, keepdims=True)
            - scaled * jnp.mean(grad_hat * scaled, -1, keepdims=True)
        )
        return grad_gain

    grad_gain_in = lax.fori_loop(0, table // chunk, backward, jnp.zeros((1, 128), f32))
    grad_tri = dot(zn[...], dp[...], 0, 0)

    def parts(values):
        high = values.astype(bf16)
        return high, (values - high.astype(f32)).astype(bf16)

    dz_high, dz_low = parts(
        jnp.concatenate([dz[rows * t : rows * t + rows, :] for t in range(rows)], axis=1)
    )
    grad_u = dot(b, dz_high, 0, 0) + dot(b, dz_low, 0, 0)
    for t in range(rows):
        du[32 * t : 32 * t + 32, :] = grad_u[:, 128 * t : 128 * t + 128]
    grad_b = dot(dz_high, u_cat, 1, 1) + dot(dz_low, u_cat, 1, 1)
    du_high, du_low = parts(
        jnp.concatenate([du[pl.ds(q, rows, stride=32), :] for q in range(32)], axis=1)
    )
    grad_outer = dot(a, du_high, 0, 0) + dot(a, du_low, 0, 0)
    grad_a = dot(du_high, w_outer, 1, 1) + dot(du_low, w_outer, 1, 1)

    grads[...] = jnp.zeros_like(grads)
    for q in range(32):
        grads[pl.ds(16 * (q // 8) + q % 8, 32, stride=64), :] = grad_outer[:, 128 * q : 128 * q + 128]
    for m in range(5):
        grads[pl.ds(8 + m, 128, stride=16), :] = grad_tri[:, 128 * m : 128 * m + 128]
    grads[pl.ds(13, 128, stride=16), :] = grad_mix
    grads[pl.ds(14, 128, stride=16), :] = jnp.concatenate(
        [grad_dist_t, grad_gain_in, grad_gain_mid, jnp.zeros((62, 128), f32)], axis=0
    ).T
    grads_out[...] = grads[...].astype(bf16)
    line = lax.broadcasted_iota(jnp.int32, (rows, 128), 0)
    lane = lax.broadcasted_iota(jnp.int32, (rows, 128), 1)
    d_out[...] = jnp.where((line == 0) & (lane == 64), loss, 0.0)
    d_out[:, 0:32] = grad_a
    d_out[:, 32:64] = grad_b


def reduce_kernel(
    grads, factor_grads, emb, ab,
    out,
    taken, taken_d, total_g, total_d, taken_n, taken_e, square, square_n, square_w,
    send_a, recv_a, send_d, recv_d, send_b, recv_b, send_e, recv_e, send_m, recv_m, send_w, recv_w,
):
    wide = lax.axis_index("wide")
    narrow = lax.axis_index("narrow")
    greet(wide, narrow)

    copies = []
    for k in range(1, wide_size):
        peer = lax.rem(wide + k, wide_size)
        copies.append(
            pltpu.make_async_remote_copy(
                src_ref=grads.at[pl.ds(pl.multiple_of(peer * 128, 128), 128)], dst_ref=taken.at[wide],
                send_sem=send_a.at[k], recv_sem=recv_a.at[k],
                device_id=(peer, narrow), device_id_type=MESH,
            )
        )
        copies.append(
            pltpu.make_async_remote_copy(
                src_ref=factor_grads, dst_ref=taken_d.at[wide],
                send_sem=send_d.at[k], recv_sem=recv_d.at[k],
                device_id=(peer, narrow), device_id_type=MESH,
            )
        )
    for copy in copies:
        copy.start()
    taken[wide] = grads[pl.ds(pl.multiple_of(wide * 128, 128), 128), :]
    taken_d[wide] = factor_grads[...]
    for copy in copies:
        copy.wait()
    total = taken[0].astype(f32)
    small = taken_d[0]
    for m in range(1, wide_size):
        total = total + taken[m].astype(f32)
        small = small + taken_d[m]
    total_g[...] = total
    total_d[...] = small

    copies = []
    for k in range(1, narrow_size):
        peer = lax.rem(narrow + k, narrow_size)
        copies.append(
            pltpu.make_async_remote_copy(
                src_ref=total_g.at[pl.ds(pl.multiple_of(peer * 16, 16), 16)], dst_ref=taken_n.at[narrow],
                send_sem=send_b.at[k], recv_sem=recv_b.at[k],
                device_id=(wide, peer), device_id_type=MESH,
            )
        )
        copies.append(
            pltpu.make_async_remote_copy(
                src_ref=total_d, dst_ref=taken_e.at[narrow],
                send_sem=send_e.at[k], recv_sem=recv_e.at[k],
                device_id=(wide, peer), device_id_type=MESH,
            )
        )
    for copy in copies:
        copy.start()
    taken_n[narrow] = total_g[pl.ds(pl.multiple_of(narrow * 16, 16), 16), :]
    taken_e[narrow] = total_d[...]
    for copy in copies:
        copy.wait()
    total = taken_n[0]
    small = taken_e[0]
    for m in range(1, narrow_size):
        total = total + taken_n[m]
        small = small + taken_e[m]

    highest = lax.Precision.HIGHEST
    factor_grad = small[:, 0:64]
    grad_emb = dot(rounded(ab[...]), factor_grad, 1, 1, highest)
    grad_ab = dot(rounded(emb[...]), factor_grad[0:vocab, :], 1, 0, highest)
    out[0:16, :] = total
    out[16:24, :] = jnp.zeros((8, 128), f32)
    out[24:32, :] = jnp.zeros((8, 128), f32)
    out[16:24, 0:tokens_padded] = grad_emb
    out[24:32, 0:64] = grad_ab
    squares = jnp.sum(jnp.sum(total * total, axis=1, keepdims=True), axis=0, keepdims=True)
    squares += jnp.sum(jnp.sum(grad_emb * grad_emb, axis=1, keepdims=True), axis=0, keepdims=True)
    squares += jnp.sum(jnp.sum(grad_ab * grad_ab, axis=1, keepdims=True), axis=0, keepdims=True)
    square[...] = jnp.broadcast_to(squares, square.shape)
    out[40:48, :] = jnp.broadcast_to(small[0:1, 64:65], (8, 128))

    copies = []
    for k in range(1, narrow_size):
        peer = lax.rem(narrow + k, narrow_size)
        copies.append(
            pltpu.make_async_remote_copy(
                src_ref=square, dst_ref=square_n.at[narrow],
                send_sem=send_m.at[k], recv_sem=recv_m.at[k],
                device_id=(wide, peer), device_id_type=MESH,
            )
        )
    for copy in copies:
        copy.start()
    square_n[narrow] = square[...]
    for copy in copies:
        copy.wait()
    total = square_n[0]
    for m in range(1, narrow_size):
        total = total + square_n[m]
    square[...] = total
    copies = []
    for k in range(1, wide_size):
        peer = lax.rem(wide + k, wide_size)
        copies.append(
            pltpu.make_async_remote_copy(
                src_ref=square, dst_ref=square_w.at[wide],
                send_sem=send_w.at[k], recv_sem=recv_w.at[k],
                device_id=(peer, narrow), device_id_type=MESH,
            )
        )
    for copy in copies:
        copy.start()
    square_w[wide] = square[...]
    for copy in copies:
        copy.wait()
    total = square_w[0]
    for m in range(1, wide_size):
        total = total + square_w[m]
    out[32:40, :] = total


def update_kernel(seg_v, reduced, *refs):
    weights, firsts, seconds = refs[0:7], refs[7:14], refs[14:21]
    loss_out, count_out, norm_out = refs[21:24]
    news, moms, vels = refs[24:31], refs[31:38], refs[38:45]
    count = jnp.zeros((4, 1), f32)
    for s in range(6):
        members = jnp.sum((seg_v[...] == s).astype(f32), axis=1, keepdims=True)
        count = count + members * members
    count_out[...] = jnp.sum(count, axis=0, keepdims=True)
    norm = jnp.sqrt(reduced[32:33, 0:1])
    norm_out[...] = norm
    loss_out[...] = reduced[40:41, 0:1]
    scale = jnp.minimum(1.0, clip_level / norm)
    tri = jnp.concatenate([reduced[8 + m : 9 + m, :] for m in range(5)], axis=1)
    grads = (
        reduced[16:24, 0:vocab],
        reduced[24:32, 0:64],
        reduced[0:8, :],
        tri,
        reduced[13:14, :],
        reduced[14:15, 0:64],
        reduced[14:15, 64:66],
    )
    for at, rate in enumerate(rates):
        clipped = grads[at] * scale
        weight = weights[at][...]
        first = beta_one * firsts[at][...] + (1.0 - beta_one) * clipped
        second = beta_two * seconds[at][...] + (1.0 - beta_two) * clipped * clipped
        ratio = (
            first
            / (1.0 - beta_one**step_count)
            / (jnp.sqrt(second / (1.0 - beta_two**step_count)) + adam_eps)
        )
        news[at][...] = weight - rate * (ratio + decay_rate * weight)
        moms[at][...] = first
        vels[at][...] = second


def shape(*dims, dtype=f32):
    return jax.ShapeDtypeStruct(dims, dtype)


in_vmem = pl.BlockSpec(memory_space=pltpu.VMEM)
in_smem = pl.BlockSpec(memory_space=pltpu.SMEM)


def gather_call(*args):
    dma = pltpu.SemaphoreType.DMA
    return pl.pallas_call(
        gather_kernel,
        out_shape=(
            shape(2048, 128, dtype=bf16),
            shape(tokens_padded, 128),
            shape(narrow_size, 16, 128, dtype=bf16),
        ),
        in_specs=[in_vmem] * len(args),
        out_specs=(in_vmem,) * 3,
        scratch_shapes=[
            VMEM((16, 128), f32),
            VMEM((narrow_size, 16, 128), f32),
            VMEM((narrow_size, 32, 128), bf16),
            VMEM((narrow_size, 32, 128), bf16),
            VMEM((tokens_padded, 128), f32),
            VMEM((narrow_size, tokens_padded, 128), f32),
            VMEM((128, 128), bf16),
            VMEM((tokens_padded, 128), f32),
            VMEM((wide_size, tokens_padded, 128), f32),
            dma((narrow_size,)), dma((narrow_size,)), dma((narrow_size,)), dma((narrow_size,)),
            dma((wide_size,)), dma((wide_size,)), dma((wide_size,)), dma((wide_size,)),
        ],
        compiler_params=pltpu.CompilerParams(
            collective_id=0, has_side_effects=True, vmem_limit_bytes=LIMIT
        ),
        name="gather_weights",
    )(*args)


def class_call(*args):
    wide_table = [VMEM((table, 128), f32)]
    own = [VMEM((own_rows * tokens_padded, 128), f32)]
    return pl.pallas_call(
        class_kernel,
        out_shape=(shape(2048, 128, dtype=bf16), shape(tokens_padded, 128)),
        in_specs=[in_smem] * 2 + [in_vmem] * (len(args) - 2),
        out_specs=(in_vmem,) * 2,
        scratch_shapes=[
            VMEM((2048, 128), f32),
            VMEM((16, length), f32),
            VMEM((32 * tokens_padded, 128), f32),
            *wide_table * 3,
            VMEM((table, 128), bf16),
            *wide_table * 7,
            VMEM((own_rows * tokens_padded, bins), f32),
            *own * 8,
            *wide_table * 4,
            VMEM((table, 640), bf16),
            *wide_table,
            VMEM((32 * tokens_padded, 128), f32),
            VMEM((2048, 128), f32),
        ],
        compiler_params=pltpu.CompilerParams(vmem_limit_bytes=LIMIT),
        name="pair_classes",
    )(*args)


def reduce_call(*args):
    dma = pltpu.SemaphoreType.DMA
    return pl.pallas_call(
        reduce_kernel,
        out_shape=shape(48, 128),
        in_specs=[in_vmem] * len(args),
        out_specs=in_vmem,
        scratch_shapes=[
            VMEM((wide_size, 128, 128), bf16),
            VMEM((wide_size, tokens_padded, 128), f32),
            VMEM((128, 128), f32),
            VMEM((tokens_padded, 128), f32),
            VMEM((narrow_size, 16, 128), f32),
            VMEM((narrow_size, tokens_padded, 128), f32),
            VMEM((8, 128), f32),
            VMEM((narrow_size, 8, 128), f32),
            VMEM((wide_size, 8, 128), f32),
            dma((wide_size,)), dma((wide_size,)), dma((wide_size,)), dma((wide_size,)),
            dma((narrow_size,)), dma((narrow_size,)), dma((narrow_size,)), dma((narrow_size,)),
            dma((narrow_size,)), dma((narrow_size,)), dma((wide_size,)), dma((wide_size,)),
        ],
        compiler_params=pltpu.CompilerParams(
            collective_id=1, has_side_effects=True, vmem_limit_bytes=LIMIT
        ),
        name="reduce_gradients",
    )(*args)


def local(tokens, segments, targets, *state):
    state = list(state)
    for at in (0, 6, 7, 13, 14, 20):
        state[at] = state[at].T
    masters = state[0:7]
    embed, w_ab = masters[0:2]
    gathered, factors, moved = gather_call(targets, *masters)
    grads, factor_grads = class_call(tokens, segments, tokens, segments, moved, gathered, factors)
    reduced = reduce_call(grads, factor_grads, embed, w_ab)
    shapes = [shape(*w.shape) for w in masters]
    outs = pl.pallas_call(
        update_kernel,
        out_shape=[shape(1, 1)] * 3 + shapes * 3,
        in_specs=[in_vmem] * (2 + 21),
        out_specs=[in_vmem] * 24,
        name="update_weights",
    )(segments, reduced, *state)
    outs = [value.reshape(()) for value in outs[0:3]] + list(outs[3:])
    for at in (3, 9, 10, 16, 17, 23):
        outs[at] = outs[at].T
    return tuple(outs)


def solution(mesh):
    both = ("wide", "narrow")
    whole = (P(None, both), P(both, None), P(both, None), P(both, None), P(both, None), P(both, None), P(None, both))
    return jax.shard_map(
        local,
        mesh=mesh,
        in_specs=(P(), P(), P(None, "wide", "narrow")) + whole * 3,
        out_specs=(P(), P(), P()) + whole * 3,
        check_vma=False,
    )
```

```python
import functools

import jax
import jax.numpy as jnp
from jax import lax
from jax.experimental import pallas as pl
from jax.experimental.pallas import tpu as pltpu
from jax.sharding import PartitionSpec as P

norm_eps = 1e-05
clip_level = 0.001
beta_one = 0.9
beta_two = 0.999
adam_eps = 1e-10
decay_rate = 0.01
step_count = 10.0
rates = (0.5, 0.016, 0.016, 0.044, 0.044, 0.044, 0.5)

f32 = jnp.float32
bf16 = jnp.bfloat16
MESH = pl.DeviceIdType.MESH
VMEM = pltpu.VMEM
LIMIT = 56 * 1024 * 1024

vocab = 33
kinds = 40
groups = 34
table = groups * kinds
own_rows = 12
own = own_rows * kinds
parts_all = groups + own_rows
bins = 64
wide_size = 16
depth_size = 4
length = 384


def dot(a, b, axis_a, axis_b, precision=None):
    return lax.dot_general(
        a, b, (((axis_a,), (axis_b,)), ((), ())), precision=precision, preferred_element_type=f32
    )


def rounded(values):
    return values.astype(bf16).astype(f32)


def halves(values):
    high = values.astype(bf16)
    return high, (values - high.astype(f32)).astype(bf16)


def whole_sum(values):
    return jnp.sum(jnp.sum(values, axis=1, keepdims=True), axis=0, keepdims=True)


def step_kernel(
    tok_s, seg_s, tok_v, seg_v, tgt, emb, ab, outer, tri, mix, dist, gain,
    out,
    pack, tstage, stage, taken, ea, ea_taken, targets_in, source, gathered,
    weights, gram, tg, u, z, xhat, rstd, zn, sb, pb, tb,
    hist, many, wa, xi, ri, zr, sr, pr, x, dx, dz1, gr, gb,
    dpt, dpr, dzt, dzr, du, grads, packed, other, sent, taken_w, sum_z, taken_z,
    d_block, d_other, d_half, d_wide, d_sum, d_depth, d_final, d_partner, d_all, square, squares,
    sz, rz, sy, ry, sg, rg, st, rt, sc, rc, s1, r1, s2, r2, s3, r3, s4, r4, s5, r5, s6, r6, s7, r7, s8, r8,
):
    wide = lax.axis_index("wide")
    narrow = lax.axis_index("narrow")
    depth = narrow // 2
    core = lax.rem(narrow, 2)
    partner = (wide, depth * 2 + 1 - core)
    deep = [(wide, lax.rem(depth + k, depth_size) * 2 + core) for k in range(1, depth_size)]
    flat = [(lax.rem(wide + k, wide_size), narrow) for k in range(1, wide_size)]

    barrier = pltpu.get_barrier_semaphore()
    for peer in [partner] + deep + flat:
        pl.semaphore_signal(barrier, inc=1, device_id=peer, device_id_type=MESH)

    def remote(source_ref, target_ref, send, receive, peer):
        return pltpu.make_async_remote_copy(
            src_ref=source_ref, dst_ref=target_ref, send_sem=send, recv_sem=receive,
            device_id=peer, device_id_type=MESH,
        )

    def start(copies):
        for copy in copies:
            copy.start()
        return copies

    def wait(copies):
        for copy in copies:
            copy.wait()

    pack[...] = jnp.zeros_like(pack)
    pack[0:8, :] = outer[...]
    for m in range(5):
        pack[8 + m : 9 + m, :] = tri[:, 128 * m : 128 * m + 128]
    pack[13:14, :] = mix[...]
    pack[14:15, 0:64] = dist[...]
    pack[14:15, 64:66] = gain[...]
    low = pack[...].astype(bf16)
    tstage[...] = jnp.zeros_like(tstage)
    for m in range(depth_size):
        tstage[m, :, 0:48] = tgt[m, 0:16, :].astype(f32)
        tstage[m, :, 64:112] = tgt[m, 8:24, :].astype(f32)
        stage[m, 0:16, :] = low
        stage[m, 16:32, :] = tstage[m].astype(bf16)
    ea[...] = jnp.zeros_like(ea)
    ea[:, 0:vocab] = rounded(emb[...])
    ea[:, 64:128] = rounded(ab[...])
    pl.semaphore_wait(barrier, 1 + len(deep) + len(flat))

    copies = []
    for k, peer in enumerate(deep):
        copies.append(remote(stage.at[peer[1] // 2], taken.at[depth], sz.at[k], rz.at[k], peer))
        copies.append(remote(ea, ea_taken.at[depth], sy.at[k], ry.at[k], peer))
    start(copies)
    taken[depth] = stage[depth]
    ea_taken[depth] = ea[...]
    wait(copies)
    for m in range(depth_size):
        source[16 * m : 16 * m + 16, :] = taken[m, 0:16, :]
        targets_in[core, m] = taken[m, 16:32, :]
    source[64:96, :] = jnp.concatenate([ea_taken[m] for m in range(depth_size)], axis=0).astype(bf16)
    wide_copies = start(
        [
            remote(source, gathered.at[core, wide], sg.at[k], rg.at[k], peer)
            for k, peer in enumerate(flat)
        ]
    )
    moved = start([remote(targets_in.at[core], targets_in.at[core], st, rt, partner)])
    gathered[core, wide] = source[...]
    core_copies = start(
        [remote(source, gathered.at[core, wide], sc.at[0], rc.at[0], partner)]
    )

    wait(moved)
    for m in range(depth_size):
        for side in range(2):
            piece = targets_in[side, m].astype(f32)
            piece = jnp.where(core == 0, piece[:, 0:48], piece[:, 64:112])
            at = 48 * (2 * m + side)
            tg[:, at : at + 48] = piece
    row0 = wide * 24 + core * own_rows
    tok_row = tok_v[pl.ds(depth, 1), :]
    seg_row = seg_v[pl.ds(depth, 1), :]
    hot = (lax.broadcasted_iota(jnp.int32, (kinds, length), 0) == tok_row).astype(f32).astype(bf16)
    bin_of = lax.broadcasted_iota(jnp.int32, (bins, length), 0).astype(f32)
    line = lax.broadcasted_iota(jnp.int32, (48, kinds), 0)
    kind_of = line
    for i in range(own_rows):
        kind_of = jnp.where(line == groups + i, tok_s[depth, row0 + i], kind_of)
    pick = (kind_of == lax.broadcasted_iota(jnp.int32, (48, kinds), 1)).astype(f32).astype(bf16)
    for i in range(own_rows):
        here = slice(kinds * i, kinds * i + kinds)
        wanted = jnp.where(seg_row == seg_s[depth, row0 + i], tg[pl.ds(4 * core + i, 1), :], -1.0)
        counts = dot(hot, (bin_of == wanted).astype(f32).astype(bf16), 1, 1)
        hist[here, :] = counts
        many[here, :] = jnp.broadcast_to(jnp.sum(counts, -1, keepdims=True), (kinds, 128))
    count = jnp.zeros((4, 1), f32)
    for s in range(6):
        members = jnp.sum((seg_v[...] == s).astype(f32), axis=1, keepdims=True)
        count = count + members * members
    count = jnp.sum(count, axis=0, keepdims=True)

    for k, copy in enumerate(wide_copies):
        copy.wait_recv()
        slot = gathered.at[core, lax.rem(wide + wide_size - 1 - k, wide_size)]
        core_copies += start([remote(slot, slot, sc.at[k + 1], rc.at[k + 1], partner)])
    for copy in wide_copies:
        copy.wait_send()
    wait(core_copies)

    for side in range(2):
        for m in range(wide_size):
            for deep_at in range(depth_size):
                at = 16 * (8 * m + 2 * deep_at + side)
                weights[at : at + 16, :] = gathered[side, m, 16 * deep_at : 16 * deep_at + 16, :].astype(f32)
    shards = gathered[:, :, 64:96, :].reshape(2 * wide_size * 32, 128)
    gram[...] = dot(shards, shards, 0, 0)
    a = dot(pick, gram[0:kinds, 64:96].astype(bf16), 1, 0).astype(bf16)
    b = gram[0:kinds, 96:128].astype(bf16)
    w_outer = jnp.concatenate(
        [weights[pl.ds(16 * (q // 8) + q % 8, 32, stride=64), :] for q in range(32)], axis=1
    ).astype(bf16)
    w_own = jnp.concatenate(
        [weights[pl.ds(8 + m, 128, stride=16), :] for m in (0, 1, 4)], axis=1
    ).astype(bf16)
    w_other = jnp.concatenate(
        [weights[pl.ds(8 + m, 128, stride=16), :] for m in (2, 3)], axis=1
    ).astype(bf16)
    w_mix = weights[pl.ds(13, 128, stride=16), :].astype(bf16)
    tail_t = weights[pl.ds(14, 128, stride=16), :].T
    dist_t = tail_t[0:bins, :].astype(bf16)
    gain_in = tail_t[64:65, :]
    gain_mid = tail_t[65:66, :]

    u_q = rounded(dot(a, w_outer, 1, 0))
    for q in range(32):
        u[pl.ds(q, 48, stride=32), :] = u_q[:, 128 * q : 128 * q + 128]
    u_all = jnp.concatenate([u[32 * t : 32 * t + 32, :] for t in range(parts_all)], axis=1).astype(bf16)
    z_cat = dot(b, u_all, 1, 0)
    for t in range(parts_all):
        z[kinds * t : kinds * t + kinds, :] = z_cat[:, 128 * t : 128 * t + 128]

    chunk = 272
    tb[table:, :] = jnp.zeros((kinds * kinds - table, 128), f32)

    def forward(step, carry):
        at = pl.ds(pl.multiple_of(step * chunk, 16), chunk)
        values = z[at, :]
        center = values - jnp.mean(values, -1, keepdims=True)
        inverse = lax.rsqrt(jnp.mean(center * center, -1, keepdims=True) + norm_eps)
        scaled = center * inverse
        normed = (scaled * gain_in).astype(bf16)
        xhat[at, :] = scaled
        rstd[at, :] = jnp.broadcast_to(inverse, scaled.shape)
        zn[at, :] = normed
        projected = dot(normed, w_other, 1, 0)
        gate = jax.nn.sigmoid(projected[:, 0:128])
        value = projected[:, 128:256]
        sb[at, :] = gate
        pb[at, :] = value
        tb[at, :] = rounded(gate * value)
        return carry

    lax.fori_loop(0, table // chunk, forward, 0)

    values = z[table:, :]
    center = values - jnp.mean(values, -1, keepdims=True)
    inverse = lax.rsqrt(jnp.mean(center * center, -1, keepdims=True) + norm_eps)
    scaled = center * inverse
    xi[...] = scaled
    ri[...] = jnp.broadcast_to(inverse, scaled.shape)
    normed = (scaled * gain_in).astype(bf16)
    zr[...] = normed
    projected = dot(normed, w_own, 1, 0)
    gate = jax.nn.sigmoid(projected[:, 0:128])
    value = projected[:, 128:256]
    sr[...] = gate
    pr[...] = value
    wa[...] = many[...] * rounded(gate * value)
    gate_out = jax.nn.sigmoid(projected[:, 256:384])

    for group in range(own_rows // 4):
        mine = range(4 * group, 4 * group + 4)

        def product(v, sums, mine=mine):
            edge = tb[pl.ds(v, kinds, stride=kinds), :]
            return tuple(
                total + wa[pl.ds(kinds * i + v, 1), :] * edge for total, i in zip(sums, mine)
            )

        sums = lax.fori_loop(0, vocab, product, (jnp.zeros((kinds, 128), f32),) * 4)
        for total, i in zip(sums, mine):
            x[kinds * i : kinds * i + kinds, :] = total

    values = x[...]
    center = values - jnp.mean(values, -1, keepdims=True)
    inverse = lax.rsqrt(jnp.mean(center * center, -1, keepdims=True) + norm_eps)
    scaled = center * inverse
    mixed = (scaled * gain_mid).astype(bf16)
    branch = dot(mixed, w_mix, 1, 0)
    update = (z[table:, :] + gate_out * branch).astype(bf16)
    logits = dot(update, dist_t, 1, 1)
    top = jnp.max(logits, -1, keepdims=True)
    powers = jnp.exp(logits - top)
    power_sum = jnp.sum(powers, -1, keepdims=True)
    counts = hist[...]
    loss = jnp.sum(many[:, 0:1] * (jnp.log(power_sum) + top), axis=0, keepdims=True) - whole_sum(
        counts * logits
    )
    grad_logits = ((many[:, 0:bins] * (powers / power_sum) - counts) / count).astype(bf16)
    grad_dist_t = dot(grad_logits, update, 0, 0)
    grad_update = dot(grad_logits, dist_t, 1, 0)
    grad_branch = (grad_update * gate_out).astype(bf16)
    dz1[...] = grad_update
    dpr[:, 256:384] = (grad_update * branch * gate_out * (1.0 - gate_out)).astype(bf16)
    grad_mix = dot(mixed, grad_branch, 0, 0)
    grad_mixed = dot(grad_branch, w_mix, 1, 1)
    grad_gain_mid = jnp.sum(grad_mixed * scaled, axis=0, keepdims=True)
    grad_hat = grad_mixed * gain_mid
    dx[...] = inverse * (
        grad_hat
        - jnp.mean(grad_hat, -1, keepdims=True)
        - scaled * jnp.mean(grad_hat * scaled, -1, keepdims=True)
    )

    gb[...] = jnp.zeros_like(gb)
    for group in range(own_rows // 4):
        mine = range(4 * group, 4 * group + 4)
        weighted = [wa[kinds * i : kinds * i + kinds, :] for i in mine]

        def edges(t, sums, mine=mine, weighted=weighted):
            at = pl.ds(pl.multiple_of(t * kinds, 8), kinds)
            edge = tb[at, :]
            right = gb[at, :]
            news = []
            for total, i, left in zip(sums, mine, weighted):
                grad = dx[pl.ds(kinds * i + t, 1), :]
                news.append(total + grad * edge)
                right = right + grad * left
            gb[at, :] = right
            return tuple(news)

        sums = lax.fori_loop(0, vocab, edges, (jnp.zeros((kinds, 128), f32),) * 4)
        for total, i in zip(sums, mine):
            here = slice(kinds * i, kinds * i + kinds)
            gr[here, :] = total * many[here, :]

    def norm_back(grad_normed, scaled, inverse):
        grad_hat = grad_normed * gain_in
        return inverse * (
            grad_hat
            - jnp.mean(grad_hat, -1, keepdims=True)
            - scaled * jnp.mean(grad_hat * scaled, -1, keepdims=True)
        )

    gate = sr[...]
    grad = gr[...] * gate
    dpr[:, 0:128] = (grad * pr[...] * (1.0 - gate)).astype(bf16)
    dpr[:, 128:256] = grad.astype(bf16)
    grad_normed = dot(dpr[...], w_own, 1, 1)
    scaled = xi[...]
    grad_gain_in = jnp.sum(grad_normed * scaled, axis=0, keepdims=True)
    dzr[...] = dz1[...] + norm_back(grad_normed, scaled, ri[...])
    grad_tri_own = dot(zr[...], dpr[...], 0, 0)

    def backward(step, grad_gain):
        at = pl.ds(pl.multiple_of(step * chunk, 16), chunk)
        gate = sb[at, :]
        grad = gb[at, :] * gate
        dpt[at, 0:128] = (grad * pb[at, :] * (1.0 - gate)).astype(bf16)
        dpt[at, 128:256] = grad.astype(bf16)
        grad_normed = dot(dpt[at, :], w_other, 1, 1)
        scaled = xhat[at, :]
        dzt[at, :] = norm_back(grad_normed, scaled, rstd[at, :])
        return grad_gain + jnp.sum(grad_normed * scaled, axis=0, keepdims=True)

    grad_gain_in = lax.fori_loop(0, table // chunk, backward, grad_gain_in)
    grad_tri_other = dot(zn[...], dpt[...], 0, 0)

    blocks = [dzt[kinds * t : kinds * t + kinds, :] for t in range(groups)]
    blocks += [dzr[kinds * i : kinds * i + kinds, :] for i in range(own_rows)]
    dz_high, dz_low = halves(jnp.concatenate(blocks, axis=1))
    grad_u = dot(b, dz_high, 0, 0) + dot(b, dz_low, 0, 0)
    for t in range(parts_all):
        du[32 * t : 32 * t + 32, :] = grad_u[:, 128 * t : 128 * t + 128]
    du[32 * parts_all :, :] = jnp.zeros((32 * (48 - parts_all), 128), f32)
    grad_b = dot(dz_high, u_all, 1, 1) + dot(dz_low, u_all, 1, 1)
    du_high, du_low = halves(
        jnp.concatenate([du[pl.ds(q, 48, stride=32), :] for q in range(32)], axis=1)
    )
    grad_outer = dot(a, du_high, 0, 0) + dot(a, du_low, 0, 0)
    grad_a_high, grad_a_low = halves(dot(du_high, w_outer, 1, 1) + dot(du_low, w_outer, 1, 1))
    grad_a = dot(pick, grad_a_high, 0, 0) + dot(pick, grad_a_low, 0, 0)

    grads[...] = jnp.zeros_like(grads)
    for q in range(32):
        grads[pl.ds(16 * (q // 8) + q % 8, 32, stride=64), :] = grad_outer[:, 128 * q : 128 * q + 128]
    for at, m in enumerate((0, 1, 4)):
        grads[pl.ds(8 + m, 128, stride=16), :] = grad_tri_own[:, 128 * at : 128 * at + 128]
    for at, m in enumerate((2, 3)):
        grads[pl.ds(8 + m, 128, stride=16), :] = grad_tri_other[:, 128 * at : 128 * at + 128]
    grads[pl.ds(13, 128, stride=16), :] = grad_mix
    grads[pl.ds(14, 128, stride=16), :] = jnp.concatenate(
        [grad_dist_t, grad_gain_in, grad_gain_mid, jnp.zeros((62, 128), f32)], axis=0
    ).T
    for side in range(2):
        for m in range(wide_size):
            for deep_at in range(depth_size):
                at = 16 * (8 * m + 2 * deep_at + side)
                packed[side, m, 16 * deep_at : 16 * deep_at + 16, :] = grads[at : at + 16, :].astype(bf16)
    d_block[...] = jnp.zeros_like(d_block)
    for side, values in ((0, grad_a), (1, grad_b)):
        d_block[side, :, 0:32] = values[0:16]
        d_block[side, :, 32:64] = values[16:32]
        d_block[side, 0:8, 64:96] = values[32:40]
    d_block[0, 0:1, 96:97] = loss

    wait(
        start(
            [
                remote(packed.at[1 - core], other, s1, r1, partner),
                remote(d_block.at[1 - core], d_other, s2, r2, partner),
            ]
        )
    )
    for m in range(wide_size):
        sent[m] = (packed[core, m].astype(f32) + other[m].astype(f32)).astype(bf16)
    d_half[...] = d_block[core] + d_other[...]
    copies = []
    for k, peer in enumerate(flat):
        copies.append(remote(sent.at[peer[0]], taken_w.at[wide], s3.at[k], r3.at[k], peer))
        copies.append(remote(d_half, d_wide.at[wide], s4.at[k], r4.at[k], peer))
    start(copies)
    taken_w[wide] = sent[wide]
    d_wide[wide] = d_half[...]
    wait(copies)
    total = taken_w[0].astype(f32)
    small = d_wide[0]
    for m in range(1, wide_size):
        total = total + taken_w[m].astype(f32)
        small = small + d_wide[m]
    sum_z[...] = total.astype(bf16)
    d_sum[...] = small
    copies = []
    for k, peer in enumerate(deep):
        copies.append(remote(sum_z, taken_z.at[depth], s5.at[k], r5.at[k], peer))
        copies.append(remote(d_sum, d_depth.at[depth], s6.at[k], r6.at[k], peer))
    start(copies)
    taken_z[depth] = sum_z[...]
    d_depth[depth] = d_sum[...]
    wait(copies)
    total = taken_z[0].astype(f32)
    small = d_depth[0]
    for m in range(1, depth_size):
        total = total + taken_z[m].astype(f32)
        small = small + d_depth[m]
    lane = lax.broadcasted_iota(jnp.int32, (16, 128), 1)
    d_final[...] = jnp.where(lane == 100, whole_sum(total * total), small)
    copies = start([remote(d_final, d_partner, s7, r7, partner)])
    grads[0:64, :] = total
    out[0:16, :] = grads[pl.ds(pl.multiple_of(depth * 16, 16), 16), :]
    wait(copies)
    square[...] = jnp.broadcast_to(d_final[0:1, 100:101] + d_partner[0:1, 100:101], square.shape)
    copies = start(
        [remote(square, squares.at[wide], s8.at[k], r8.at[k], peer) for k, peer in enumerate(flat)]
    )
    squares[wide] = square[...]

    highest = lax.Precision.HIGHEST
    first = jnp.where(core == 0, d_final[...], d_partner[...])
    second = jnp.where(core == 0, d_partner[...], d_final[...])
    for side, values in ((0, first), (1, second)):
        at = slice(32 * side, 32 * side + 32)
        d_all[0:16, at] = values[:, 0:32]
        d_all[16:32, at] = values[:, 32:64]
        d_all[32:40, at] = values[0:8, 64:96]
    d_total = d_all[...]
    out[16:24, :] = jnp.zeros((8, 128), f32)
    out[24:32, :] = jnp.zeros((8, 128), f32)
    out[16:24, 0:kinds] = dot(ea[:, 64:128], d_total, 1, 1, highest)
    out[24:32, 0:64] = dot(ea[:, 0:kinds], d_total, 1, 0, highest)
    extra = whole_sum(dot(gram[0:kinds, 0:kinds], d_total, 1, 0, highest) * d_total)
    extra += whole_sum(dot(d_total, gram[64:128, 64:128], 1, 0, highest) * d_total)
    out[40:48, :] = jnp.broadcast_to(first[0:1, 96:97], (8, 128))
    wait(copies)
    total = squares[0]
    for m in range(1, wide_size):
        total = total + squares[m]
    out[32:40, :] = total + extra


def update_kernel(seg_v, reduced, *refs):
    weights, firsts, seconds = refs[0:7], refs[7:14], refs[14:21]
    loss_out, count_out, norm_out = refs[21:24]
    news, moms, vels = refs[24:31], refs[31:38], refs[38:45]
    count = jnp.zeros((4, 1), f32)
    for s in range(6):
        members = jnp.sum((seg_v[...] == s).astype(f32), axis=1, keepdims=True)
        count = count + members * members
    count_out[...] = jnp.sum(count, axis=0, keepdims=True)
    norm = jnp.sqrt(reduced[32:33, 0:1])
    norm_out[...] = norm
    loss_out[...] = reduced[40:41, 0:1]
    scale = jnp.minimum(1.0, clip_level / norm)
    tri = jnp.concatenate([reduced[8 + m : 9 + m, :] for m in range(5)], axis=1)
    grads = (
        reduced[16:24, 0:vocab],
        reduced[24:32, 0:64],
        reduced[0:8, :],
        tri,
        reduced[13:14, :],
        reduced[14:15, 0:64],
        reduced[14:15, 64:66],
    )
    for at, rate in enumerate(rates):
        clipped = grads[at] * scale
        weight = weights[at][...]
        first = beta_one * firsts[at][...] + (1.0 - beta_one) * clipped
        second = beta_two * seconds[at][...] + (1.0 - beta_two) * clipped * clipped
        ratio = (
            first
            / (1.0 - beta_one**step_count)
            / (jnp.sqrt(second / (1.0 - beta_two**step_count)) + adam_eps)
        )
        news[at][...] = weight - rate * (ratio + decay_rate * weight)
        moms[at][...] = first
        vels[at][...] = second


def shape(*dims, dtype=f32):
    return jax.ShapeDtypeStruct(dims, dtype)


in_vmem = pl.BlockSpec(memory_space=pltpu.VMEM)
in_smem = pl.BlockSpec(memory_space=pltpu.SMEM)


def shape(*dims, dtype=f32):
    return jax.ShapeDtypeStruct(dims, dtype)


in_vmem = pl.BlockSpec(memory_space=pltpu.VMEM)
in_smem = pl.BlockSpec(memory_space=pltpu.SMEM)


def step_call(*args):
    def sems(*dims):
        return [pltpu.SemaphoreType.DMA(dims), pltpu.SemaphoreType.DMA(dims)]

    def one():
        return [pltpu.SemaphoreType.DMA, pltpu.SemaphoreType.DMA]

    full = VMEM((table, 128), f32)
    mine = VMEM((own, 128), f32)
    block = VMEM((16, 128), f32)
    return pl.pallas_call(
        step_kernel,
        out_shape=shape(48, 128),
        in_specs=[in_smem] * 2 + [in_vmem] * (len(args) - 2),
        out_specs=in_vmem,
        scratch_shapes=[
            block,
            VMEM((depth_size, 16, 128), f32),
            VMEM((depth_size, 32, 128), bf16),
            VMEM((depth_size, 32, 128), bf16),
            VMEM((8, 128), f32),
            VMEM((depth_size, 8, 128), f32),
            VMEM((2, depth_size, 16, 128), bf16),
            VMEM((96, 128), bf16),
            VMEM((2, wide_size, 96, 128), bf16),
            VMEM((2048, 128), f32),
            VMEM((128, 128), f32),
            VMEM((16, length), f32),
            VMEM((32 * 48, 128), f32),
            VMEM((kinds * parts_all, 128), f32),
            full, full,
            VMEM((table, 128), bf16),
            full, full,
            VMEM((kinds * kinds, 128), f32),
            VMEM((own, bins), f32),
            mine, mine, mine, mine,
            VMEM((own, 128), bf16),
            mine, mine, mine, mine, mine, mine,
            full,
            VMEM((table, 256), bf16),
            VMEM((own, 384), bf16),
            full,
            mine,
            VMEM((32 * 48, 128), f32),
            VMEM((2048, 128), f32),
            VMEM((2, wide_size, 64, 128), bf16),
            VMEM((wide_size, 64, 128), bf16),
            VMEM((wide_size, 64, 128), bf16),
            VMEM((wide_size, 64, 128), bf16),
            VMEM((64, 128), bf16),
            VMEM((depth_size, 64, 128), bf16),
            VMEM((2, 16, 128), f32),
            block, block,
            VMEM((wide_size, 16, 128), f32),
            block,
            VMEM((depth_size, 16, 128), f32),
            block, block,
            VMEM((kinds, 64), f32),
            VMEM((8, 128), f32),
            VMEM((wide_size, 8, 128), f32),
            *sems(depth_size), *sems(depth_size), *sems(wide_size), *one(), *sems(wide_size),
            *one(), *one(), *sems(wide_size), *sems(wide_size), *sems(depth_size), *sems(depth_size),
            *one(), *sems(wide_size),
        ],
        compiler_params=pltpu.CompilerParams(
            collective_id=0, has_side_effects=True, vmem_limit_bytes=LIMIT
        ),
        name="pair_step",
    )(*args)


def local(tokens, segments, targets, *state):
    state = list(state)
    for at in (0, 6, 7, 13, 14, 20):
        state[at] = state[at].T
    masters = state[0:7]
    reduced = step_call(tokens, segments, tokens, segments, targets, *masters)
    shapes = [shape(*w.shape) for w in masters]
    outs = pl.pallas_call(
        update_kernel,
        out_shape=[shape(1, 1)] * 3 + shapes * 3,
        in_specs=[in_vmem] * (2 + 21),
        out_specs=[in_vmem] * 24,
        name="update_weights",
    )(segments, reduced, *state)
    outs = [value.reshape(()) for value in outs[0:3]] + list(outs[3:])
    for at in (3, 9, 10, 16, 17, 23):
        outs[at] = outs[at].T
    return tuple(outs)


def solution(mesh):
    both = ("wide", "narrow")
    whole = (P(None, both), P(both, None), P(both, None), P(both, None), P(both, None), P(both, None), P(None, both))
    return jax.shard_map(
        local,
        mesh=mesh,
        in_specs=(P(), P(), P(None, "wide", "narrow")) + whole * 3,
        out_specs=(P(), P(), P()) + whole * 3,
        check_vma=False,
    )
```

```python
import functools

import jax
import jax.numpy as jnp
from jax import lax
from jax.experimental import pallas as pl
from jax.experimental.pallas import tpu as pltpu
from jax.sharding import PartitionSpec as P

norm_eps = 1e-05
clip_level = 0.001
beta_one = 0.9
beta_two = 0.999
adam_eps = 1e-10
decay_rate = 0.01
step_count = 10.0
rates = (0.5, 0.016, 0.016, 0.044, 0.044, 0.044, 0.5)

f32 = jnp.float32
bf16 = jnp.bfloat16
MESH = pl.DeviceIdType.MESH
VMEM = pltpu.VMEM
LIMIT = 56 * 1024 * 1024

vocab = 33
kinds = 40
groups = 34
table = groups * kinds
own_rows = 12
own = own_rows * kinds
parts_all = groups + own_rows
bins = 64
wide_size = 16
depth_size = 4
length = 384


def dot(a, b, axis_a, axis_b, precision=None):
    return lax.dot_general(
        a, b, (((axis_a,), (axis_b,)), ((), ())), precision=precision, preferred_element_type=f32
    )


def rounded(values):
    return values.astype(bf16).astype(f32)


def halves(values):
    high = values.astype(bf16)
    return high, (values - high.astype(f32)).astype(bf16)


def whole_sum(values):
    return jnp.sum(jnp.sum(values, axis=1, keepdims=True), axis=0, keepdims=True)


def hops(step):
    return sum(min(part, 4 - part) for part in step)


flat_steps = sorted(
    [(dy, dx) for dy in range(4) for dx in range(4) if (dy, dx) != (0, 0)], key=hops, reverse=True
)
deep_steps = (2, 1, 3)


def step_kernel(*refs):
    inputs, refs = refs[:24], refs[24:]
    out, refs = refs[0], refs[1:]
    held, refs = refs[:24], refs[24:]
    (
        tok_s, seg_s, loaded,
        state, tstage, stage, taken, ea, targets_in, source, gathered,
        weights, gram, tg, u, z, xhat, rstd, zn, sb, pb, tb,
        hist, many, wa, xi, ri, zr, sr, pr, x, dx, dz1, gr, gb,
        dpt, dpr, dzt, dzr, du, grads, packed, other, sent, taken_w, sum_z, taken_z,
        d_block, d_other, d_final, d_partner, d_all, square, squares, square_c, square_p,
        sz, rz, sg, rg, st, rt, sc, rc, s1, r1, s2, r2, s3, r3, s5, r5, s7, r7, s8, r8, s9, r9,
    ) = refs
    wide = lax.axis_index("wide")
    narrow = lax.axis_index("narrow")
    depth = narrow // 2
    core = lax.rem(narrow, 2)
    row, column = wide // 4, lax.rem(wide, 4)

    def at_step(dy, dx):
        return lax.rem(row + dy, 4) * 4 + lax.rem(column + dx, 4)

    partner = (wide, depth * 2 + 1 - core)
    deep = [(wide, lax.rem(depth + k, depth_size) * 2 + core) for k in deep_steps]
    flat = [(at_step(dy, dx), narrow) for dy, dx in flat_steps]
    flat_from = [at_step(4 - dy, 4 - dx) for dy, dx in flat_steps]

    barrier = pltpu.get_barrier_semaphore()
    for peer in flat + deep + [partner]:
        pl.semaphore_signal(barrier, inc=1, device_id=peer, device_id_type=MESH)

    loads = [pltpu.make_async_copy(a, b, loaded.at[k]) for k, (a, b) in enumerate(zip(inputs, held))]
    loads.append(pltpu.make_async_copy(inputs[0], tok_s, loaded.at[24]))
    loads.append(pltpu.make_async_copy(inputs[1], seg_s, loaded.at[25]))
    for load in loads:
        load.start()

    def remote(source_ref, target_ref, send, receive, peer):
        return pltpu.make_async_remote_copy(
            src_ref=source_ref, dst_ref=target_ref, send_sem=send, recv_sem=receive,
            device_id=peer, device_id_type=MESH,
        )

    def start(copies):
        for copy in copies:
            copy.start()
        return copies

    def wait(copies):
        for copy in copies:
            copy.wait()

    state[...] = jnp.zeros_like(state)
    tstage[...] = jnp.zeros_like(tstage)
    stage[...] = jnp.zeros_like(stage)
    ea[...] = jnp.zeros_like(ea)
    for load in loads:
        load.wait()
    tok_v, seg_v, tgt = held[0:3]
    for kind in range(3):
        emb, ab, outer, tri, mix, dist, gain = held[3 + 7 * kind : 10 + 7 * kind]
        state[kind, 0:8, :] = outer[...]
        for m in range(5):
            state[kind, 8 + m : 9 + m, :] = tri[:, 128 * m : 128 * m + 128]
        state[kind, 13:14, :] = mix[...]
        state[kind, 14:15, 0:64] = dist[...]
        state[kind, 14:15, 64:66] = gain[...]
        state[kind, 16:24, 0:vocab] = emb[...]
        state[kind, 24:32, 0:64] = ab[...]
    ea[0:8, 0:vocab] = rounded(held[3][...])
    ea[0:8, 64:128] = rounded(held[4][...])
    low = state[0, 0:16, :].astype(bf16)
    low_ea = ea[...].astype(bf16)
    for m in range(depth_size):
        tstage[m, :, 0:48] = tgt[m, 0:16, :].astype(f32)
        tstage[m, :, 64:112] = tgt[m, 8:24, :].astype(f32)
        stage[m, 0:16, :] = low
        stage[m, 16:32, :] = tstage[m].astype(bf16)
        stage[m, 32:48, :] = low_ea
    pl.semaphore_wait(barrier, 1 + len(deep) + len(flat))

    copies = start(
        [
            remote(stage.at[peer[1] // 2], taken.at[depth], sz.at[k], rz.at[k], peer)
            for k, peer in enumerate(deep)
        ]
    )
    taken[depth] = stage[depth]
    wait(copies)
    for m in range(depth_size):
        source[16 * m : 16 * m + 16, :] = taken[m, 0:16, :]
        targets_in[core, m] = taken[m, 16:32, :]
    source[64:96, :] = jnp.concatenate(
        [taken[m, 32:48, :].astype(f32)[0:8] for m in range(depth_size)], axis=0
    ).astype(bf16)
    wide_copies = start(
        [
            remote(source, gathered.at[core, wide], sg.at[k], rg.at[k], peer)
            for k, peer in enumerate(flat)
        ]
    )
    moved = start([remote(targets_in.at[core], targets_in.at[core], st, rt, partner)])
    gathered[core, wide] = source[...]
    core_copies = start(
        [remote(source, gathered.at[core, wide], sc.at[0], rc.at[0], partner)]
    )

    wait(moved)
    for m in range(depth_size):
        for side in range(2):
            piece = targets_in[side, m].astype(f32)
            piece = jnp.where(core == 0, piece[:, 0:48], piece[:, 64:112])
            at = 48 * (2 * m + side)
            tg[:, at : at + 48] = piece
    row0 = wide * 24 + core * own_rows
    tok_row = tok_v[pl.ds(depth, 1), :]
    seg_row = seg_v[pl.ds(depth, 1), :]
    hot = (lax.broadcasted_iota(jnp.int32, (kinds, length), 0) == tok_row).astype(f32).astype(bf16)
    bin_of = lax.broadcasted_iota(jnp.int32, (bins, length), 0).astype(f32)
    line = lax.broadcasted_iota(jnp.int32, (48, kinds), 0)
    kind_of = line
    for i in range(own_rows):
        kind_of = jnp.where(line == groups + i, tok_s[depth, row0 + i], kind_of)
    pick = (kind_of == lax.broadcasted_iota(jnp.int32, (48, kinds), 1)).astype(f32).astype(bf16)
    for i in range(own_rows):
        here = slice(kinds * i, kinds * i + kinds)
        wanted = jnp.where(seg_row == seg_s[depth, row0 + i], tg[pl.ds(4 * core + i, 1), :], -1.0)
        counts = dot(hot, (bin_of == wanted).astype(f32).astype(bf16), 1, 1)
        hist[here, :] = counts
        many[here, :] = jnp.broadcast_to(jnp.sum(counts, -1, keepdims=True), (kinds, 128))
    count = jnp.zeros((4, 1), f32)
    for s in range(6):
        members = jnp.sum((seg_v[...] == s).astype(f32), axis=1, keepdims=True)
        count = count + members * members
    count = jnp.sum(count, axis=0, keepdims=True)

    for k in reversed(range(wide_size - 1)):
        wide_copies[k].wait_recv()
        slot = gathered.at[core, flat_from[k]]
        core_copies += start([remote(slot, slot, sc.at[k + 1], rc.at[k + 1], partner)])
    for copy in wide_copies:
        copy.wait_send()
    wait(core_copies)

    for side in range(2):
        for m in range(wide_size):
            for deep_at in range(depth_size):
                at = 16 * (8 * m + 2 * deep_at + side)
                weights[at : at + 16, :] = gathered[side, m, 16 * deep_at : 16 * deep_at + 16, :].astype(f32)
    shards = gathered[:, :, 64:96, :].reshape(2 * wide_size * 32, 128)
    gram[...] = dot(shards, shards, 0, 0)
    a = dot(pick, gram[0:kinds, 64:96].astype(bf16), 1, 0).astype(bf16)
    b = gram[0:kinds, 96:128].astype(bf16)
    w_outer = jnp.concatenate(
        [weights[pl.ds(16 * (q // 8) + q % 8, 32, stride=64), :] for q in range(32)], axis=1
    ).astype(bf16)
    w_own = jnp.concatenate(
        [weights[pl.ds(8 + m, 128, stride=16), :] for m in (0, 1, 4)], axis=1
    ).astype(bf16)
    w_other = jnp.concatenate(
        [weights[pl.ds(8 + m, 128, stride=16), :] for m in (2, 3)], axis=1
    ).astype(bf16)
    w_mix = weights[pl.ds(13, 128, stride=16), :].astype(bf16)
    tail_t = weights[pl.ds(14, 128, stride=16), :].T
    dist_t = tail_t[0:bins, :].astype(bf16)
    gain_in = tail_t[64:65, :]
    gain_mid = tail_t[65:66, :]

    u_q = rounded(dot(a, w_outer, 1, 0))
    for q in range(32):
        u[pl.ds(q, 48, stride=32), :] = u_q[:, 128 * q : 128 * q + 128]
    u_all = jnp.concatenate([u[32 * t : 32 * t + 32, :] for t in range(parts_all)], axis=1).astype(bf16)
    z_cat = dot(b, u_all, 1, 0)
    for t in range(parts_all):
        z[kinds * t : kinds * t + kinds, :] = z_cat[:, 128 * t : 128 * t + 128]

    chunk = 272
    tb[table:, :] = jnp.zeros((kinds * kinds - table, 128), f32)

    def forward(step, carry):
        at = pl.ds(pl.multiple_of(step * chunk, 16), chunk)
        values = z[at, :]
        center = values - jnp.mean(values, -1, keepdims=True)
        inverse = lax.rsqrt(jnp.mean(center * center, -1, keepdims=True) + norm_eps)
        scaled = center * inverse
        normed = (scaled * gain_in).astype(bf16)
        xhat[at, :] = scaled
        rstd[at, :] = jnp.broadcast_to(inverse, scaled.shape)
        zn[at, :] = normed
        projected = dot(normed, w_other, 1, 0)
        gate = jax.nn.sigmoid(projected[:, 0:128])
        value = projected[:, 128:256]
        sb[at, :] = gate
        pb[at, :] = value
        tb[at, :] = rounded(gate * value)
        return carry

    lax.fori_loop(0, table // chunk, forward, 0, unroll=True)

    values = z[table:, :]
    center = values - jnp.mean(values, -1, keepdims=True)
    inverse = lax.rsqrt(jnp.mean(center * center, -1, keepdims=True) + norm_eps)
    scaled = center * inverse
    xi[...] = scaled
    ri[...] = jnp.broadcast_to(inverse, scaled.shape)
    normed = (scaled * gain_in).astype(bf16)
    zr[...] = normed
    projected = dot(normed, w_own, 1, 0)
    gate = jax.nn.sigmoid(projected[:, 0:128])
    value = projected[:, 128:256]
    sr[...] = gate
    pr[...] = value
    wa[...] = many[...] * rounded(gate * value)
    gate_out = jax.nn.sigmoid(projected[:, 256:384])

    for group in range(own_rows // 4):
        mine = range(4 * group, 4 * group + 4)

        def product(v, sums, mine=mine):
            edge = tb[pl.ds(v, kinds, stride=kinds), :]
            return tuple(
                total + wa[pl.ds(kinds * i + v, 1), :] * edge for total, i in zip(sums, mine)
            )

        sums = lax.fori_loop(0, vocab, product, (jnp.zeros((kinds, 128), f32),) * 4, unroll=11)
        for total, i in zip(sums, mine):
            x[kinds * i : kinds * i + kinds, :] = total

    values = x[...]
    center = values - jnp.mean(values, -1, keepdims=True)
    inverse = lax.rsqrt(jnp.mean(center * center, -1, keepdims=True) + norm_eps)
    scaled = center * inverse
    mixed = (scaled * gain_mid).astype(bf16)
    branch = dot(mixed, w_mix, 1, 0)
    update = (z[table:, :] + gate_out * branch).astype(bf16)
    logits = dot(update, dist_t, 1, 1)
    top = jnp.max(logits, -1, keepdims=True)
    powers = jnp.exp(logits - top)
    power_sum = jnp.sum(powers, -1, keepdims=True)
    counts = hist[...]
    loss = jnp.sum(many[:, 0:1] * (jnp.log(power_sum) + top), axis=0, keepdims=True) - whole_sum(
        counts * logits
    )
    grad_logits = ((many[:, 0:bins] * (powers / power_sum) - counts) / count).astype(bf16)
    grad_dist_t = dot(grad_logits, update, 0, 0)
    grad_update = dot(grad_logits, dist_t, 1, 0)
    grad_branch = (grad_update * gate_out).astype(bf16)
    dz1[...] = grad_update
    dpr[:, 256:384] = (grad_update * branch * gate_out * (1.0 - gate_out)).astype(bf16)
    grad_mix = dot(mixed, grad_branch, 0, 0)
    grad_mixed = dot(grad_branch, w_mix, 1, 1)
    grad_gain_mid = jnp.sum(grad_mixed * scaled, axis=0, keepdims=True)
    grad_hat = grad_mixed * gain_mid
    dx[...] = inverse * (
        grad_hat
        - jnp.mean(grad_hat, -1, keepdims=True)
        - scaled * jnp.mean(grad_hat * scaled, -1, keepdims=True)
    )

    gb[...] = jnp.zeros_like(gb)
    for group in range(own_rows // 4):
        mine = range(4 * group, 4 * group + 4)
        weighted = [wa[kinds * i : kinds * i + kinds, :] for i in mine]

        def edges(t, sums, mine=mine, weighted=weighted):
            at = pl.ds(pl.multiple_of(t * kinds, 8), kinds)
            edge = tb[at, :]
            right = gb[at, :]
            news = []
            for total, i, left in zip(sums, mine, weighted):
                grad = dx[pl.ds(kinds * i + t, 1), :]
                news.append(total + grad * edge)
                right = right + grad * left
            gb[at, :] = right
            return tuple(news)

        sums = lax.fori_loop(0, vocab, edges, (jnp.zeros((kinds, 128), f32),) * 4, unroll=11)
        for total, i in zip(sums, mine):
            here = slice(kinds * i, kinds * i + kinds)
            gr[here, :] = total * many[here, :]

    def norm_back(grad_normed, scaled, inverse):
        grad_hat = grad_normed * gain_in
        return inverse * (
            grad_hat
            - jnp.mean(grad_hat, -1, keepdims=True)
            - scaled * jnp.mean(grad_hat * scaled, -1, keepdims=True)
        )

    gate = sr[...]
    grad = gr[...] * gate
    dpr[:, 0:128] = (grad * pr[...] * (1.0 - gate)).astype(bf16)
    dpr[:, 128:256] = grad.astype(bf16)
    grad_normed = dot(dpr[...], w_own, 1, 1)
    scaled = xi[...]
    grad_gain_in = jnp.sum(grad_normed * scaled, axis=0, keepdims=True)
    dzr[...] = dz1[...] + norm_back(grad_normed, scaled, ri[...])
    grad_tri_own = dot(zr[...], dpr[...], 0, 0)

    def backward(step, grad_gain):
        at = pl.ds(pl.multiple_of(step * chunk, 16), chunk)
        gate = sb[at, :]
        grad = gb[at, :] * gate
        dpt[at, 0:128] = (grad * pb[at, :] * (1.0 - gate)).astype(bf16)
        dpt[at, 128:256] = grad.astype(bf16)
        grad_normed = dot(dpt[at, :], w_other, 1, 1)
        scaled = xhat[at, :]
        dzt[at, :] = norm_back(grad_normed, scaled, rstd[at, :])
        return grad_gain + jnp.sum(grad_normed * scaled, axis=0, keepdims=True)

    grad_gain_in = lax.fori_loop(0, table // chunk, backward, grad_gain_in, unroll=True)
    grad_tri_other = dot(zn[...], dpt[...], 0, 0)

    blocks = [dzt[kinds * t : kinds * t + kinds, :] for t in range(groups)]
    blocks += [dzr[kinds * i : kinds * i + kinds, :] for i in range(own_rows)]
    dz_high, dz_low = halves(jnp.concatenate(blocks, axis=1))
    grad_u = dot(b, dz_high, 0, 0) + dot(b, dz_low, 0, 0)
    for t in range(parts_all):
        du[32 * t : 32 * t + 32, :] = grad_u[:, 128 * t : 128 * t + 128]
    du[32 * parts_all :, :] = jnp.zeros((32 * (48 - parts_all), 128), f32)
    grad_b = dot(dz_high, u_all, 1, 1) + dot(dz_low, u_all, 1, 1)
    du_high, du_low = halves(
        jnp.concatenate([du[pl.ds(q, 48, stride=32), :] for q in range(32)], axis=1)
    )
    grad_outer = dot(a, du_high, 0, 0) + dot(a, du_low, 0, 0)
    grad_a_high, grad_a_low = halves(dot(du_high, w_outer, 1, 1) + dot(du_low, w_outer, 1, 1))
    grad_a = dot(pick, grad_a_high, 0, 0) + dot(pick, grad_a_low, 0, 0)

    grads[...] = jnp.zeros_like(grads)
    for q in range(32):
        grads[pl.ds(16 * (q // 8) + q % 8, 32, stride=64), :] = grad_outer[:, 128 * q : 128 * q + 128]
    for at, m in enumerate((0, 1, 4)):
        grads[pl.ds(8 + m, 128, stride=16), :] = grad_tri_own[:, 128 * at : 128 * at + 128]
    for at, m in enumerate((2, 3)):
        grads[pl.ds(8 + m, 128, stride=16), :] = grad_tri_other[:, 128 * at : 128 * at + 128]
    grads[pl.ds(13, 128, stride=16), :] = grad_mix
    grads[pl.ds(14, 128, stride=16), :] = jnp.concatenate(
        [grad_dist_t, grad_gain_in, grad_gain_mid, jnp.zeros((62, 128), f32)], axis=0
    ).T
    for side in range(2):
        for m in range(wide_size):
            for deep_at in range(depth_size):
                at = 16 * (8 * m + 2 * deep_at + side)
                packed[side, m, 16 * deep_at : 16 * deep_at + 16, :] = grads[at : at + 16, :].astype(bf16)
    d_block[...] = jnp.zeros_like(d_block)
    for side, values in ((0, grad_a), (1, grad_b)):
        d_block[side, :, 0:32] = values[0:16]
        d_block[side, :, 32:64] = values[16:32]
        d_block[side, 0:8, 64:96] = values[32:40]
    d_block[0, 0:1, 96:97] = loss

    wait(
        start(
            [
                remote(packed.at[1 - core], other, s1, r1, partner),
                remote(d_block.at[1 - core], d_other, s2, r2, partner),
            ]
        )
    )
    lane = lax.broadcasted_iota(jnp.int32, (16, 128), 1)

    def split_loss(block):
        held_loss = jnp.sum(jnp.where((lane >= 96) & (lane < 99), block, 0.0), axis=1, keepdims=True)
        high = rounded(held_loss)
        middle = rounded(held_loss - high)
        block = jnp.where(lane == 96, high, block)
        block = jnp.where(lane == 97, middle, block)
        return jnp.where(lane == 98, held_loss - high - middle, block).astype(bf16)

    small = split_loss(d_block[core] + d_other[...])
    copies = []
    for k, peer in enumerate(flat):
        sent[peer[0], 0:64, :] = (
            packed[core, peer[0]].astype(f32) + other[peer[0]].astype(f32)
        ).astype(bf16)
        sent[peer[0], 64:80, :] = small
        copies += start([remote(sent.at[peer[0]], taken_w.at[wide], s3.at[k], r3.at[k], peer)])
    taken_w[wide, 0:64, :] = (packed[core, wide].astype(f32) + other[wide].astype(f32)).astype(bf16)
    taken_w[wide, 64:80, :] = small
    wait(copies)
    total = taken_w[0].astype(f32)
    for m in range(1, wide_size):
        total = total + taken_w[m].astype(f32)
    sum_z[0:64, :] = total[0:64].astype(bf16)
    sum_z[64:80, :] = split_loss(total[64:80])
    copies = start(
        [
            remote(sum_z, taken_z.at[depth], s5.at[k], r5.at[k], peer)
            for k, peer in enumerate(deep)
        ]
    )
    taken_z[depth] = sum_z[...]
    wait(copies)
    total = taken_z[0].astype(f32)
    for m in range(1, depth_size):
        total = total + taken_z[m].astype(f32)
    square[...] = jnp.broadcast_to(whole_sum(total[0:64] * total[0:64]), square.shape)
    copies = start(
        [remote(square, squares.at[wide], s8.at[k], r8.at[k], peer) for k, peer in enumerate(flat)]
    )
    d_final[...] = total[64:80]
    d_copies = start([remote(d_final, d_partner, s7, r7, partner)])
    squares[wide] = square[...]
    grads[0:64, :] = total[0:64]

    wait(d_copies)
    highest = lax.Precision.HIGHEST
    first = jnp.where(core == 0, d_final[...], d_partner[...])
    second = jnp.where(core == 0, d_partner[...], d_final[...])
    for side, values in ((0, first), (1, second)):
        at = slice(32 * side, 32 * side + 32)
        d_all[0:16, at] = values[:, 0:32]
        d_all[16:32, at] = values[:, 32:64]
        d_all[32:40, at] = values[0:8, 64:96]
    d_total = d_all[...]
    grad = x
    grad[0:16, :] = grads[pl.ds(pl.multiple_of(depth * 16, 16), 16), :]
    grad[16:32, :] = jnp.zeros((16, 128), f32)
    grad[16:24, 0:kinds] = dot(ea[0:8, 64:128], d_total, 1, 1, highest)
    grad[24:32, 0:64] = dot(ea[0:8, 0:kinds], d_total, 1, 0, highest)
    extra = whole_sum(dot(gram[0:kinds, 0:kinds], d_total, 1, 0, highest) * d_total)
    extra += whole_sum(dot(d_total, gram[64:128, 64:128], 1, 0, highest) * d_total)
    loss_sum = jnp.sum(first[0:1, 96:99], axis=1, keepdims=True)
    line = lax.broadcasted_iota(jnp.int32, (32, 128), 0)
    lane = lax.broadcasted_iota(jnp.int32, (32, 128), 1)
    slow = (line < 8) | (line >= 24)
    fast = ((line >= 16) & (line < 24)) | ((line == 14) & (lane >= 64))
    rate = jnp.where(slow, rates[1], jnp.where(fast, rates[0], rates[3]))
    weight = state[0]
    first_part = beta_one * state[1]
    second_part = beta_two * state[2]
    wait(copies)
    total = squares[0]
    for m in range(1, wide_size):
        total = total + squares[m]
    square_c[...] = total
    wait(start([remote(square_c, square_p, s9, r9, partner)]))
    norm = jnp.sqrt(square_c[0:1, 0:1] + square_p[0:1, 0:1] + extra)
    clipped = grad[0:32, :] * jnp.minimum(1.0, clip_level / norm)
    moment = first_part + (1.0 - beta_one) * clipped
    speed = second_part + (1.0 - beta_two) * clipped * clipped
    ratio = (
        moment
        / (1.0 - beta_one**step_count)
        / (jnp.sqrt(speed / (1.0 - beta_two**step_count)) + adam_eps)
    )
    out[0:32, :] = weight - rate * (ratio + decay_rate * weight)
    out[32:64, :] = moment
    out[64:96, :] = speed
    line = lax.broadcasted_iota(jnp.int32, (8, 128), 0)
    out[96:104, :] = jnp.where(line == 0, loss_sum, jnp.where(line == 1, count, norm))


def place_kernel(stepped, *outs):
    for at in range(3):
        outs[at][...] = stepped[96 + at : 97 + at, 0:1]
    for kind in range(3):
        emb, ab, outer, tri, mix, dist, gain = outs[3 + 7 * kind : 10 + 7 * kind]
        base = 32 * kind
        outer[...] = stepped[base : base + 8, :]
        for m in range(5):
            tri[:, 128 * m : 128 * m + 128] = stepped[base + 8 + m : base + 9 + m, :]
        mix[...] = stepped[base + 13 : base + 14, :]
        dist[...] = stepped[base + 14 : base + 15, 0:64]
        gain[...] = stepped[base + 14 : base + 15, 64:66]
        emb[...] = stepped[base + 16 : base + 24, 0:vocab]
        ab[...] = stepped[base + 24 : base + 32, 0:64]


def shape(*dims, dtype=f32):
    return jax.ShapeDtypeStruct(dims, dtype)


in_vmem = pl.BlockSpec(memory_space=pltpu.VMEM)


def step_call(*args):
    def sems(*dims):
        return [pltpu.SemaphoreType.DMA(dims), pltpu.SemaphoreType.DMA(dims)]

    def one():
        return [pltpu.SemaphoreType.DMA, pltpu.SemaphoreType.DMA]

    full = VMEM((table, 128), f32)
    mine = VMEM((own, 128), f32)
    block = VMEM((16, 128), f32)
    return pl.pallas_call(
        step_kernel,
        out_shape=shape(104, 128),
        in_specs=[pl.BlockSpec(memory_space=pl.ANY)] * len(args),
        out_specs=in_vmem,
        scratch_shapes=[
            *[VMEM(arg.shape, arg.dtype) for arg in args],
            pltpu.SMEM(args[0].shape, jnp.int32), pltpu.SMEM(args[1].shape, jnp.int32),
            pltpu.SemaphoreType.DMA((26,)),
            VMEM((3, 32, 128), f32),
            VMEM((depth_size, 16, 128), f32),
            VMEM((depth_size, 48, 128), bf16),
            VMEM((depth_size, 48, 128), bf16),
            block,
            VMEM((2, depth_size, 16, 128), bf16),
            VMEM((96, 128), bf16),
            VMEM((2, wide_size, 96, 128), bf16),
            VMEM((2048, 128), f32),
            VMEM((128, 128), f32),
            VMEM((16, length), f32),
            VMEM((32 * 48, 128), f32),
            VMEM((kinds * parts_all, 128), f32),
            full, full,
            VMEM((table, 128), bf16),
            full, full,
            VMEM((kinds * kinds, 128), f32),
            VMEM((own, bins), f32),
            mine, mine, mine, mine,
            VMEM((own, 128), bf16),
            mine, mine, mine, mine, mine, mine,
            full,
            VMEM((table, 256), bf16),
            VMEM((own, 384), bf16),
            full,
            mine,
            VMEM((32 * 48, 128), f32),
            VMEM((2048, 128), f32),
            VMEM((2, wide_size, 64, 128), bf16),
            VMEM((wide_size, 64, 128), bf16),
            VMEM((wide_size, 80, 128), bf16),
            VMEM((wide_size, 80, 128), bf16),
            VMEM((80, 128), bf16),
            VMEM((depth_size, 80, 128), bf16),
            VMEM((2, 16, 128), f32),
            block, block, block,
            VMEM((kinds, 64), f32),
            VMEM((8, 128), f32),
            VMEM((wide_size, 8, 128), f32),
            VMEM((8, 128), f32), VMEM((8, 128), f32),
            *sems(depth_size), *sems(wide_size), *one(), *sems(wide_size),
            *one(), *one(), *sems(wide_size), *sems(depth_size), *one(), *sems(wide_size), *one(),
        ],
        compiler_params=pltpu.CompilerParams(
            collective_id=0, has_side_effects=True, vmem_limit_bytes=LIMIT
        ),
        name="pair_step",
    )(*args)


def local(tokens, segments, targets, *state):
    state = list(state)
    for at in (0, 6, 7, 13, 14, 20):
        state[at] = state[at].T
    stepped = step_call(tokens, segments, targets, *state)
    shapes = [shape(*w.shape) for w in state[0:7]]
    outs = pl.pallas_call(
        place_kernel,
        out_shape=[shape(1, 1)] * 3 + shapes * 3,
        in_specs=[in_vmem],
        out_specs=[in_vmem] * 24,
        name="place_outputs",
    )(stepped)
    outs = [value.reshape(()) for value in outs[0:3]] + list(outs[3:])
    for at in (3, 9, 10, 16, 17, 23):
        outs[at] = outs[at].T
    return tuple(outs)


def solution(mesh):
    both = ("wide", "narrow")
    whole = (P(None, both), P(both, None), P(both, None), P(both, None), P(both, None), P(both, None), P(None, both))
    return jax.shard_map(
        local,
        mesh=mesh,
        in_specs=(P(), P(), P(None, "wide", "narrow")) + whole * 3,
        out_specs=(P(), P(), P()) + whole * 3,
        check_vma=False,
    )
```

```python
import functools

import jax
import jax.numpy as jnp
from jax import lax
from jax.experimental import pallas as pl
from jax.experimental.pallas import tpu as pltpu
from jax.sharding import PartitionSpec as P

norm_eps = 1e-05
clip_level = 0.001
beta_one = 0.9
beta_two = 0.999
adam_eps = 1e-10
decay_rate = 0.01
step_count = 10.0
rates = (0.5, 0.016, 0.016, 0.044, 0.044, 0.044, 0.5)

f32 = jnp.float32
bf16 = jnp.bfloat16
MESH = pl.DeviceIdType.MESH
VMEM = pltpu.VMEM
LIMIT = 56 * 1024 * 1024

vocab = 33
kinds = 40
groups = 34
table = groups * kinds
own_rows = 12
own = own_rows * kinds
parts_all = groups + own_rows
bins = 64
wide_size = 16
depth_size = 4
length = 384


def dot(a, b, axis_a, axis_b, precision=None):
    return lax.dot_general(
        a, b, (((axis_a,), (axis_b,)), ((), ())), precision=precision, preferred_element_type=f32
    )


def rounded(values):
    return values.astype(bf16).astype(f32)


def halves(values):
    high = values.astype(bf16)
    return high, (values - high.astype(f32)).astype(bf16)


def whole_sum(values):
    return jnp.sum(jnp.sum(values, axis=1, keepdims=True), axis=0, keepdims=True)


flat_steps = [(dy, dx) for dy in (2, 1, 3, 0) for dx in (2, 1, 3, 0) if (dy, dx) != (0, 0)]
deep_steps = (2, 1, 3)


def step_kernel(*refs):
    inputs, refs = refs[:24], refs[24:]
    out, refs = refs[0], refs[1:]
    held, refs = refs[:24], refs[24:]
    (
        tok_s, seg_s, loaded, ready,
        state, tstage, stage, taken, ea, targets_in, source, gathered,
        weights, gram, tg, u, z, xhat, rstd, zn, sb, pb, tb,
        hist, many, wa, xi, ri, zr, sr, pr, x, dx, dz1, gr, gb,
        dpt, dpr, dzt, dzr, du, grads, packed, other, sent, taken_w, sum_z, taken_z,
        d_block, d_other, d_final, d_partner, d_all, square, squares, square_c, square_p,
        sz, rz, sg, rg, st, rt, sc, rc, s1, r1, s2, r2, s3, r3, s5, r5, s7, r7, s8, r8, s9, r9,
    ) = refs
    wide = lax.axis_index("wide")
    narrow = lax.axis_index("narrow")
    depth = narrow // 2
    core = lax.rem(narrow, 2)
    row, column = wide // 4, lax.rem(wide, 4)

    def at_step(dy, dx):
        return lax.rem(row + dy, 4) * 4 + lax.rem(column + dx, 4)

    partner = (wide, depth * 2 + 1 - core)
    deep = [(wide, lax.rem(depth + k, depth_size) * 2 + core) for k in deep_steps]
    flat = [(at_step(dy, dx), narrow) for dy, dx in flat_steps]
    flat_from = [at_step(4 - dy, 4 - dx) for dy, dx in flat_steps]

    barrier = pltpu.get_barrier_semaphore()
    line_x = [(at_step(0, d), narrow) for d in deep_steps]
    line_y = [(at_step(d, 0), narrow) for d in deep_steps]
    for peer in line_y + line_x + deep + [partner]:
        pl.semaphore_signal(barrier, inc=1, device_id=peer, device_id_type=MESH)

    loads = [pltpu.make_async_copy(a, b, loaded.at[k]) for k, (a, b) in enumerate(zip(inputs, held))]
    loads.append(pltpu.make_async_copy(inputs[0], tok_s, loaded.at[24]))
    loads.append(pltpu.make_async_copy(inputs[1], seg_s, loaded.at[25]))
    for load in loads:
        load.start()

    def remote(source_ref, target_ref, send, receive, peer):
        return pltpu.make_async_remote_copy(
            src_ref=source_ref, dst_ref=target_ref, send_sem=send, recv_sem=receive,
            device_id=peer, device_id_type=MESH,
        )

    def start(copies):
        for copy in copies:
            copy.start()
        return copies

    def wait(copies):
        for copy in copies:
            copy.wait()

    state[...] = jnp.zeros_like(state)
    tstage[...] = jnp.zeros_like(tstage)
    stage[...] = jnp.zeros_like(stage)
    ea[...] = jnp.zeros_like(ea)
    for load in loads:
        load.wait()
    tok_v, seg_v, tgt = held[0:3]
    def keep(kind):
        emb, ab, outer, tri, mix, dist, gain = held[3 + 7 * kind : 10 + 7 * kind]
        state[kind, 0:8, :] = outer[...]
        for m in range(5):
            state[kind, 8 + m : 9 + m, :] = tri[:, 128 * m : 128 * m + 128]
        state[kind, 13:14, :] = mix[...]
        state[kind, 14:15, 0:64] = dist[...]
        state[kind, 14:15, 64:66] = gain[...]
        state[kind, 16:24, 0:vocab] = emb[...]
        state[kind, 24:32, 0:64] = ab[...]

    keep(0)
    ea[0:8, 0:vocab] = rounded(held[3][...])
    ea[0:8, 64:128] = rounded(held[4][...])
    low = state[0, 0:16, :].astype(bf16)
    low_ea = ea[...].astype(bf16)
    for m in range(depth_size):
        tstage[m, :, 0:48] = tgt[m, 0:16, :].astype(f32)
        tstage[m, :, 64:112] = tgt[m, 8:24, :].astype(f32)
        stage[m, 0:16, :] = low
        stage[m, 16:32, :] = tstage[m].astype(bf16)
        stage[m, 32:48, :] = low_ea
    pl.semaphore_wait(barrier, 1 + len(deep) + len(line_x) + len(line_y))
    for peer in line_x:
        pl.semaphore_signal(ready, inc=1, device_id=peer, device_id_type=MESH)

    copies = start(
        [
            remote(stage.at[peer[1] // 2], taken.at[depth], sz.at[k], rz.at[k], peer)
            for k, peer in enumerate(deep)
        ]
    )
    taken[depth] = stage[depth]
    keep(1)
    keep(2)
    wait(copies)
    for m in range(depth_size):
        source[16 * m : 16 * m + 16, :] = taken[m, 0:16, :]
        targets_in[core, m] = taken[m, 16:32, :]
    source[64:96, :] = jnp.concatenate(
        [taken[m, 32:48, :].astype(f32)[0:8] for m in range(depth_size)], axis=0
    ).astype(bf16)
    pl.semaphore_wait(ready, len(line_x))
    wide_copies = start(
        [
            remote(source, gathered.at[core, wide], sg.at[k], rg.at[k], peer)
            for k, peer in enumerate(flat)
        ]
    )
    moved = start([remote(targets_in.at[core], targets_in.at[core], st, rt, partner)])
    gathered[core, wide] = source[...]
    core_copies = start(
        [remote(source, gathered.at[core, wide], sc.at[0], rc.at[0], partner)]
    )

    wait(moved)
    for m in range(depth_size):
        for side in range(2):
            piece = targets_in[side, m].astype(f32)
            piece = jnp.where(core == 0, piece[:, 0:48], piece[:, 64:112])
            at = 48 * (2 * m + side)
            tg[:, at : at + 48] = piece
    row0 = wide * 24 + core * own_rows
    tok_row = tok_v[pl.ds(depth, 1), :]
    seg_row = seg_v[pl.ds(depth, 1), :]
    hot = (lax.broadcasted_iota(jnp.int32, (kinds, length), 0) == tok_row).astype(f32).astype(bf16)
    bin_of = lax.broadcasted_iota(jnp.int32, (bins, length), 0).astype(f32)
    line = lax.broadcasted_iota(jnp.int32, (48, kinds), 0)
    kind_of = line
    for i in range(own_rows):
        kind_of = jnp.where(line == groups + i, tok_s[depth, row0 + i], kind_of)
    pick = (kind_of == lax.broadcasted_iota(jnp.int32, (48, kinds), 1)).astype(f32).astype(bf16)
    for i in range(own_rows):
        here = slice(kinds * i, kinds * i + kinds)
        wanted = jnp.where(seg_row == seg_s[depth, row0 + i], tg[pl.ds(4 * core + i, 1), :], -1.0)
        counts = dot(hot, (bin_of == wanted).astype(f32).astype(bf16), 1, 1)
        hist[here, :] = counts
        many[here, :] = jnp.broadcast_to(jnp.sum(counts, -1, keepdims=True), (kinds, 128))
    count = jnp.zeros((4, 1), f32)
    for s in range(6):
        members = jnp.sum((seg_v[...] == s).astype(f32), axis=1, keepdims=True)
        count = count + members * members
    count = jnp.sum(count, axis=0, keepdims=True)

    for k in reversed(range(wide_size - 1)):
        wide_copies[k].wait_recv()
        slot = gathered.at[core, flat_from[k]]
        core_copies += start([remote(slot, slot, sc.at[k + 1], rc.at[k + 1], partner)])
    for copy in wide_copies:
        copy.wait_send()
    wait(core_copies)

    for side in range(2):
        for m in range(wide_size):
            for deep_at in range(depth_size):
                at = 16 * (8 * m + 2 * deep_at + side)
                weights[at : at + 16, :] = gathered[side, m, 16 * deep_at : 16 * deep_at + 16, :].astype(f32)
    shards = gathered[:, :, 64:96, :].reshape(2 * wide_size * 32, 128)
    gram[...] = dot(shards, shards, 0, 0)
    a = dot(pick, gram[0:kinds, 64:96].astype(bf16), 1, 0).astype(bf16)
    b = gram[0:kinds, 96:128].astype(bf16)
    w_outer = jnp.concatenate(
        [weights[pl.ds(16 * (q // 8) + q % 8, 32, stride=64), :] for q in range(32)], axis=1
    ).astype(bf16)
    w_own = jnp.concatenate(
        [weights[pl.ds(8 + m, 128, stride=16), :] for m in (0, 1, 4)], axis=1
    ).astype(bf16)
    w_other = jnp.concatenate(
        [weights[pl.ds(8 + m, 128, stride=16), :] for m in (2, 3)], axis=1
    ).astype(bf16)
    w_mix = weights[pl.ds(13, 128, stride=16), :].astype(bf16)
    tail_t = weights[pl.ds(14, 128, stride=16), :].T
    dist_t = tail_t[0:bins, :].astype(bf16)
    gain_in = tail_t[64:65, :]
    gain_mid = tail_t[65:66, :]

    u_q = rounded(dot(a, w_outer, 1, 0))
    for q in range(32):
        u[pl.ds(q, 48, stride=32), :] = u_q[:, 128 * q : 128 * q + 128]
    u_all = jnp.concatenate([u[32 * t : 32 * t + 32, :] for t in range(parts_all)], axis=1).astype(bf16)
    z_cat = dot(b, u_all, 1, 0)
    for t in range(parts_all):
        z[kinds * t : kinds * t + kinds, :] = z_cat[:, 128 * t : 128 * t + 128]

    chunk = 272
    tb[table:, :] = jnp.zeros((kinds * kinds - table, 128), f32)

    def forward(step, carry):
        at = pl.ds(pl.multiple_of(step * chunk, 16), chunk)
        values = z[at, :]
        center = values - jnp.mean(values, -1, keepdims=True)
        inverse = lax.rsqrt(jnp.mean(center * center, -1, keepdims=True) + norm_eps)
        scaled = center * inverse
        normed = (scaled * gain_in).astype(bf16)
        xhat[at, :] = scaled
        rstd[at, :] = jnp.broadcast_to(inverse, scaled.shape)
        zn[at, :] = normed
        projected = dot(normed, w_other, 1, 0)
        gate = jax.nn.sigmoid(projected[:, 0:128])
        value = projected[:, 128:256]
        sb[at, :] = gate
        pb[at, :] = value
        tb[at, :] = rounded(gate * value)
        return carry

    lax.fori_loop(0, table // chunk, forward, 0, unroll=True)

    values = z[table:, :]
    center = values - jnp.mean(values, -1, keepdims=True)
    inverse = lax.rsqrt(jnp.mean(center * center, -1, keepdims=True) + norm_eps)
    scaled = center * inverse
    xi[...] = scaled
    ri[...] = jnp.broadcast_to(inverse, scaled.shape)
    normed = (scaled * gain_in).astype(bf16)
    zr[...] = normed
    projected = dot(normed, w_own, 1, 0)
    gate = jax.nn.sigmoid(projected[:, 0:128])
    value = projected[:, 128:256]
    sr[...] = gate
    pr[...] = value
    wa[...] = many[...] * rounded(gate * value)
    gate_out = jax.nn.sigmoid(projected[:, 256:384])

    for group in range(own_rows // 4):
        mine = range(4 * group, 4 * group + 4)

        def product(v, sums, mine=mine):
            edge = tb[pl.ds(v, kinds, stride=kinds), :]
            return tuple(
                total + wa[pl.ds(kinds * i + v, 1), :] * edge for total, i in zip(sums, mine)
            )

        sums = lax.fori_loop(0, vocab, product, (jnp.zeros((kinds, 128), f32),) * 4, unroll=11)
        for total, i in zip(sums, mine):
            x[kinds * i : kinds * i + kinds, :] = total

    values = x[...]
    center = values - jnp.mean(values, -1, keepdims=True)
    inverse = lax.rsqrt(jnp.mean(center * center, -1, keepdims=True) + norm_eps)
    scaled = center * inverse
    mixed = (scaled * gain_mid).astype(bf16)
    branch = dot(mixed, w_mix, 1, 0)
    update = (z[table:, :] + gate_out * branch).astype(bf16)
    logits = dot(update, dist_t, 1, 1)
    top = jnp.max(logits, -1, keepdims=True)
    powers = jnp.exp(logits - top)
    power_sum = jnp.sum(powers, -1, keepdims=True)
    counts = hist[...]
    loss = jnp.sum(many[:, 0:1] * (jnp.log(power_sum) + top), axis=0, keepdims=True) - whole_sum(
        counts * logits
    )
    grad_logits = ((many[:, 0:bins] * (powers / power_sum) - counts) / count).astype(bf16)
    grad_dist_t = dot(grad_logits, update, 0, 0)
    grad_update = dot(grad_logits, dist_t, 1, 0)
    grad_branch = (grad_update * gate_out).astype(bf16)
    dz1[...] = grad_update
    dpr[:, 256:384] = (grad_update * branch * gate_out * (1.0 - gate_out)).astype(bf16)
    grad_mix = dot(mixed, grad_branch, 0, 0)
    grad_mixed = dot(grad_branch, w_mix, 1, 1)
    grad_gain_mid = jnp.sum(grad_mixed * scaled, axis=0, keepdims=True)
    grad_hat = grad_mixed * gain_mid
    dx[...] = inverse * (
        grad_hat
        - jnp.mean(grad_hat, -1, keepdims=True)
        - scaled * jnp.mean(grad_hat * scaled, -1, keepdims=True)
    )

    gb[...] = jnp.zeros_like(gb)
    for group in range(own_rows // 4):
        mine = range(4 * group, 4 * group + 4)
        weighted = [wa[kinds * i : kinds * i + kinds, :] for i in mine]

        def edges(t, sums, mine=mine, weighted=weighted):
            at = pl.ds(pl.multiple_of(t * kinds, 8), kinds)
            edge = tb[at, :]
            right = gb[at, :]
            news = []
            for total, i, left in zip(sums, mine, weighted):
                grad = dx[pl.ds(kinds * i + t, 1), :]
                news.append(total + grad * edge)
                right = right + grad * left
            gb[at, :] = right
            return tuple(news)

        sums = lax.fori_loop(0, vocab, edges, (jnp.zeros((kinds, 128), f32),) * 4, unroll=11)
        for total, i in zip(sums, mine):
            here = slice(kinds * i, kinds * i + kinds)
            gr[here, :] = total * many[here, :]

    def norm_back(grad_normed, scaled, inverse):
        grad_hat = grad_normed * gain_in
        return inverse * (
            grad_hat
            - jnp.mean(grad_hat, -1, keepdims=True)
            - scaled * jnp.mean(grad_hat * scaled, -1, keepdims=True)
        )

    gate = sr[...]
    grad = gr[...] * gate
    dpr[:, 0:128] = (grad * pr[...] * (1.0 - gate)).astype(bf16)
    dpr[:, 128:256] = grad.astype(bf16)
    grad_normed = dot(dpr[...], w_own, 1, 1)
    scaled = xi[...]
    grad_gain_in = jnp.sum(grad_normed * scaled, axis=0, keepdims=True)
    dzr[...] = dz1[...] + norm_back(grad_normed, scaled, ri[...])
    grad_tri_own = dot(zr[...], dpr[...], 0, 0)

    def backward(step, grad_gain):
        at = pl.ds(pl.multiple_of(step * chunk, 16), chunk)
        gate = sb[at, :]
        grad = gb[at, :] * gate
        dpt[at, 0:128] = (grad * pb[at, :] * (1.0 - gate)).astype(bf16)
        dpt[at, 128:256] = grad.astype(bf16)
        grad_normed = dot(dpt[at, :], w_other, 1, 1)
        scaled = xhat[at, :]
        dzt[at, :] = norm_back(grad_normed, scaled, rstd[at, :])
        return grad_gain + jnp.sum(grad_normed * scaled, axis=0, keepdims=True)

    grad_gain_in = lax.fori_loop(0, table // chunk, backward, grad_gain_in, unroll=True)
    grad_tri_other = dot(zn[...], dpt[...], 0, 0)

    blocks = [dzt[kinds * t : kinds * t + kinds, :] for t in range(groups)]
    blocks += [dzr[kinds * i : kinds * i + kinds, :] for i in range(own_rows)]
    dz_all = jnp.concatenate(blocks, axis=1).astype(bf16)
    grad_u = dot(b, dz_all, 0, 0)
    for t in range(parts_all):
        du[32 * t : 32 * t + 32, :] = grad_u[:, 128 * t : 128 * t + 128]
    du[32 * parts_all :, :] = jnp.zeros((32 * (48 - parts_all), 128), f32)
    grad_b = dot(dz_all, u_all, 1, 1)
    du_all = jnp.concatenate(
        [du[pl.ds(q, 48, stride=32), :] for q in range(32)], axis=1
    ).astype(bf16)
    grad_outer = dot(a, du_all, 0, 0)
    grad_a_high, grad_a_low = halves(dot(du_all, w_outer, 1, 1))
    grad_a = dot(pick, grad_a_high, 0, 0) + dot(pick, grad_a_low, 0, 0)

    grads[...] = jnp.zeros_like(grads)
    for q in range(32):
        grads[pl.ds(16 * (q // 8) + q % 8, 32, stride=64), :] = grad_outer[:, 128 * q : 128 * q + 128]
    for at, m in enumerate((0, 1, 4)):
        grads[pl.ds(8 + m, 128, stride=16), :] = grad_tri_own[:, 128 * at : 128 * at + 128]
    for at, m in enumerate((2, 3)):
        grads[pl.ds(8 + m, 128, stride=16), :] = grad_tri_other[:, 128 * at : 128 * at + 128]
    grads[pl.ds(13, 128, stride=16), :] = grad_mix
    grads[pl.ds(14, 128, stride=16), :] = jnp.concatenate(
        [grad_dist_t, grad_gain_in, grad_gain_mid, jnp.zeros((62, 128), f32)], axis=0
    ).T
    for side in range(2):
        for m in range(wide_size):
            for deep_at in range(depth_size):
                at = 16 * (8 * m + 2 * deep_at + side)
                packed[side, m, 16 * deep_at : 16 * deep_at + 16, :] = grads[at : at + 16, :].astype(bf16)
    d_block[...] = jnp.zeros_like(d_block)
    for side, values in ((0, grad_a), (1, grad_b)):
        d_block[side, :, 0:32] = values[0:16]
        d_block[side, :, 32:64] = values[16:32]
        d_block[side, 0:8, 64:96] = values[32:40]
    d_block[0, 0:1, 96:97] = loss

    d_copies = start([remote(d_block.at[1 - core], d_other, s2, r2, partner)])
    core_copies = []
    for k, dy in enumerate((2, 1, 3, 0)):
        at = pl.ds(lax.rem(row + dy, 4) * 4, 4)
        core_copies += start(
            [remote(packed.at[1 - core, at], other.at[at], s1.at[k], r1.at[k], partner)]
        )
    wait(d_copies)
    lane = lax.broadcasted_iota(jnp.int32, (16, 128), 1)

    def split_loss(block):
        held_loss = jnp.sum(jnp.where((lane >= 96) & (lane < 99), block, 0.0), axis=1, keepdims=True)
        high = rounded(held_loss)
        middle = rounded(held_loss - high)
        block = jnp.where(lane == 96, high, block)
        block = jnp.where(lane == 97, middle, block)
        return jnp.where(lane == 98, held_loss - high - middle, block).astype(bf16)

    small = split_loss(d_block[core] + d_other[...])
    copies = []
    for k, peer in enumerate(flat):
        if k in (0, 4, 8, 12):
            core_copies[k // 4].wait()
        sent[peer[0], 0:64, :] = (
            packed[core, peer[0]].astype(f32) + other[peer[0]].astype(f32)
        ).astype(bf16)
        sent[peer[0], 64:80, :] = small
        copies += start([remote(sent.at[peer[0]], taken_w.at[wide], s3.at[k], r3.at[k], peer)])
    taken_w[wide, 0:64, :] = (packed[core, wide].astype(f32) + other[wide].astype(f32)).astype(bf16)
    taken_w[wide, 64:80, :] = small
    wait(copies)
    total = taken_w[0].astype(f32)
    for m in range(1, wide_size):
        total = total + taken_w[m].astype(f32)
    sum_z[0:64, :] = total[0:64].astype(bf16)
    sum_z[64:80, :] = split_loss(total[64:80])
    copies = start(
        [
            remote(sum_z, taken_z.at[depth], s5.at[k], r5.at[k], peer)
            for k, peer in enumerate(deep)
        ]
    )
    taken_z[depth] = sum_z[...]
    wait(copies)
    total = taken_z[0].astype(f32)
    for m in range(1, depth_size):
        total = total + taken_z[m].astype(f32)
    square[...] = jnp.broadcast_to(whole_sum(total[0:64] * total[0:64]), square.shape)
    copies = start(
        [remote(square, squares.at[wide], s8.at[k], r8.at[k], peer) for k, peer in enumerate(flat)]
    )
    d_final[...] = total[64:80]
    d_copies = start([remote(d_final, d_partner, s7, r7, partner)])
    squares[wide] = square[...]
    grads[0:64, :] = total[0:64]

    wait(d_copies)
    highest = lax.Precision.HIGHEST
    first = jnp.where(core == 0, d_final[...], d_partner[...])
    second = jnp.where(core == 0, d_partner[...], d_final[...])
    for side, values in ((0, first), (1, second)):
        at = slice(32 * side, 32 * side + 32)
        d_all[0:16, at] = values[:, 0:32]
        d_all[16:32, at] = values[:, 32:64]
        d_all[32:40, at] = values[0:8, 64:96]
    d_total = d_all[...]
    grad = x
    grad[0:16, :] = grads[pl.ds(pl.multiple_of(depth * 16, 16), 16), :]
    grad[16:32, :] = jnp.zeros((16, 128), f32)
    grad[16:24, 0:kinds] = dot(ea[0:8, 64:128], d_total, 1, 1, highest)
    grad[24:32, 0:64] = dot(ea[0:8, 0:kinds], d_total, 1, 0, highest)
    extra = whole_sum(dot(gram[0:kinds, 0:kinds], d_total, 1, 0, highest) * d_total)
    extra += whole_sum(dot(d_total, gram[64:128, 64:128], 1, 0, highest) * d_total)
    loss_sum = jnp.sum(first[0:1, 96:99], axis=1, keepdims=True)
    line = lax.broadcasted_iota(jnp.int32, (32, 128), 0)
    lane = lax.broadcasted_iota(jnp.int32, (32, 128), 1)
    slow = (line < 8) | (line >= 24)
    fast = ((line >= 16) & (line < 24)) | ((line == 14) & (lane >= 64))
    rate = jnp.where(slow, rates[1], jnp.where(fast, rates[0], rates[3]))
    weight = state[0]
    first_part = beta_one * state[1]
    second_part = beta_two * state[2]
    wait(copies)
    total = squares[0]
    for m in range(1, wide_size):
        total = total + squares[m]
    square_c[...] = total
    wait(start([remote(square_c, square_p, s9, r9, partner)]))
    norm = jnp.sqrt(square_c[0:1, 0:1] + square_p[0:1, 0:1] + extra)
    clipped = grad[0:32, :] * jnp.minimum(1.0, clip_level / norm)
    moment = first_part + (1.0 - beta_one) * clipped
    speed = second_part + (1.0 - beta_two) * clipped * clipped
    ratio = (
        moment
        / (1.0 - beta_one**step_count)
        / (jnp.sqrt(speed / (1.0 - beta_two**step_count)) + adam_eps)
    )
    out[0:32, :] = weight - rate * (ratio + decay_rate * weight)
    out[32:64, :] = moment
    out[64:96, :] = speed
    line = lax.broadcasted_iota(jnp.int32, (8, 128), 0)
    out[96:104, :] = jnp.where(line == 0, loss_sum, jnp.where(line == 1, count, norm))


def place_kernel(stepped, *outs):
    for at in range(3):
        outs[at][...] = stepped[96 + at : 97 + at, 0:1]
    for kind in range(3):
        emb, ab, outer, tri, mix, dist, gain = outs[3 + 7 * kind : 10 + 7 * kind]
        base = 32 * kind
        outer[...] = stepped[base : base + 8, :]
        for m in range(5):
            tri[:, 128 * m : 128 * m + 128] = stepped[base + 8 + m : base + 9 + m, :]
        mix[...] = stepped[base + 13 : base + 14, :]
        dist[...] = stepped[base + 14 : base + 15, 0:64]
        gain[...] = stepped[base + 14 : base + 15, 64:66]
        emb[...] = stepped[base + 16 : base + 24, 0:vocab]
        ab[...] = stepped[base + 24 : base + 32, 0:64]


def shape(*dims, dtype=f32):
    return jax.ShapeDtypeStruct(dims, dtype)


in_vmem = pl.BlockSpec(memory_space=pltpu.VMEM)


def step_call(*args):
    def sems(*dims):
        return [pltpu.SemaphoreType.DMA(dims), pltpu.SemaphoreType.DMA(dims)]

    def one():
        return [pltpu.SemaphoreType.DMA, pltpu.SemaphoreType.DMA]

    full = VMEM((table, 128), f32)
    mine = VMEM((own, 128), f32)
    block = VMEM((16, 128), f32)
    return pl.pallas_call(
        step_kernel,
        out_shape=shape(104, 128),
        in_specs=[pl.BlockSpec(memory_space=pl.ANY)] * len(args),
        out_specs=in_vmem,
        scratch_shapes=[
            *[VMEM(arg.shape, arg.dtype) for arg in args],
            pltpu.SMEM(args[0].shape, jnp.int32), pltpu.SMEM(args[1].shape, jnp.int32),
            pltpu.SemaphoreType.DMA((26,)),
            pltpu.SemaphoreType.REGULAR,
            VMEM((3, 32, 128), f32),
            VMEM((depth_size, 16, 128), f32),
            VMEM((depth_size, 48, 128), bf16),
            VMEM((depth_size, 48, 128), bf16),
            block,
            VMEM((2, depth_size, 16, 128), bf16),
            VMEM((96, 128), bf16),
            VMEM((2, wide_size, 96, 128), bf16),
            VMEM((2048, 128), f32),
            VMEM((128, 128), f32),
            VMEM((16, length), f32),
            VMEM((32 * 48, 128), f32),
            VMEM((kinds * parts_all, 128), f32),
            full, full,
            VMEM((table, 128), bf16),
            full, full,
            VMEM((kinds * kinds, 128), f32),
            VMEM((own, bins), f32),
            mine, mine, mine, mine,
            VMEM((own, 128), bf16),
            mine, mine, mine, mine, mine, mine,
            full,
            VMEM((table, 256), bf16),
            VMEM((own, 384), bf16),
            full,
            mine,
            VMEM((32 * 48, 128), f32),
            VMEM((2048, 128), f32),
            VMEM((2, wide_size, 64, 128), bf16),
            VMEM((wide_size, 64, 128), bf16),
            VMEM((wide_size, 80, 128), bf16),
            VMEM((wide_size, 80, 128), bf16),
            VMEM((80, 128), bf16),
            VMEM((depth_size, 80, 128), bf16),
            VMEM((2, 16, 128), f32),
            block, block, block,
            VMEM((kinds, 64), f32),
            VMEM((8, 128), f32),
            VMEM((wide_size, 8, 128), f32),
            VMEM((8, 128), f32), VMEM((8, 128), f32),
            *sems(depth_size), *sems(wide_size), *one(), *sems(wide_size),
            *sems(4), *one(), *sems(wide_size), *sems(depth_size), *one(), *sems(wide_size), *one(),
        ],
        compiler_params=pltpu.CompilerParams(
            collective_id=0, has_side_effects=True, vmem_limit_bytes=LIMIT
        ),
        name="pair_step",
    )(*args)


def local(tokens, segments, targets, *state):
    state = list(state)
    for at in (0, 6, 7, 13, 14, 20):
        state[at] = state[at].T
    stepped = step_call(tokens, segments, targets, *state)
    shapes = [shape(*w.shape) for w in state[0:7]]
    outs = pl.pallas_call(
        place_kernel,
        out_shape=[shape(1, 1)] * 3 + shapes * 3,
        in_specs=[in_vmem],
        out_specs=[in_vmem] * 24,
        name="place_outputs",
    )(stepped)
    outs = [value.reshape(()) for value in outs[0:3]] + list(outs[3:])
    for at in (3, 9, 10, 16, 17, 23):
        outs[at] = outs[at].T
    return tuple(outs)


def solution(mesh):
    both = ("wide", "narrow")
    whole = (P(None, both), P(both, None), P(both, None), P(both, None), P(both, None), P(both, None), P(None, both))
    return jax.shard_map(
        local,
        mesh=mesh,
        in_specs=(P(), P(), P(None, "wide", "narrow")) + whole * 3,
        out_specs=(P(), P(), P()) + whole * 3,
        check_vma=False,
    )
```

```python
import functools

import jax
import jax.numpy as jnp
from jax import lax
from jax.experimental import pallas as pl
from jax.experimental.pallas import tpu as pltpu
from jax.sharding import PartitionSpec as P

norm_eps = 1e-05
clip_level = 0.001
beta_one = 0.9
beta_two = 0.999
adam_eps = 1e-10
decay_rate = 0.01
step_count = 10.0
rates = (0.5, 0.016, 0.016, 0.044, 0.044, 0.044, 0.5)

f32 = jnp.float32
bf16 = jnp.bfloat16
MESH = pl.DeviceIdType.MESH
VMEM = pltpu.VMEM
LIMIT = 56 * 1024 * 1024

vocab = 33
kinds = 40
groups = 34
table = groups * kinds
side_by_side = 4
columns_by = 4
own_rows = 12
own = own_rows * kinds
parts_all = groups + own_rows
bins = 64
wide_size = 16
depth_size = 4
length = 384


def dot(a, b, axis_a, axis_b, precision=None):
    return lax.dot_general(
        a, b, (((axis_a,), (axis_b,)), ((), ())), precision=precision, preferred_element_type=f32
    )


def rounded(values):
    return values.astype(bf16).astype(f32)


def halves(values):
    high = values.astype(bf16)
    return high, (values - high.astype(f32)).astype(bf16)


def whole_sum(values):
    return jnp.sum(jnp.sum(values, axis=1, keepdims=True), axis=0, keepdims=True)


flat_steps = [(dy, dx) for dy in (2, 1, 3, 0) for dx in (2, 1, 3, 0) if (dy, dx) != (0, 0)]
deep_steps = (2, 1, 3)


def step_kernel(*refs):
    inputs, refs = refs[:24], refs[24:]
    out, refs = refs[0], refs[1:]
    held, refs = refs[:24], refs[24:]
    (
        tok_s, seg_s, loaded, ready,
        state, tstage, stage, taken, ea, targets_in, source, gathered,
        weights, gram, tg, u, z, xhat, rstd, zn, sb, pb, tb,
        hist, many, wa, xi, ri, zr, sr, pr, x, dx, dz1, gr, gb,
        dpt, dpr, du, grads, packed, other, sent, taken_w, sum_z, taken_z,
        d_block, d_other, d_final, d_partner, d_all, square, squares,
        sz, rz, sg, rg, st, rt, sc, rc, s1, r1, s2, r2, s3, r3, s5, r5, s7, r7, s8, r8,
    ) = refs
    wide = lax.axis_index("wide")
    narrow = lax.axis_index("narrow")
    depth = narrow // 2
    core = lax.rem(narrow, 2)
    row, column = wide // 4, lax.rem(wide, 4)

    def at_step(dy, dx):
        return lax.rem(row + dy, 4) * 4 + lax.rem(column + dx, 4)

    across = depth * 2 + 1 - core
    partner = (wide, across)
    deep = [(wide, lax.rem(depth + k, depth_size) * 2 + core) for k in deep_steps]
    flat = [(at_step(dy, dx), narrow) for dy, dx in flat_steps]
    flat_from = [at_step(4 - dy, 4 - dx) for dy, dx in flat_steps]

    barrier = pltpu.get_barrier_semaphore()
    line_x = [(at_step(0, d), narrow) for d in deep_steps]
    line_y = [(at_step(d, 0), narrow) for d in deep_steps]
    for peer in line_y + line_x + deep + [partner]:
        pl.semaphore_signal(barrier, inc=1, device_id=peer, device_id_type=MESH)

    loads = [pltpu.make_async_copy(a, b, loaded.at[k]) for k, (a, b) in enumerate(zip(inputs, held))]
    loads.append(pltpu.make_async_copy(inputs[0], tok_s, loaded.at[24]))
    loads.append(pltpu.make_async_copy(inputs[1], seg_s, loaded.at[25]))
    for load in loads:
        load.start()

    def remote(source_ref, target_ref, send, receive, peer):
        return pltpu.make_async_remote_copy(
            src_ref=source_ref, dst_ref=target_ref, send_sem=send, recv_sem=receive,
            device_id=peer, device_id_type=MESH,
        )

    def start(copies):
        for copy in copies:
            copy.start()
        return copies

    def wait(copies):
        for copy in copies:
            copy.wait()

    state[...] = jnp.zeros_like(state)
    tstage[...] = jnp.zeros_like(tstage)
    stage[...] = jnp.zeros_like(stage)
    ea[...] = jnp.zeros_like(ea)
    for load in loads:
        load.wait()
    tok_v, seg_v, tgt = held[0:3]
    def keep(kind):
        emb, ab, outer, tri, mix, dist, gain = held[3 + 7 * kind : 10 + 7 * kind]
        state[kind, 0:8, :] = outer[...]
        for m in range(5):
            state[kind, 8 + m : 9 + m, :] = tri[:, 128 * m : 128 * m + 128]
        state[kind, 13:14, :] = mix[...]
        state[kind, 14:15, 0:64] = dist[...]
        state[kind, 14:15, 64:66] = gain[...]
        state[kind, 16:24, 0:vocab] = emb[...]
        state[kind, 24:32, 0:64] = ab[...]

    keep(0)
    ea[0:8, 0:vocab] = rounded(held[3][...])
    ea[0:8, 64:128] = rounded(held[4][...])
    low = state[0, 0:16, :].astype(bf16)
    low_ea = ea[...].astype(bf16)
    for m in range(depth_size):
        tstage[m, :, 0:48] = tgt[m, 0:16, :].astype(f32)
        tstage[m, :, 64:112] = tgt[m, 8:24, :].astype(f32)
        stage[m, 0:16, :] = low
        stage[m, 16:32, :] = tstage[m].astype(bf16)
        stage[m, 32:48, :] = low_ea
    pl.semaphore_wait(barrier, 1 + len(deep) + len(line_x) + len(line_y))
    for peer in line_x:
        pl.semaphore_signal(ready, inc=1, device_id=peer, device_id_type=MESH)

    copies = start(
        [
            remote(stage.at[peer[1] // 2], taken.at[depth], sz.at[k], rz.at[k], peer)
            for k, peer in enumerate(deep)
        ]
    )
    taken[depth] = stage[depth]
    keep(1)
    keep(2)
    wait(copies)
    for m in range(depth_size):
        source[16 * m : 16 * m + 16, :] = taken[m, 0:16, :]
        targets_in[core, m] = taken[m, 16:32, :]
    source[64:96, :] = jnp.concatenate(
        [taken[m, 32:48, :].astype(f32)[0:8] for m in range(depth_size)], axis=0
    ).astype(bf16)
    pl.semaphore_wait(ready, len(line_x))
    wide_copies = start(
        [
            remote(source, gathered.at[core, wide], sg.at[k], rg.at[k], peer)
            for k, peer in enumerate(flat)
        ]
    )
    moved = start([remote(targets_in.at[core], targets_in.at[core], st, rt, partner)])
    gathered[core, wide] = source[...]
    core_copies = start(
        [remote(source, gathered.at[core, wide], sc.at[0], rc.at[0], partner)]
    )

    tb[table:, :] = jnp.zeros((kinds * kinds - table, 128), f32)
    gb[vocab * kinds :, :] = jnp.zeros((table - vocab * kinds, 128), f32)
    du[32 * parts_all :, :] = jnp.zeros((32 * (48 - parts_all), 128), f32)
    grads[pl.ds(15, 128, stride=16), :] = jnp.zeros((128, 128), f32)
    wait(moved)
    for m in range(depth_size):
        for side in range(2):
            piece = targets_in[side, m].astype(f32)
            piece = jnp.where(core == 0, piece[:, 0:48], piece[:, 64:112])
            at = 48 * (2 * m + side)
            tg[:, at : at + 48] = piece
    row0 = wide * 24 + core * own_rows
    tok_row = tok_v[pl.ds(depth, 1), :]
    seg_row = seg_v[pl.ds(depth, 1), :]
    hot = (lax.broadcasted_iota(jnp.int32, (kinds, length), 0) == tok_row).astype(f32).astype(bf16)
    bin_of = lax.broadcasted_iota(jnp.int32, (bins, length), 0).astype(f32)
    line = lax.broadcasted_iota(jnp.int32, (48, kinds), 0)
    kind_of = line
    for i in range(own_rows):
        kind_of = jnp.where(line == groups + i, tok_s[depth, row0 + i], kind_of)
    pick = (kind_of == lax.broadcasted_iota(jnp.int32, (48, kinds), 1)).astype(f32).astype(bf16)
    for i in range(own_rows):
        here = slice(kinds * i, kinds * i + kinds)
        wanted = jnp.where(seg_row == seg_s[depth, row0 + i], tg[pl.ds(4 * core + i, 1), :], -1.0)
        counts = dot(hot, (bin_of == wanted).astype(f32).astype(bf16), 1, 1)
        hist[here, :] = counts
        many[here, :] = jnp.broadcast_to(jnp.sum(counts, -1, keepdims=True), (kinds, 128))
    count = jnp.zeros((4, 1), f32)
    for s in range(6):
        members = jnp.sum((seg_v[...] == s).astype(f32), axis=1, keepdims=True)
        count = count + members * members
    count = jnp.sum(count, axis=0, keepdims=True)

    def unpack(side, m):
        for deep_at in range(depth_size):
            at = pl.ds(pl.multiple_of(16 * (8 * m + 2 * deep_at + side), 16), 16)
            weights[at, :] = gathered[side, m, 16 * deep_at : 16 * deep_at + 16, :].astype(f32)

    unpack(core, wide)
    for k in reversed(range(wide_size - 1)):
        wide_copies[k].wait_recv()
        slot = gathered.at[core, flat_from[k]]
        core_copies += start([remote(slot, slot, sc.at[k + 1], rc.at[k + 1], partner)])
        unpack(core, flat_from[k])
    for copy, m in zip(core_copies, [wide] + flat_from[::-1]):
        copy.wait_recv()
        unpack(1 - core, m)
    for copy in wide_copies + core_copies:
        copy.wait_send()
    shards = gathered[:, :, 64:96, :].reshape(2 * wide_size * 32, 128)
    gram[...] = dot(shards, shards, 0, 0)
    a = dot(pick, gram[0:kinds, 64:96].astype(bf16), 1, 0).astype(bf16)
    b = gram[0:kinds, 96:128].astype(bf16)
    w_outer = jnp.concatenate(
        [weights[pl.ds(16 * (q // 8) + q % 8, 32, stride=64), :] for q in range(32)], axis=1
    ).astype(bf16)
    w_own = jnp.concatenate(
        [weights[pl.ds(8 + m, 128, stride=16), :] for m in (0, 1, 4)], axis=1
    ).astype(bf16)
    w_other = jnp.concatenate(
        [weights[pl.ds(8 + m, 128, stride=16), :] for m in (2, 3)], axis=1
    ).astype(bf16)
    w_mix = weights[pl.ds(13, 128, stride=16), :].astype(bf16)
    tail_t = weights[pl.ds(14, 128, stride=16), :].T
    dist_t = tail_t[0:bins, :].astype(bf16)
    gain_in = tail_t[64:65, :]
    gain_mid = tail_t[65:66, :]

    u_q = rounded(dot(a, w_outer, 1, 0))
    for q in range(32):
        u[pl.ds(q, 48, stride=32), :] = u_q[:, 128 * q : 128 * q + 128]
    u_all = jnp.concatenate([u[32 * t : 32 * t + 32, :] for t in range(parts_all)], axis=1).astype(bf16)
    z_cat = dot(b, u_all, 1, 0)
    pairs = jnp.concatenate([z_cat[:, 128 * t : 128 * t + 128] for t in range(groups)], axis=0)
    own_pairs = jnp.concatenate(
        [z_cat[:, 128 * t : 128 * t + 128] for t in range(groups, parts_all)], axis=0
    )
    z[...] = own_pairs

    center = pairs - jnp.mean(pairs, -1, keepdims=True)
    inverse = lax.rsqrt(jnp.mean(center * center, -1, keepdims=True) + norm_eps)
    scaled = center * inverse
    normed = (scaled * gain_in).astype(bf16)
    xhat[...] = scaled
    rstd[...] = jnp.broadcast_to(inverse, scaled.shape)
    zn[...] = normed
    projected = dot(normed, w_other, 1, 0)
    gate = jax.nn.sigmoid(projected[:, 0:128])
    value = projected[:, 128:256]
    sb[...] = gate
    pb[...] = value
    tb[0:table, :] = rounded(gate * value)

    center = own_pairs - jnp.mean(own_pairs, -1, keepdims=True)
    inverse = lax.rsqrt(jnp.mean(center * center, -1, keepdims=True) + norm_eps)
    scaled = center * inverse
    xi[...] = scaled
    ri[...] = jnp.broadcast_to(inverse, scaled.shape)
    normed = (scaled * gain_in).astype(bf16)
    zr[...] = normed
    projected = dot(normed, w_own, 1, 0)
    gate = jax.nn.sigmoid(projected[:, 0:128])
    value = projected[:, 128:256]
    sr[...] = gate
    pr[...] = value
    wa[...] = many[...] * rounded(gate * value)
    gate_out = jax.nn.sigmoid(projected[:, 256:384])

    for group in range(own_rows // columns_by):
        mine = range(columns_by * group, columns_by * group + columns_by)

        def product(v, sums, mine=mine):
            edge = tb[pl.ds(v, kinds, stride=kinds), :]
            return tuple(
                total + wa[pl.ds(kinds * i + v, 1), :] * edge for total, i in zip(sums, mine)
            )

        sums = lax.fori_loop(
            0, vocab, product, (jnp.zeros((kinds, 128), f32),) * columns_by, unroll=33
        )
        for total, i in zip(sums, mine):
            x[kinds * i : kinds * i + kinds, :] = total

    values = x[...]
    center = values - jnp.mean(values, -1, keepdims=True)
    inverse = lax.rsqrt(jnp.mean(center * center, -1, keepdims=True) + norm_eps)
    scaled = center * inverse
    mixed = (scaled * gain_mid).astype(bf16)
    branch = dot(mixed, w_mix, 1, 0)
    update = (z[...] + gate_out * branch).astype(bf16)
    logits = dot(update, dist_t, 1, 1)
    top = jnp.max(logits, -1, keepdims=True)
    powers = jnp.exp(logits - top)
    power_sum = jnp.sum(powers, -1, keepdims=True)
    counts = hist[...]
    loss = jnp.sum(many[:, 0:1] * (jnp.log(power_sum) + top), axis=0, keepdims=True) - whole_sum(
        counts * logits
    )
    grad_logits = ((many[:, 0:bins] * (powers / power_sum) - counts) / count).astype(bf16)
    grad_dist_t = dot(grad_logits, update, 0, 0)
    grad_update = dot(grad_logits, dist_t, 1, 0)
    grad_branch = (grad_update * gate_out).astype(bf16)
    dz1[...] = grad_update
    dpr[:, 256:384] = (grad_update * branch * gate_out * (1.0 - gate_out)).astype(bf16)
    grad_mix = dot(mixed, grad_branch, 0, 0)
    grad_mixed = dot(grad_branch, w_mix, 1, 1)
    grad_gain_mid = jnp.sum(grad_mixed * scaled, axis=0, keepdims=True)
    grad_hat = grad_mixed * gain_mid
    dx[...] = inverse * (
        grad_hat
        - jnp.mean(grad_hat, -1, keepdims=True)
        - scaled * jnp.mean(grad_hat * scaled, -1, keepdims=True)
    )

    for group in range(own_rows // side_by_side):
        mine = range(side_by_side * group, side_by_side * group + side_by_side)

        def edges(t, sums, mine=mine, group=group):
            at = pl.ds(pl.multiple_of(t * kinds, 8), kinds)
            edge = tb[at, :]
            right = gb[at, :] if group else jnp.zeros((kinds, 128), f32)
            news = []
            for total, i in zip(sums, mine):
                grad = dx[pl.ds(kinds * i + t, 1), :]
                news.append(total + grad * edge)
                right = right + grad * wa[kinds * i : kinds * i + kinds, :]
            gb[at, :] = right
            return tuple(news)

        sums = lax.fori_loop(
            0, vocab, edges, (jnp.zeros((kinds, 128), f32),) * side_by_side, unroll=33
        )
        for total, i in zip(sums, mine):
            here = slice(kinds * i, kinds * i + kinds)
            gr[here, :] = total * many[here, :]

    def norm_back(grad_normed, scaled, inverse):
        grad_hat = grad_normed * gain_in
        return inverse * (
            grad_hat
            - jnp.mean(grad_hat, -1, keepdims=True)
            - scaled * jnp.mean(grad_hat * scaled, -1, keepdims=True)
        )

    gate = sr[...]
    grad = gr[...] * gate
    dpr[:, 0:128] = (grad * pr[...] * (1.0 - gate)).astype(bf16)
    dpr[:, 128:256] = grad.astype(bf16)
    grad_normed = dot(dpr[...], w_own, 1, 1)
    scaled = xi[...]
    grad_gain_in = jnp.sum(grad_normed * scaled, axis=0, keepdims=True)
    grad_own = dz1[...] + norm_back(grad_normed, scaled, ri[...])
    grad_tri_own = dot(zr[...], dpr[...], 0, 0)

    gate = sb[...]
    grad = gb[...] * gate
    dpt[:, 0:128] = (grad * pb[...] * (1.0 - gate)).astype(bf16)
    dpt[:, 128:256] = grad.astype(bf16)
    grad_normed = dot(dpt[...], w_other, 1, 1)
    scaled = xhat[...]
    grad_table = norm_back(grad_normed, scaled, rstd[...])
    grad_gain_in = grad_gain_in + jnp.sum(grad_normed * scaled, axis=0, keepdims=True)
    grad_tri_other = dot(zn[...], dpt[...], 0, 0)

    blocks = [grad_table[kinds * t : kinds * t + kinds, :] for t in range(groups)]
    blocks += [grad_own[kinds * i : kinds * i + kinds, :] for i in range(own_rows)]
    dz_all = jnp.concatenate(blocks, axis=1).astype(bf16)
    grad_u = dot(b, dz_all, 0, 0)
    for t in range(parts_all):
        du[32 * t : 32 * t + 32, :] = grad_u[:, 128 * t : 128 * t + 128]
    grad_b = dot(dz_all, u_all, 1, 1)
    du_all = jnp.concatenate(
        [du[pl.ds(q, 48, stride=32), :] for q in range(32)], axis=1
    ).astype(bf16)
    grad_outer = dot(a, du_all, 0, 0)
    grad_a_high, grad_a_low = halves(dot(du_all, w_outer, 1, 1))
    grad_a = dot(pick, grad_a_high, 0, 0) + dot(pick, grad_a_low, 0, 0)

    for q in range(32):
        grads[pl.ds(16 * (q // 8) + q % 8, 32, stride=64), :] = grad_outer[:, 128 * q : 128 * q + 128]
    for at, m in enumerate((0, 1, 4)):
        grads[pl.ds(8 + m, 128, stride=16), :] = grad_tri_own[:, 128 * at : 128 * at + 128]
    for at, m in enumerate((2, 3)):
        grads[pl.ds(8 + m, 128, stride=16), :] = grad_tri_other[:, 128 * at : 128 * at + 128]
    grads[pl.ds(13, 128, stride=16), :] = grad_mix
    grads[pl.ds(14, 128, stride=16), :] = jnp.concatenate(
        [grad_dist_t, grad_gain_in, grad_gain_mid, jnp.zeros((62, 128), f32)], axis=0
    ).T
    for side in range(2):
        for m in range(wide_size):
            for deep_at in range(depth_size):
                at = 16 * (8 * m + 2 * deep_at + side)
                packed[side, m, 16 * deep_at : 16 * deep_at + 16, :] = grads[at : at + 16, :].astype(bf16)
    d_block[...] = jnp.zeros_like(d_block)
    for side, values in ((0, grad_a), (1, grad_b)):
        d_block[side, :, 0:32] = values[0:16]
        d_block[side, :, 32:64] = values[16:32]
        d_block[side, 0:8, 64:96] = values[32:40]
    d_block[0, 0:1, 96:97] = loss

    d_copies = start([remote(d_block.at[1 - core], d_other, s2, r2, partner)])
    core_copies = []
    for k, dy in enumerate((2, 1, 3, 0)):
        at = pl.ds(lax.rem(row + dy, 4) * 4, 4)
        core_copies += start(
            [remote(packed.at[1 - core, at], other.at[at], s1.at[k], r1.at[k], partner)]
        )
    wait(d_copies)
    lane = lax.broadcasted_iota(jnp.int32, (16, 128), 1)

    def split_loss(block):
        held_loss = jnp.sum(jnp.where((lane >= 96) & (lane < 99), block, 0.0), axis=1, keepdims=True)
        high = rounded(held_loss)
        middle = rounded(held_loss - high)
        block = jnp.where(lane == 96, high, block)
        block = jnp.where(lane == 97, middle, block)
        return jnp.where(lane == 98, held_loss - high - middle, block).astype(bf16)

    small = split_loss(d_block[core] + d_other[...])
    copies = []
    for k, peer in enumerate(flat):
        if k in (0, 4, 8, 12):
            core_copies[k // 4].wait()
        sent[peer[0], 0:64, :] = (
            packed[core, peer[0]].astype(f32) + other[peer[0]].astype(f32)
        ).astype(bf16)
        sent[peer[0], 64:80, :] = small
        copies += start([remote(sent.at[peer[0]], taken_w.at[wide], s3.at[k], r3.at[k], peer)])
    taken_w[wide, 0:64, :] = (packed[core, wide].astype(f32) + other[wide].astype(f32)).astype(bf16)
    taken_w[wide, 64:80, :] = small
    wait(copies)
    total = taken_w[0].astype(f32)
    for m in range(1, wide_size):
        total = total + taken_w[m].astype(f32)
    sum_z[0:64, :] = total[0:64].astype(bf16)
    sum_z[64:80, :] = split_loss(total[64:80])
    copies = start(
        [
            remote(sum_z, taken_z.at[depth], s5.at[k], r5.at[k], peer)
            for k, peer in enumerate(deep)
        ]
    )
    taken_z[depth] = sum_z[...]
    wait(copies)
    total = taken_z[0].astype(f32)
    for m in range(1, depth_size):
        total = total + taken_z[m].astype(f32)
    square[...] = jnp.broadcast_to(whole_sum(total[0:64] * total[0:64]), square.shape)
    copies = []
    for k, peer in enumerate(flat + [(wide, narrow)]):
        for other_core, device in enumerate((narrow, across)):
            if k < wide_size - 1 or other_core:
                at = 2 * k + other_core
                copies += start(
                    [remote(square, squares.at[core, wide], s8.at[at], r8.at[at], (peer[0], device))]
                )
    d_final[...] = total[64:80]
    d_copies = start([remote(d_final, d_partner, s7, r7, partner)])
    squares[core, wide] = square[...]
    grads[0:64, :] = total[0:64]

    wait(d_copies)
    highest = lax.Precision.HIGHEST
    first = jnp.where(core == 0, d_final[...], d_partner[...])
    second = jnp.where(core == 0, d_partner[...], d_final[...])
    for side, values in ((0, first), (1, second)):
        at = slice(32 * side, 32 * side + 32)
        d_all[0:16, at] = values[:, 0:32]
        d_all[16:32, at] = values[:, 32:64]
        d_all[32:40, at] = values[0:8, 64:96]
    d_total = d_all[...]
    grad = x
    grad[0:16, :] = grads[pl.ds(pl.multiple_of(depth * 16, 16), 16), :]
    grad[16:32, :] = jnp.zeros((16, 128), f32)
    grad[16:24, 0:kinds] = dot(ea[0:8, 64:128], d_total, 1, 1, highest)
    grad[24:32, 0:64] = dot(ea[0:8, 0:kinds], d_total, 1, 0, highest)
    extra = whole_sum(dot(gram[0:kinds, 0:kinds], d_total, 1, 0, highest) * d_total)
    extra += whole_sum(dot(d_total, gram[64:128, 64:128], 1, 0, highest) * d_total)
    loss_sum = jnp.sum(first[0:1, 96:99], axis=1, keepdims=True)
    line = lax.broadcasted_iota(jnp.int32, (32, 128), 0)
    lane = lax.broadcasted_iota(jnp.int32, (32, 128), 1)
    slow = (line < 8) | (line >= 24)
    fast = ((line >= 16) & (line < 24)) | ((line == 14) & (lane >= 64))
    rate = jnp.where(slow, rates[1], jnp.where(fast, rates[0], rates[3]))
    weight = state[0]
    first_part = beta_one * state[1]
    second_part = beta_two * state[2]
    wait(copies)
    total = squares[0, 0] + squares[1, 0]
    for m in range(1, wide_size):
        total = total + (squares[0, m] + squares[1, m])
    norm = jnp.sqrt(total[0:1, 0:1] + extra)
    clipped = grad[0:32, :] * jnp.minimum(1.0, clip_level / norm)
    moment = first_part + (1.0 - beta_one) * clipped
    speed = second_part + (1.0 - beta_two) * clipped * clipped
    ratio = (
        moment
        / (1.0 - beta_one**step_count)
        / (jnp.sqrt(speed / (1.0 - beta_two**step_count)) + adam_eps)
    )
    out[0:32, :] = weight - rate * (ratio + decay_rate * weight)
    out[32:64, :] = moment
    out[64:96, :] = speed
    line = lax.broadcasted_iota(jnp.int32, (8, 128), 0)
    out[96:104, :] = jnp.where(line == 0, loss_sum, jnp.where(line == 1, count, norm))


def place_kernel(stepped, *outs):
    for at in range(3):
        outs[at][...] = stepped[96 + at : 97 + at, 0:1]
    for kind in range(3):
        emb, ab, outer, tri, mix, dist, gain = outs[3 + 7 * kind : 10 + 7 * kind]
        base = 32 * kind
        outer[...] = stepped[base : base + 8, :]
        for m in range(5):
            tri[:, 128 * m : 128 * m + 128] = stepped[base + 8 + m : base + 9 + m, :]
        mix[...] = stepped[base + 13 : base + 14, :]
        dist[...] = stepped[base + 14 : base + 15, 0:64]
        gain[...] = stepped[base + 14 : base + 15, 64:66]
        emb[...] = stepped[base + 16 : base + 24, 0:vocab]
        ab[...] = stepped[base + 24 : base + 32, 0:64]


def shape(*dims, dtype=f32):
    return jax.ShapeDtypeStruct(dims, dtype)


in_vmem = pl.BlockSpec(memory_space=pltpu.VMEM)


def step_call(*args):
    def sems(*dims):
        return [pltpu.SemaphoreType.DMA(dims), pltpu.SemaphoreType.DMA(dims)]

    def one():
        return [pltpu.SemaphoreType.DMA, pltpu.SemaphoreType.DMA]

    full = VMEM((table, 128), f32)
    mine = VMEM((own, 128), f32)
    block = VMEM((16, 128), f32)
    return pl.pallas_call(
        step_kernel,
        out_shape=shape(104, 128),
        in_specs=[pl.BlockSpec(memory_space=pl.ANY)] * len(args),
        out_specs=in_vmem,
        scratch_shapes=[
            *[VMEM(arg.shape, arg.dtype) for arg in args],
            pltpu.SMEM(args[0].shape, jnp.int32), pltpu.SMEM(args[1].shape, jnp.int32),
            pltpu.SemaphoreType.DMA((26,)),
            pltpu.SemaphoreType.REGULAR,
            VMEM((3, 32, 128), f32),
            VMEM((depth_size, 16, 128), f32),
            VMEM((depth_size, 48, 128), bf16),
            VMEM((depth_size, 48, 128), bf16),
            block,
            VMEM((2, depth_size, 16, 128), bf16),
            VMEM((96, 128), bf16),
            VMEM((2, wide_size, 96, 128), bf16),
            VMEM((2048, 128), f32),
            VMEM((128, 128), f32),
            VMEM((16, length), f32),
            VMEM((32 * 48, 128), f32),
            VMEM((own, 128), f32),
            full, full,
            VMEM((table, 128), bf16),
            full, full,
            VMEM((kinds * kinds, 128), f32),
            VMEM((own, bins), f32),
            mine, mine, mine, mine,
            VMEM((own, 128), bf16),
            mine, mine, mine, mine, mine, mine,
            full,
            VMEM((table, 256), bf16),
            VMEM((own, 384), bf16),
            VMEM((32 * 48, 128), f32),
            VMEM((2048, 128), f32),
            VMEM((2, wide_size, 64, 128), bf16),
            VMEM((wide_size, 64, 128), bf16),
            VMEM((wide_size, 80, 128), bf16),
            VMEM((wide_size, 80, 128), bf16),
            VMEM((80, 128), bf16),
            VMEM((depth_size, 80, 128), bf16),
            VMEM((2, 16, 128), f32),
            block, block, block,
            VMEM((kinds, 64), f32),
            VMEM((8, 128), f32),
            VMEM((2, wide_size, 8, 128), f32),
            *sems(depth_size), *sems(wide_size), *one(), *sems(wide_size),
            *sems(4), *one(), *sems(wide_size), *sems(depth_size), *one(), *sems(2 * wide_size),
        ],
        compiler_params=pltpu.CompilerParams(
            collective_id=0, has_side_effects=True, vmem_limit_bytes=LIMIT
        ),
        name="pair_step",
    )(*args)


def local(tokens, segments, targets, *state):
    state = list(state)
    for at in (0, 6, 7, 13, 14, 20):
        state[at] = state[at].T
    stepped = step_call(tokens, segments, targets, *state)
    shapes = [shape(*w.shape) for w in state[0:7]]
    outs = pl.pallas_call(
        place_kernel,
        out_shape=[shape(1, 1)] * 3 + shapes * 3,
        in_specs=[in_vmem],
        out_specs=[in_vmem] * 24,
        name="place_outputs",
    )(stepped)
    outs = [value.reshape(()) for value in outs[0:3]] + list(outs[3:])
    for at in (3, 9, 10, 16, 17, 23):
        outs[at] = outs[at].T
    return tuple(outs)


def solution(mesh):
    both = ("wide", "narrow")
    whole = (P(None, both), P(both, None), P(both, None), P(both, None), P(both, None), P(both, None), P(None, both))
    return jax.shard_map(
        local,
        mesh=mesh,
        in_specs=(P(), P(), P(None, "wide", "narrow")) + whole * 3,
        out_specs=(P(), P(), P()) + whole * 3,
        check_vma=False,
    )
```

```python
import functools

import jax
import jax.numpy as jnp
from jax import lax
from jax.experimental import pallas as pl
from jax.experimental.pallas import tpu as pltpu
from jax.sharding import PartitionSpec as P

norm_eps = 1e-05
clip_level = 0.001
beta_one = 0.9
beta_two = 0.999
adam_eps = 1e-10
decay_rate = 0.01
step_count = 10.0
rates = (0.5, 0.016, 0.016, 0.044, 0.044, 0.044, 0.5)

f32 = jnp.float32
bf16 = jnp.bfloat16
MESH = pl.DeviceIdType.MESH
VMEM = pltpu.VMEM
LIMIT = 56 * 1024 * 1024

vocab = 33
kinds = 40
groups = 34
table = groups * kinds
pitch = 40
side_by_side = 4
columns_by = 4
own_rows = 12
own = own_rows * kinds
parts_all = groups + own_rows
bins = 64
wide_size = 16
depth_size = 4
length = 384


def dot(a, b, axis_a, axis_b, precision=None):
    return lax.dot_general(
        a, b, (((axis_a,), (axis_b,)), ((), ())), precision=precision, preferred_element_type=f32
    )


def rounded(values):
    return values.astype(bf16).astype(f32)


def halves(values):
    high = values.astype(bf16)
    return high, (values - high.astype(f32)).astype(bf16)


def whole_sum(values):
    return jnp.sum(jnp.sum(values, axis=1, keepdims=True), axis=0, keepdims=True)


flat_steps = [(dy, dx) for dy in (2, 1, 3, 0) for dx in (2, 1, 3, 0) if (dy, dx) != (0, 0)]
deep_steps = (2, 1, 3)


def step_kernel(*refs):
    inputs, refs = refs[:24], refs[24:]
    out, refs = refs[0], refs[1:]
    held, refs = refs[:24], refs[24:]
    (
        tok_s, seg_s, loaded, ready,
        state, tstage, stage, taken, ea, targets_in, source, gathered,
        outer_rows, other_rows, gram, tg, u, z, xhat, rstd, zn, sb, pb, tb,
        hist, many, wa, xi, ri, zr, sr, pr, x, dx, dz1, gr, gb,
        dpt, dpr, du, outer_grads, other_grads, packed, other, sent, taken_w, sum_z, taken_z,
        d_block, d_other, d_final, d_partner, d_all, square, squares,
        sz, rz, sg, rg, st, rt, sc, rc, s1, r1, s2, r2, s3, r3, s5, r5, s7, r7, s8, r8,
    ) = refs
    wide = lax.axis_index("wide")
    narrow = lax.axis_index("narrow")
    depth = narrow // 2
    core = lax.rem(narrow, 2)
    row, column = wide // 4, lax.rem(wide, 4)

    def at_step(dy, dx):
        return lax.rem(row + dy, 4) * 4 + lax.rem(column + dx, 4)

    across = depth * 2 + 1 - core
    partner = (wide, across)
    deep = [(wide, lax.rem(depth + k, depth_size) * 2 + core) for k in deep_steps]
    flat = [(at_step(dy, dx), narrow) for dy, dx in flat_steps]
    flat_from = [at_step(4 - dy, 4 - dx) for dy, dx in flat_steps]

    barrier = pltpu.get_barrier_semaphore()
    line_x = [(at_step(0, d), narrow) for d in deep_steps]
    line_y = [(at_step(d, 0), narrow) for d in deep_steps]
    for peer in line_y + line_x + deep + [partner]:
        pl.semaphore_signal(barrier, inc=1, device_id=peer, device_id_type=MESH)

    loads = [pltpu.make_async_copy(a, b, loaded.at[k]) for k, (a, b) in enumerate(zip(inputs, held))]
    loads.append(pltpu.make_async_copy(inputs[0], tok_s, loaded.at[24]))
    loads.append(pltpu.make_async_copy(inputs[1], seg_s, loaded.at[25]))
    for load in loads:
        load.start()

    def remote(source_ref, target_ref, send, receive, peer):
        return pltpu.make_async_remote_copy(
            src_ref=source_ref, dst_ref=target_ref, send_sem=send, recv_sem=receive,
            device_id=peer, device_id_type=MESH,
        )

    def start(copies):
        for copy in copies:
            copy.start()
        return copies

    def wait(copies):
        for copy in copies:
            copy.wait()

    state[...] = jnp.zeros_like(state)
    tstage[...] = jnp.zeros_like(tstage)
    stage[...] = jnp.zeros_like(stage)
    ea[...] = jnp.zeros_like(ea)
    for load in loads:
        load.wait()
    tok_v, seg_v, tgt = held[0:3]
    def keep(kind):
        emb, ab, outer, tri, mix, dist, gain = held[3 + 7 * kind : 10 + 7 * kind]
        state[kind, 0:8, :] = outer[...]
        for m in range(5):
            state[kind, 8 + m : 9 + m, :] = tri[:, 128 * m : 128 * m + 128]
        state[kind, 13:14, :] = mix[...]
        state[kind, 14:15, 0:64] = dist[...]
        state[kind, 14:15, 64:66] = gain[...]
        state[kind, 16:24, 0:vocab] = emb[...]
        state[kind, 24:32, 0:64] = ab[...]

    keep(0)
    ea[0:8, 0:vocab] = rounded(held[3][...])
    ea[0:8, 64:128] = rounded(held[4][...])
    low = state[0, 0:16, :].astype(bf16)
    low_ea = ea[...].astype(bf16)
    for m in range(depth_size):
        tstage[m, :, 0:48] = tgt[m, 0:16, :].astype(f32)
        tstage[m, :, 64:112] = tgt[m, 8:24, :].astype(f32)
        stage[m, 0:16, :] = low
        stage[m, 16:32, :] = tstage[m].astype(bf16)
        stage[m, 32:48, :] = low_ea
    pl.semaphore_wait(barrier, 1 + len(deep) + len(line_x) + len(line_y))
    for peer in line_x:
        pl.semaphore_signal(ready, inc=1, device_id=peer, device_id_type=MESH)

    copies = start(
        [
            remote(stage.at[peer[1] // 2], taken.at[depth], sz.at[k], rz.at[k], peer)
            for k, peer in enumerate(deep)
        ]
    )
    taken[depth] = stage[depth]
    keep(1)
    keep(2)
    wait(copies)
    for m in range(depth_size):
        source[16 * m : 16 * m + 16, :] = taken[m, 0:16, :]
        targets_in[core, m] = taken[m, 16:32, :]
    source[64:96, :] = jnp.concatenate(
        [taken[m, 32:48, :].astype(f32)[0:8] for m in range(depth_size)], axis=0
    ).astype(bf16)
    pl.semaphore_wait(ready, len(line_x))
    wide_copies = start(
        [
            remote(source, gathered.at[core, wide], sg.at[k], rg.at[k], peer)
            for k, peer in enumerate(flat)
        ]
    )
    moved = start([remote(targets_in.at[core], targets_in.at[core], st, rt, partner)])
    gathered[core, wide] = source[...]
    core_copies = start(
        [remote(source, gathered.at[core, wide], sc.at[0], rc.at[0], partner)]
    )

    tb[table:, :] = jnp.zeros((kinds * kinds - table, 128), f32)
    gb[vocab * kinds :, :] = jnp.zeros((table - vocab * kinds, 128), f32)
    du[pitch * parts_all :, :] = jnp.zeros((pitch * (48 - parts_all), 128), f32)
    other_grads[pl.ds(7, 128, stride=8), :] = jnp.zeros((128, 128), f32)
    wait(moved)
    for m in range(depth_size):
        for side in range(2):
            piece = targets_in[side, m].astype(f32)
            piece = jnp.where(core == 0, piece[:, 0:48], piece[:, 64:112])
            at = 48 * (2 * m + side)
            tg[:, at : at + 48] = piece
    row0 = wide * 24 + core * own_rows
    tok_row = tok_v[pl.ds(depth, 1), :]
    seg_row = seg_v[pl.ds(depth, 1), :]
    hot = (lax.broadcasted_iota(jnp.int32, (kinds, length), 0) == tok_row).astype(f32).astype(bf16)
    bin_of = lax.broadcasted_iota(jnp.int32, (bins, length), 0).astype(f32)
    line = lax.broadcasted_iota(jnp.int32, (48, kinds), 0)
    kind_of = line
    for i in range(own_rows):
        kind_of = jnp.where(line == groups + i, tok_s[depth, row0 + i], kind_of)
    pick = (kind_of == lax.broadcasted_iota(jnp.int32, (48, kinds), 1)).astype(f32).astype(bf16)
    for i in range(own_rows):
        here = slice(kinds * i, kinds * i + kinds)
        wanted = jnp.where(seg_row == seg_s[depth, row0 + i], tg[pl.ds(4 * core + i, 1), :], -1.0)
        counts = dot(hot, (bin_of == wanted).astype(f32).astype(bf16), 1, 1)
        hist[here, :] = counts
        many[here, :] = jnp.broadcast_to(jnp.sum(counts, -1, keepdims=True), (kinds, 128))
    count = jnp.zeros((4, 1), f32)
    for s in range(6):
        members = jnp.sum((seg_v[...] == s).astype(f32), axis=1, keepdims=True)
        count = count + members * members
    count = jnp.sum(count, axis=0, keepdims=True)

    def unpack(side, m):
        for deep_at in range(depth_size):
            values = gathered[side, m, 16 * deep_at : 16 * deep_at + 16, :].astype(f32)
            at = pitch * (2 * m + deep_at // 2) + 8 * (2 * (deep_at % 2) + side)
            outer_rows[pl.ds(pl.multiple_of(at, 8), 8), :] = values[0:8]
            at = 8 * (8 * m + 2 * deep_at + side)
            other_rows[pl.ds(pl.multiple_of(at, 8), 8), :] = values[8:16]

    unpack(core, wide)
    for k in reversed(range(wide_size - 1)):
        wide_copies[k].wait_recv()
        slot = gathered.at[core, flat_from[k]]
        core_copies += start([remote(slot, slot, sc.at[k + 1], rc.at[k + 1], partner)])
        unpack(core, flat_from[k])
    shards = gathered[core, :, 64:96, :].reshape(wide_size * 32, 128)
    products = dot(shards, shards, 0, 0)
    order = [wide] + flat_from[::-1]
    for first, last in ((0, 12), (12, 16)):
        for copy, m in zip(core_copies[first:last], order[first:last]):
            copy.wait_recv()
            unpack(1 - core, m)
        shards = jnp.concatenate([gathered[1 - core, m, 64:96, :] for m in order[first:last]], axis=0)
        products = products + dot(shards, shards, 0, 0)
    gram[...] = products
    for copy in wide_copies + core_copies:
        copy.wait_send()
    a = dot(pick, gram[0:kinds, 64:96].astype(bf16), 1, 0).astype(bf16)
    b = gram[0:kinds, 96:128].astype(bf16)
    w_outer = jnp.concatenate(
        [outer_rows[pl.ds(q, 32, stride=pitch), :] for q in range(32)], axis=1
    ).astype(bf16)
    w_own = jnp.concatenate(
        [other_rows[pl.ds(m, 128, stride=8), :] for m in (0, 1, 4)], axis=1
    ).astype(bf16)
    w_other = jnp.concatenate(
        [other_rows[pl.ds(m, 128, stride=8), :] for m in (2, 3)], axis=1
    ).astype(bf16)
    w_mix = other_rows[pl.ds(5, 128, stride=8), :].astype(bf16)
    tail_t = other_rows[pl.ds(6, 128, stride=8), :].T
    dist_t = tail_t[0:bins, :].astype(bf16)
    gain_in = tail_t[64:65, :]
    gain_mid = tail_t[65:66, :]

    u_q = rounded(dot(a, w_outer, 1, 0))
    for q in range(32):
        u[pl.ds(q, 48, stride=pitch), :] = u_q[:, 128 * q : 128 * q + 128]
    u_all = jnp.concatenate([u[pitch * t : pitch * t + 32, :] for t in range(parts_all)], axis=1).astype(bf16)
    z_cat = dot(b, u_all, 1, 0)
    pairs = jnp.concatenate([z_cat[:, 128 * t : 128 * t + 128] for t in range(groups)], axis=0)
    own_pairs = jnp.concatenate(
        [z_cat[:, 128 * t : 128 * t + 128] for t in range(groups, parts_all)], axis=0
    )
    z[...] = own_pairs

    center = pairs - jnp.mean(pairs, -1, keepdims=True)
    inverse = lax.rsqrt(jnp.mean(center * center, -1, keepdims=True) + norm_eps)
    scaled = center * inverse
    normed = (scaled * gain_in).astype(bf16)
    xhat[...] = scaled
    rstd[...] = jnp.broadcast_to(inverse, scaled.shape)
    zn[...] = normed
    projected = dot(normed, w_other, 1, 0)
    gate = jax.nn.sigmoid(projected[:, 0:128])
    value = projected[:, 128:256]
    sb[...] = gate
    pb[...] = value
    tb[0:table, :] = rounded(gate * value)

    center = own_pairs - jnp.mean(own_pairs, -1, keepdims=True)
    inverse = lax.rsqrt(jnp.mean(center * center, -1, keepdims=True) + norm_eps)
    scaled = center * inverse
    xi[...] = scaled
    ri[...] = jnp.broadcast_to(inverse, scaled.shape)
    normed = (scaled * gain_in).astype(bf16)
    zr[...] = normed
    projected = dot(normed, w_own, 1, 0)
    gate = jax.nn.sigmoid(projected[:, 0:128])
    value = projected[:, 128:256]
    sr[...] = gate
    pr[...] = value
    wa[...] = many[...] * rounded(gate * value)
    gate_out = jax.nn.sigmoid(projected[:, 256:384])

    for group in range(own_rows // columns_by):
        mine = range(columns_by * group, columns_by * group + columns_by)

        def product(v, sums, mine=mine):
            edge = tb[pl.ds(v, kinds, stride=kinds), :]
            return tuple(
                total + wa[pl.ds(kinds * i + v, 1), :] * edge for total, i in zip(sums, mine)
            )

        sums = lax.fori_loop(
            0, vocab, product, (jnp.zeros((kinds, 128), f32),) * columns_by, unroll=33
        )
        for total, i in zip(sums, mine):
            x[kinds * i : kinds * i + kinds, :] = total

    values = x[...]
    center = values - jnp.mean(values, -1, keepdims=True)
    inverse = lax.rsqrt(jnp.mean(center * center, -1, keepdims=True) + norm_eps)
    scaled = center * inverse
    mixed = (scaled * gain_mid).astype(bf16)
    branch = dot(mixed, w_mix, 1, 0)
    update = (z[...] + gate_out * branch).astype(bf16)
    logits = dot(update, dist_t, 1, 1)
    top = jnp.max(logits, -1, keepdims=True)
    powers = jnp.exp(logits - top)
    power_sum = jnp.sum(powers, -1, keepdims=True)
    counts = hist[...]
    loss = jnp.sum(many[:, 0:1] * (jnp.log(power_sum) + top), axis=0, keepdims=True) - whole_sum(
        counts * logits
    )
    grad_logits = ((many[:, 0:bins] * (powers / power_sum) - counts) / count).astype(bf16)
    grad_dist_t = dot(grad_logits, update, 0, 0)
    grad_update = dot(grad_logits, dist_t, 1, 0)
    grad_branch = (grad_update * gate_out).astype(bf16)
    dz1[...] = grad_update
    dpr[:, 256:384] = (grad_update * branch * gate_out * (1.0 - gate_out)).astype(bf16)
    grad_mix = dot(mixed, grad_branch, 0, 0)
    grad_mixed = dot(grad_branch, w_mix, 1, 1)
    grad_gain_mid = jnp.sum(grad_mixed * scaled, axis=0, keepdims=True)
    grad_hat = grad_mixed * gain_mid
    dx[...] = inverse * (
        grad_hat
        - jnp.mean(grad_hat, -1, keepdims=True)
        - scaled * jnp.mean(grad_hat * scaled, -1, keepdims=True)
    )

    for group in range(own_rows // side_by_side):
        mine = range(side_by_side * group, side_by_side * group + side_by_side)

        def edges(t, sums, mine=mine, group=group):
            at = pl.ds(pl.multiple_of(t * kinds, 8), kinds)
            edge = tb[at, :]
            right = gb[at, :] if group else jnp.zeros((kinds, 128), f32)
            news = []
            for total, i in zip(sums, mine):
                grad = dx[pl.ds(kinds * i + t, 1), :]
                news.append(total + grad * edge)
                right = right + grad * wa[kinds * i : kinds * i + kinds, :]
            gb[at, :] = right
            return tuple(news)

        sums = lax.fori_loop(
            0, vocab, edges, (jnp.zeros((kinds, 128), f32),) * side_by_side, unroll=33
        )
        for total, i in zip(sums, mine):
            here = slice(kinds * i, kinds * i + kinds)
            gr[here, :] = total * many[here, :]

    def norm_back(grad_normed, scaled, inverse):
        grad_hat = grad_normed * gain_in
        return inverse * (
            grad_hat
            - jnp.mean(grad_hat, -1, keepdims=True)
            - scaled * jnp.mean(grad_hat * scaled, -1, keepdims=True)
        )

    gate = sr[...]
    grad = gr[...] * gate
    dpr[:, 0:128] = (grad * pr[...] * (1.0 - gate)).astype(bf16)
    dpr[:, 128:256] = grad.astype(bf16)
    grad_normed = dot(dpr[...], w_own, 1, 1)
    scaled = xi[...]
    grad_gain_in = jnp.sum(grad_normed * scaled, axis=0, keepdims=True)
    grad_own = dz1[...] + norm_back(grad_normed, scaled, ri[...])
    grad_tri_own = dot(zr[...], dpr[...], 0, 0)

    gate = sb[...]
    grad = gb[...] * gate
    dpt[:, 0:128] = (grad * pb[...] * (1.0 - gate)).astype(bf16)
    dpt[:, 128:256] = grad.astype(bf16)
    grad_normed = dot(dpt[...], w_other, 1, 1)
    scaled = xhat[...]
    grad_table = norm_back(grad_normed, scaled, rstd[...])
    grad_gain_in = grad_gain_in + jnp.sum(grad_normed * scaled, axis=0, keepdims=True)
    grad_tri_other = dot(zn[...], dpt[...], 0, 0)

    blocks = [grad_table[kinds * t : kinds * t + kinds, :] for t in range(groups)]
    blocks += [grad_own[kinds * i : kinds * i + kinds, :] for i in range(own_rows)]
    dz_all = jnp.concatenate(blocks, axis=1).astype(bf16)
    grad_u = dot(b, dz_all, 0, 0)
    for t in range(parts_all):
        du[pitch * t : pitch * t + 32, :] = grad_u[:, 128 * t : 128 * t + 128]
    grad_b = dot(dz_all, u_all, 1, 1)
    du_all = jnp.concatenate(
        [du[pl.ds(q, 48, stride=pitch), :] for q in range(32)], axis=1
    ).astype(bf16)
    grad_outer = dot(a, du_all, 0, 0)
    grad_a_high, grad_a_low = halves(dot(du_all, w_outer, 1, 1))
    grad_a = dot(pick, grad_a_high, 0, 0) + dot(pick, grad_a_low, 0, 0)

    for q in range(32):
        outer_grads[pl.ds(q, 32, stride=pitch), :] = grad_outer[:, 128 * q : 128 * q + 128]
    for at, m in enumerate((0, 1, 4)):
        other_grads[pl.ds(m, 128, stride=8), :] = grad_tri_own[:, 128 * at : 128 * at + 128]
    for at, m in enumerate((2, 3)):
        other_grads[pl.ds(m, 128, stride=8), :] = grad_tri_other[:, 128 * at : 128 * at + 128]
    other_grads[pl.ds(5, 128, stride=8), :] = grad_mix
    other_grads[pl.ds(6, 128, stride=8), :] = jnp.concatenate(
        [grad_dist_t, grad_gain_in, grad_gain_mid, jnp.zeros((62, 128), f32)], axis=0
    ).T
    for side in range(2):
        for m in range(wide_size):
            for deep_at in range(depth_size):
                at = pitch * (2 * m + deep_at // 2) + 8 * (2 * (deep_at % 2) + side)
                values = [outer_grads[at : at + 8, :]]
                at = 8 * (8 * m + 2 * deep_at + side)
                values.append(other_grads[at : at + 8, :])
                packed[side, m, 16 * deep_at : 16 * deep_at + 16, :] = jnp.concatenate(values, axis=0).astype(bf16)
    d_block[...] = jnp.zeros_like(d_block)
    for side, values in ((0, grad_a), (1, grad_b)):
        d_block[side, :, 0:32] = values[0:16]
        d_block[side, :, 32:64] = values[16:32]
        d_block[side, 0:8, 64:96] = values[32:40]
    d_block[0, 0:1, 96:97] = loss

    d_copies = start([remote(d_block.at[1 - core], d_other, s2, r2, partner)])
    core_copies = []
    for k, dy in enumerate((2, 1, 3, 0)):
        at = pl.ds(lax.rem(row + dy, 4) * 4, 4)
        core_copies += start(
            [remote(packed.at[1 - core, at], other.at[at], s1.at[k], r1.at[k], partner)]
        )
    wait(d_copies)
    lane = lax.broadcasted_iota(jnp.int32, (16, 128), 1)

    def split_loss(block):
        held_loss = jnp.sum(jnp.where((lane >= 96) & (lane < 99), block, 0.0), axis=1, keepdims=True)
        high = rounded(held_loss)
        middle = rounded(held_loss - high)
        block = jnp.where(lane == 96, high, block)
        block = jnp.where(lane == 97, middle, block)
        return jnp.where(lane == 98, held_loss - high - middle, block).astype(bf16)

    small = split_loss(d_block[core] + d_other[...])
    copies = []
    for k, peer in enumerate(flat):
        if k in (0, 4, 8, 12):
            core_copies[k // 4].wait()
        sent[peer[0], 0:64, :] = (
            packed[core, peer[0]].astype(f32) + other[peer[0]].astype(f32)
        ).astype(bf16)
        sent[peer[0], 64:80, :] = small
        copies += start([remote(sent.at[peer[0]], taken_w.at[wide], s3.at[k], r3.at[k], peer)])
    taken_w[wide, 0:64, :] = (packed[core, wide].astype(f32) + other[wide].astype(f32)).astype(bf16)
    taken_w[wide, 64:80, :] = small
    wait(copies)
    total = taken_w[0].astype(f32)
    for m in range(1, wide_size):
        total = total + taken_w[m].astype(f32)
    sum_z[0:64, :] = total[0:64].astype(bf16)
    sum_z[64:80, :] = split_loss(total[64:80])
    copies = start(
        [
            remote(sum_z, taken_z.at[depth], s5.at[k], r5.at[k], peer)
            for k, peer in enumerate(deep)
        ]
    )
    taken_z[depth] = sum_z[...]
    wait(copies)
    total = taken_z[0].astype(f32)
    for m in range(1, depth_size):
        total = total + taken_z[m].astype(f32)
    square[...] = jnp.broadcast_to(whole_sum(total[0:64] * total[0:64]), square.shape)
    copies = []
    for k, peer in enumerate(flat + [(wide, narrow)]):
        for other_core, device in enumerate((narrow, across)):
            if k < wide_size - 1 or other_core:
                at = 2 * k + other_core
                copies += start(
                    [remote(square, squares.at[core, wide], s8.at[at], r8.at[at], (peer[0], device))]
                )
    d_final[...] = total[64:80]
    d_copies = start([remote(d_final, d_partner, s7, r7, partner)])
    squares[core, wide] = square[...]
    other_grads[0:64, :] = total[0:64]

    wait(d_copies)
    highest = lax.Precision.HIGHEST
    first = jnp.where(core == 0, d_final[...], d_partner[...])
    second = jnp.where(core == 0, d_partner[...], d_final[...])
    for side, values in ((0, first), (1, second)):
        at = slice(32 * side, 32 * side + 32)
        d_all[0:16, at] = values[:, 0:32]
        d_all[16:32, at] = values[:, 32:64]
        d_all[32:40, at] = values[0:8, 64:96]
    d_total = d_all[...]
    grad = x
    grad[0:16, :] = other_grads[pl.ds(pl.multiple_of(depth * 16, 16), 16), :]
    grad[16:32, :] = jnp.zeros((16, 128), f32)
    grad[16:24, 0:kinds] = dot(ea[0:8, 64:128], d_total, 1, 1, highest)
    grad[24:32, 0:64] = dot(ea[0:8, 0:kinds], d_total, 1, 0, highest)
    extra = whole_sum(dot(gram[0:kinds, 0:kinds], d_total, 1, 0, highest) * d_total)
    extra += whole_sum(dot(d_total, gram[64:128, 64:128], 1, 0, highest) * d_total)
    loss_sum = jnp.sum(first[0:1, 96:99], axis=1, keepdims=True)
    line = lax.broadcasted_iota(jnp.int32, (32, 128), 0)
    lane = lax.broadcasted_iota(jnp.int32, (32, 128), 1)
    slow = (line < 8) | (line >= 24)
    fast = ((line >= 16) & (line < 24)) | ((line == 14) & (lane >= 64))
    rate = jnp.where(slow, rates[1], jnp.where(fast, rates[0], rates[3]))
    weight = state[0]
    first_part = beta_one * state[1]
    second_part = beta_two * state[2]
    wait(copies)
    total = squares[0, 0] + squares[1, 0]
    for m in range(1, wide_size):
        total = total + (squares[0, m] + squares[1, m])
    norm = jnp.sqrt(total[0:1, 0:1] + extra)
    clipped = grad[0:32, :] * jnp.minimum(1.0, clip_level / norm)
    moment = first_part + (1.0 - beta_one) * clipped
    speed = second_part + (1.0 - beta_two) * clipped * clipped
    ratio = (
        moment
        / (1.0 - beta_one**step_count)
        / (jnp.sqrt(speed / (1.0 - beta_two**step_count)) + adam_eps)
    )
    out[0:32, :] = weight - rate * (ratio + decay_rate * weight)
    out[32:64, :] = moment
    out[64:96, :] = speed
    line = lax.broadcasted_iota(jnp.int32, (8, 128), 0)
    out[96:104, :] = jnp.where(line == 0, loss_sum, jnp.where(line == 1, count, norm))


def place_kernel(stepped, *outs):
    for at in range(3):
        outs[at][...] = stepped[96 + at : 97 + at, 0:1]
    for kind in range(3):
        emb, ab, outer, tri, mix, dist, gain = outs[3 + 7 * kind : 10 + 7 * kind]
        base = 32 * kind
        outer[...] = stepped[base : base + 8, :]
        for m in range(5):
            tri[:, 128 * m : 128 * m + 128] = stepped[base + 8 + m : base + 9 + m, :]
        mix[...] = stepped[base + 13 : base + 14, :]
        dist[...] = stepped[base + 14 : base + 15, 0:64]
        gain[...] = stepped[base + 14 : base + 15, 64:66]
        emb[...] = stepped[base + 16 : base + 24, 0:vocab]
        ab[...] = stepped[base + 24 : base + 32, 0:64]


def shape(*dims, dtype=f32):
    return jax.ShapeDtypeStruct(dims, dtype)


in_vmem = pl.BlockSpec(memory_space=pltpu.VMEM)


def step_call(*args):
    def sems(*dims):
        return [pltpu.SemaphoreType.DMA(dims), pltpu.SemaphoreType.DMA(dims)]

    def one():
        return [pltpu.SemaphoreType.DMA, pltpu.SemaphoreType.DMA]

    full = VMEM((table, 128), f32)
    mine = VMEM((own, 128), f32)
    block = VMEM((16, 128), f32)
    return pl.pallas_call(
        step_kernel,
        out_shape=shape(104, 128),
        in_specs=[pl.BlockSpec(memory_space=pl.ANY)] * len(args),
        out_specs=in_vmem,
        scratch_shapes=[
            *[VMEM(arg.shape, arg.dtype) for arg in args],
            pltpu.SMEM(args[0].shape, jnp.int32), pltpu.SMEM(args[1].shape, jnp.int32),
            pltpu.SemaphoreType.DMA((26,)),
            pltpu.SemaphoreType.REGULAR,
            VMEM((3, 32, 128), f32),
            VMEM((depth_size, 16, 128), f32),
            VMEM((depth_size, 48, 128), bf16),
            VMEM((depth_size, 48, 128), bf16),
            block,
            VMEM((2, depth_size, 16, 128), bf16),
            VMEM((96, 128), bf16),
            VMEM((2, wide_size, 96, 128), bf16),
            VMEM((32 * pitch, 128), f32), VMEM((1024, 128), f32),
            VMEM((128, 128), f32),
            VMEM((16, length), f32),
            VMEM((pitch * 48, 128), f32),
            VMEM((own, 128), f32),
            full, full,
            VMEM((table, 128), bf16),
            full, full,
            VMEM((kinds * kinds, 128), f32),
            VMEM((own, bins), f32),
            mine, mine, mine, mine,
            VMEM((own, 128), bf16),
            mine, mine, mine, mine, mine, mine,
            full,
            VMEM((table, 256), bf16),
            VMEM((own, 384), bf16),
            VMEM((pitch * 48, 128), f32),
            VMEM((32 * pitch, 128), f32), VMEM((1024, 128), f32),
            VMEM((2, wide_size, 64, 128), bf16),
            VMEM((wide_size, 64, 128), bf16),
            VMEM((wide_size, 80, 128), bf16),
            VMEM((wide_size, 80, 128), bf16),
            VMEM((80, 128), bf16),
            VMEM((depth_size, 80, 128), bf16),
            VMEM((2, 16, 128), f32),
            block, block, block,
            VMEM((kinds, 64), f32),
            VMEM((8, 128), f32),
            VMEM((2, wide_size, 8, 128), f32),
            *sems(depth_size), *sems(wide_size), *one(), *sems(wide_size),
            *sems(4), *one(), *sems(wide_size), *sems(depth_size), *one(), *sems(2 * wide_size),
        ],
        compiler_params=pltpu.CompilerParams(
            collective_id=0, has_side_effects=True, vmem_limit_bytes=LIMIT
        ),
        name="pair_step",
    )(*args)


def local(tokens, segments, targets, *state):
    state = list(state)
    for at in (0, 6, 7, 13, 14, 20):
        state[at] = state[at].T
    stepped = step_call(tokens, segments, targets, *state)
    shapes = [shape(*w.shape) for w in state[0:7]]
    outs = pl.pallas_call(
        place_kernel,
        out_shape=[shape(1, 1)] * 3 + shapes * 3,
        in_specs=[in_vmem],
        out_specs=[in_vmem] * 24,
        name="place_outputs",
    )(stepped)
    outs = [value.reshape(()) for value in outs[0:3]] + list(outs[3:])
    for at in (3, 9, 10, 16, 17, 23):
        outs[at] = outs[at].T
    return tuple(outs)


def solution(mesh):
    both = ("wide", "narrow")
    whole = (P(None, both), P(both, None), P(both, None), P(both, None), P(both, None), P(both, None), P(None, both))
    return jax.shard_map(
        local,
        mesh=mesh,
        in_specs=(P(), P(), P(None, "wide", "narrow")) + whole * 3,
        out_specs=(P(), P(), P()) + whole * 3,
        check_vma=False,
    )
```

```python
import functools

import jax
import jax.numpy as jnp
from jax import lax
from jax.experimental import pallas as pl
from jax.experimental.pallas import tpu as pltpu
from jax.sharding import PartitionSpec as P

norm_eps = 1e-05
clip_level = 0.001
beta_one = 0.9
beta_two = 0.999
adam_eps = 1e-10
decay_rate = 0.01
step_count = 10.0
rates = (0.5, 0.016, 0.016, 0.044, 0.044, 0.044, 0.5)

f32 = jnp.float32
bf16 = jnp.bfloat16
MESH = pl.DeviceIdType.MESH
VMEM = pltpu.VMEM
LIMIT = 56 * 1024 * 1024

vocab = 33
kinds = 40
groups = 34
table = groups * kinds
pitch = 40
side_by_side = 4
columns_by = 4
own_rows = 12
own = own_rows * kinds
parts_all = groups + own_rows
bins = 64
wide_size = 16
depth_size = 4
length = 384


def dot(a, b, axis_a, axis_b, precision=None):
    return lax.dot_general(
        a, b, (((axis_a,), (axis_b,)), ((), ())), precision=precision, preferred_element_type=f32
    )


def rounded(values):
    return values.astype(bf16).astype(f32)


def halves(values):
    high = values.astype(bf16)
    return high, (values - high.astype(f32)).astype(bf16)


def whole_sum(values):
    return jnp.sum(jnp.sum(values, axis=0, keepdims=True), axis=1, keepdims=True)


flat_steps = [(dy, dx) for dy in (2, 1, 3, 0) for dx in (2, 1, 3, 0) if (dy, dx) != (0, 0)]
deep_steps = (2, 1, 3)


def step_kernel(*refs):
    inputs, refs = refs[:24], refs[24:]
    out, refs = refs[0], refs[1:]
    held, refs = refs[:24], refs[24:]
    (
        tok_s, seg_s, loaded, ready,
        state, tstage, stage, taken, ea, targets_in, source, gathered,
        outer_rows, other_rows, gram, tg, u, z, xhat, rstd, zn, sb, pb, tb,
        hist, many, wa, xi, ri, zr, sr, pr, x, dx, dz1, gr, gb,
        dpt, dpr, du, outer_grads, other_grads, packed, other, sent, taken_w, sum_z, taken_z,
        d_block, d_other, d_final, d_partner, d_all, square, squares,
        sz, rz, sg, rg, st, rt, sc, rc, s1, r1, s2, r2, s3, r3, s5, r5, s7, r7, s8, r8,
    ) = refs
    wide = lax.axis_index("wide")
    narrow = lax.axis_index("narrow")
    depth = narrow // 2
    core = lax.rem(narrow, 2)
    row, column = wide // 4, lax.rem(wide, 4)

    def at_step(dy, dx):
        return lax.rem(row + dy, 4) * 4 + lax.rem(column + dx, 4)

    across = depth * 2 + 1 - core
    partner = (wide, across)
    deep = [(wide, lax.rem(depth + k, depth_size) * 2 + core) for k in deep_steps]
    flat = [(at_step(dy, dx), narrow) for dy, dx in flat_steps]
    flat_from = [at_step(4 - dy, 4 - dx) for dy, dx in flat_steps]

    barrier = pltpu.get_barrier_semaphore()
    line_x = [(at_step(0, d), narrow) for d in deep_steps]
    line_y = [(at_step(d, 0), narrow) for d in deep_steps]
    for peer in line_y + line_x + deep + [partner]:
        pl.semaphore_signal(barrier, inc=1, device_id=peer, device_id_type=MESH)

    loads = [pltpu.make_async_copy(a, b, loaded.at[k]) for k, (a, b) in enumerate(zip(inputs, held))]
    loads.append(pltpu.make_async_copy(inputs[0], tok_s, loaded.at[24]))
    loads.append(pltpu.make_async_copy(inputs[1], seg_s, loaded.at[25]))
    for load in loads:
        load.start()

    def remote(source_ref, target_ref, send, receive, peer):
        return pltpu.make_async_remote_copy(
            src_ref=source_ref, dst_ref=target_ref, send_sem=send, recv_sem=receive,
            device_id=peer, device_id_type=MESH,
        )

    def start(copies):
        for copy in copies:
            copy.start()
        return copies

    def wait(copies):
        for copy in copies:
            copy.wait()

    state[...] = jnp.zeros_like(state)
    tstage[...] = jnp.zeros_like(tstage)
    stage[...] = jnp.zeros_like(stage)
    ea[...] = jnp.zeros_like(ea)
    for load in loads:
        load.wait()
    tok_v, seg_v, tgt = held[0:3]
    def keep(kind):
        emb, ab, outer, tri, mix, dist, gain = held[3 + 7 * kind : 10 + 7 * kind]
        state[kind, 0:8, :] = outer[...]
        for m in range(5):
            state[kind, 8 + m : 9 + m, :] = tri[:, 128 * m : 128 * m + 128]
        state[kind, 13:14, :] = mix[...]
        state[kind, 14:15, 0:64] = dist[...]
        state[kind, 14:15, 64:66] = gain[...]
        state[kind, 16:24, 0:vocab] = emb[...]
        state[kind, 24:32, 0:64] = ab[...]

    keep(0)
    ea[0:8, 0:vocab] = rounded(held[3][...])
    ea[0:8, 64:128] = rounded(held[4][...])
    low = state[0, 0:16, :].astype(bf16)
    low_ea = ea[...].astype(bf16)
    for m in range(depth_size):
        tstage[m, :, 0:48] = tgt[m, 0:16, :].astype(f32)
        tstage[m, :, 64:112] = tgt[m, 8:24, :].astype(f32)
        stage[m, 0:16, :] = low
        stage[m, 16:32, :] = tstage[m].astype(bf16)
        stage[m, 32:48, :] = low_ea
    pl.semaphore_wait(barrier, 1 + len(deep) + len(line_x) + len(line_y))
    for peer in line_x:
        pl.semaphore_signal(ready, inc=1, device_id=peer, device_id_type=MESH)

    copies = start(
        [
            remote(stage.at[peer[1] // 2], taken.at[depth], sz.at[k], rz.at[k], peer)
            for k, peer in enumerate(deep)
        ]
    )
    taken[depth] = stage[depth]
    keep(1)
    keep(2)
    wait(copies)
    for m in range(depth_size):
        source[16 * m : 16 * m + 16, :] = taken[m, 0:16, :]
        targets_in[core, m] = taken[m, 16:32, :]
    source[64:96, :] = jnp.concatenate(
        [taken[m, 32:48, :].astype(f32)[0:8] for m in range(depth_size)], axis=0
    ).astype(bf16)
    pl.semaphore_wait(ready, len(line_x))
    wide_copies = start(
        [
            remote(source, gathered.at[core, wide], sg.at[k], rg.at[k], peer)
            for k, peer in enumerate(flat)
        ]
    )
    moved = start([remote(targets_in.at[core], targets_in.at[core], st, rt, partner)])
    gathered[core, wide] = source[...]
    core_copies = start(
        [remote(source, gathered.at[core, wide], sc.at[0], rc.at[0], partner)]
    )

    tb[table:, :] = jnp.zeros((kinds * kinds - table, 128), f32)
    gb[vocab * kinds :, :] = jnp.zeros((table - vocab * kinds, 128), f32)
    du[pitch * parts_all :, :] = jnp.zeros((pitch * (48 - parts_all), 128), f32)
    other_grads[pl.ds(7, 128, stride=8), :] = jnp.zeros((128, 128), f32)
    wait(moved)
    for m in range(depth_size):
        for side in range(2):
            piece = targets_in[side, m].astype(f32)
            piece = jnp.where(core == 0, piece[:, 0:48], piece[:, 64:112])
            at = 48 * (2 * m + side)
            tg[:, at : at + 48] = piece
    row0 = wide * 24 + core * own_rows
    tok_row = tok_v[pl.ds(depth, 1), :]
    seg_row = seg_v[pl.ds(depth, 1), :]
    hot = (lax.broadcasted_iota(jnp.int32, (kinds, length), 0) == tok_row).astype(f32).astype(bf16)
    bin_of = lax.broadcasted_iota(jnp.int32, (bins, length), 0).astype(f32)
    line = lax.broadcasted_iota(jnp.int32, (48, kinds), 0)
    kind_of = line
    for i in range(own_rows):
        kind_of = jnp.where(line == groups + i, tok_s[depth, row0 + i], kind_of)
    pick = (kind_of == lax.broadcasted_iota(jnp.int32, (48, kinds), 1)).astype(f32).astype(bf16)
    for i in range(own_rows):
        here = slice(kinds * i, kinds * i + kinds)
        wanted = jnp.where(seg_row == seg_s[depth, row0 + i], tg[pl.ds(4 * core + i, 1), :], -1.0)
        counts = dot(hot, (bin_of == wanted).astype(f32).astype(bf16), 1, 1)
        hist[here, :] = counts
        many[here, :] = jnp.broadcast_to(jnp.sum(counts, -1, keepdims=True), (kinds, 128))
    count = jnp.zeros((4, 1), f32)
    for s in range(6):
        members = jnp.sum((seg_v[...] == s).astype(f32), axis=1, keepdims=True)
        count = count + members * members
    count = jnp.sum(count, axis=0, keepdims=True)

    def unpack(side, m):
        for deep_at in range(depth_size):
            values = gathered[side, m, 16 * deep_at : 16 * deep_at + 16, :].astype(f32)
            at = pitch * (2 * m + deep_at // 2) + 8 * (2 * (deep_at % 2) + side)
            outer_rows[pl.ds(pl.multiple_of(at, 8), 8), :] = values[0:8]
            at = 8 * (8 * m + 2 * deep_at + side)
            other_rows[pl.ds(pl.multiple_of(at, 8), 8), :] = values[8:16]

    unpack(core, wide)
    for k in reversed(range(wide_size - 1)):
        wide_copies[k].wait_recv()
        slot = gathered.at[core, flat_from[k]]
        core_copies += start([remote(slot, slot, sc.at[k + 1], rc.at[k + 1], partner)])
        unpack(core, flat_from[k])
    for copy, m in zip(core_copies, [wide] + flat_from[::-1]):
        copy.wait_recv()
        unpack(1 - core, m)
    for copy in wide_copies + core_copies:
        copy.wait_send()
    shards = gathered[:, :, 64:96, :].reshape(2 * wide_size * 32, 128)
    gram[...] = dot(shards, shards, 0, 0)
    a = dot(pick, gram[0:kinds, 64:96].astype(bf16), 1, 0).astype(bf16)
    b = gram[0:kinds, 96:128].astype(bf16)
    w_outer = jnp.concatenate(
        [outer_rows[pl.ds(q, 32, stride=pitch), :] for q in range(32)], axis=1
    ).astype(bf16)
    w_own = jnp.concatenate(
        [other_rows[pl.ds(m, 128, stride=8), :] for m in (0, 1, 4)], axis=1
    ).astype(bf16)
    w_other = jnp.concatenate(
        [other_rows[pl.ds(m, 128, stride=8), :] for m in (2, 3)], axis=1
    ).astype(bf16)
    w_mix = other_rows[pl.ds(5, 128, stride=8), :].astype(bf16)
    tail_t = other_rows[pl.ds(6, 128, stride=8), :].T
    dist_t = tail_t[0:bins, :].astype(bf16)
    gain_in = tail_t[64:65, :]
    gain_mid = tail_t[65:66, :]

    u_q = rounded(dot(a, w_outer, 1, 0))
    for q in range(32):
        u[pl.ds(q, 48, stride=pitch), :] = u_q[:, 128 * q : 128 * q + 128]
    u_all = jnp.concatenate([u[pitch * t : pitch * t + 32, :] for t in range(parts_all)], axis=1).astype(bf16)
    z_cat = dot(b, u_all, 1, 0)
    pairs = jnp.concatenate([z_cat[:, 128 * t : 128 * t + 128] for t in range(groups)], axis=0)
    own_pairs = jnp.concatenate(
        [z_cat[:, 128 * t : 128 * t + 128] for t in range(groups, parts_all)], axis=0
    )
    z[...] = own_pairs

    center = pairs - jnp.mean(pairs, -1, keepdims=True)
    inverse = lax.rsqrt(jnp.mean(center * center, -1, keepdims=True) + norm_eps)
    scaled = center * inverse
    normed = (scaled * gain_in).astype(bf16)
    xhat[...] = scaled
    rstd[...] = jnp.broadcast_to(inverse, scaled.shape)
    zn[...] = normed
    projected = dot(normed, w_other, 1, 0)
    gate = jax.nn.sigmoid(projected[:, 0:128])
    value = projected[:, 128:256]
    sb[...] = gate
    pb[...] = value
    tb[0:table, :] = rounded(gate * value)

    center = own_pairs - jnp.mean(own_pairs, -1, keepdims=True)
    inverse = lax.rsqrt(jnp.mean(center * center, -1, keepdims=True) + norm_eps)
    scaled = center * inverse
    xi[...] = scaled
    ri[...] = jnp.broadcast_to(inverse, scaled.shape)
    normed = (scaled * gain_in).astype(bf16)
    zr[...] = normed
    projected = dot(normed, w_own, 1, 0)
    gate = jax.nn.sigmoid(projected[:, 0:128])
    value = projected[:, 128:256]
    sr[...] = gate
    pr[...] = value
    wa[...] = many[...] * rounded(gate * value)
    gate_out = jax.nn.sigmoid(projected[:, 256:384])

    for group in range(own_rows // columns_by):
        mine = range(columns_by * group, columns_by * group + columns_by)

        def product(v, sums, mine=mine):
            edge = tb[pl.ds(v, kinds, stride=kinds), :]
            return tuple(
                total + wa[pl.ds(kinds * i + v, 1), :] * edge for total, i in zip(sums, mine)
            )

        sums = lax.fori_loop(
            0, vocab, product, (jnp.zeros((kinds, 128), f32),) * columns_by, unroll=33
        )
        for total, i in zip(sums, mine):
            x[kinds * i : kinds * i + kinds, :] = total

    values = x[...]
    center = values - jnp.mean(values, -1, keepdims=True)
    inverse = lax.rsqrt(jnp.mean(center * center, -1, keepdims=True) + norm_eps)
    scaled = center * inverse
    mixed = (scaled * gain_mid).astype(bf16)
    branch = dot(mixed, w_mix, 1, 0)
    update = (z[...] + gate_out * branch).astype(bf16)
    logits = dot(update, dist_t, 1, 1)
    top = jnp.max(logits, -1, keepdims=True)
    powers = jnp.exp(logits - top)
    power_sum = jnp.sum(powers, -1, keepdims=True)
    counts = hist[...]
    loss = jnp.sum(many[:, 0:1] * (jnp.log(power_sum) + top), axis=0, keepdims=True) - whole_sum(
        counts * logits
    )
    grad_logits = ((many[:, 0:bins] * (powers / power_sum) - counts) / count).astype(bf16)
    grad_dist_t = dot(grad_logits, update, 0, 0)
    grad_update = dot(grad_logits, dist_t, 1, 0)
    grad_branch = (grad_update * gate_out).astype(bf16)
    dz1[...] = grad_update
    dpr[:, 256:384] = (grad_update * branch * gate_out * (1.0 - gate_out)).astype(bf16)
    grad_mix = dot(mixed, grad_branch, 0, 0)
    grad_mixed = dot(grad_branch, w_mix, 1, 1)
    grad_gain_mid = jnp.sum(grad_mixed * scaled, axis=0, keepdims=True)
    grad_hat = grad_mixed * gain_mid
    dx[...] = inverse * (
        grad_hat
        - jnp.mean(grad_hat, -1, keepdims=True)
        - scaled * jnp.mean(grad_hat * scaled, -1, keepdims=True)
    )

    for group in range(own_rows // side_by_side):
        mine = range(side_by_side * group, side_by_side * group + side_by_side)

        def edges(t, sums, mine=mine, group=group):
            at = pl.ds(pl.multiple_of(t * kinds, 8), kinds)
            edge = tb[at, :]
            right = gb[at, :] if group else jnp.zeros((kinds, 128), f32)
            news = []
            for total, i in zip(sums, mine):
                grad = dx[pl.ds(kinds * i + t, 1), :]
                news.append(total + grad * edge)
                right = right + grad * wa[kinds * i : kinds * i + kinds, :]
            gb[at, :] = right
            return tuple(news)

        sums = lax.fori_loop(
            0, vocab, edges, (jnp.zeros((kinds, 128), f32),) * side_by_side, unroll=33
        )
        for total, i in zip(sums, mine):
            here = slice(kinds * i, kinds * i + kinds)
            gr[here, :] = total * many[here, :]

    def norm_back(grad_normed, scaled, inverse):
        grad_hat = grad_normed * gain_in
        return inverse * (
            grad_hat
            - jnp.mean(grad_hat, -1, keepdims=True)
            - scaled * jnp.mean(grad_hat * scaled, -1, keepdims=True)
        )

    gate = sr[...]
    grad = gr[...] * gate
    dpr[:, 0:128] = (grad * pr[...] * (1.0 - gate)).astype(bf16)
    dpr[:, 128:256] = grad.astype(bf16)
    grad_normed = dot(dpr[...], w_own, 1, 1)
    scaled = xi[...]
    grad_gain_in = jnp.sum(grad_normed * scaled, axis=0, keepdims=True)
    grad_own = dz1[...] + norm_back(grad_normed, scaled, ri[...])
    grad_tri_own = dot(zr[...], dpr[...], 0, 0)

    gate = sb[...]
    grad = gb[...] * gate
    dpt[:, 0:128] = (grad * pb[...] * (1.0 - gate)).astype(bf16)
    dpt[:, 128:256] = grad.astype(bf16)
    grad_normed = dot(dpt[...], w_other, 1, 1)
    scaled = xhat[...]
    grad_table = norm_back(grad_normed, scaled, rstd[...])
    grad_gain_in = grad_gain_in + jnp.sum(grad_normed * scaled, axis=0, keepdims=True)
    grad_tri_other = dot(zn[...], dpt[...], 0, 0)

    blocks = [grad_table[kinds * t : kinds * t + kinds, :] for t in range(groups)]
    blocks += [grad_own[kinds * i : kinds * i + kinds, :] for i in range(own_rows)]
    dz_all = jnp.concatenate(blocks, axis=1).astype(bf16)
    grad_u = dot(b, dz_all, 0, 0)
    for t in range(parts_all):
        du[pitch * t : pitch * t + 32, :] = grad_u[:, 128 * t : 128 * t + 128]
    grad_b = dot(dz_all, u_all, 1, 1)
    du_all = jnp.concatenate(
        [du[pl.ds(q, 48, stride=pitch), :] for q in range(32)], axis=1
    ).astype(bf16)
    grad_outer = dot(a, du_all, 0, 0)
    grad_a_high, grad_a_low = halves(dot(du_all, w_outer, 1, 1))
    grad_a = dot(pick, grad_a_high, 0, 0) + dot(pick, grad_a_low, 0, 0)

    for q in range(32):
        outer_grads[pl.ds(q, 32, stride=pitch), :] = grad_outer[:, 128 * q : 128 * q + 128]
    for at, m in enumerate((0, 1, 4)):
        other_grads[pl.ds(m, 128, stride=8), :] = grad_tri_own[:, 128 * at : 128 * at + 128]
    for at, m in enumerate((2, 3)):
        other_grads[pl.ds(m, 128, stride=8), :] = grad_tri_other[:, 128 * at : 128 * at + 128]
    other_grads[pl.ds(5, 128, stride=8), :] = grad_mix
    other_grads[pl.ds(6, 128, stride=8), :] = jnp.concatenate(
        [grad_dist_t, grad_gain_in, grad_gain_mid, jnp.zeros((62, 128), f32)], axis=0
    ).T
    for side in range(2):
        for m in range(wide_size):
            for deep_at in range(depth_size):
                at = pitch * (2 * m + deep_at // 2) + 8 * (2 * (deep_at % 2) + side)
                values = [outer_grads[at : at + 8, :]]
                at = 8 * (8 * m + 2 * deep_at + side)
                values.append(other_grads[at : at + 8, :])
                packed[side, m, 16 * deep_at : 16 * deep_at + 16, :] = jnp.concatenate(values, axis=0).astype(bf16)
    d_block[...] = jnp.zeros_like(d_block)
    for side, values in ((0, grad_a), (1, grad_b)):
        d_block[side, :, 0:32] = values[0:16]
        d_block[side, :, 32:64] = values[16:32]
        d_block[side, 0:8, 64:96] = values[32:40]
    d_block[0, 0:1, 96:97] = loss

    d_copies = start([remote(d_block.at[1 - core], d_other, s2, r2, partner)])
    core_copies = []
    for k, dy in enumerate((2, 1, 3, 0)):
        at = pl.ds(lax.rem(row + dy, 4) * 4, 4)
        core_copies += start(
            [remote(packed.at[1 - core, at], other.at[at], s1.at[k], r1.at[k], partner)]
        )
    wait(d_copies)
    lane = lax.broadcasted_iota(jnp.int32, (16, 128), 1)

    def split_loss(block):
        held_loss = jnp.sum(jnp.where((lane >= 96) & (lane < 99), block, 0.0), axis=1, keepdims=True)
        high = rounded(held_loss)
        middle = rounded(held_loss - high)
        block = jnp.where(lane == 96, high, block)
        block = jnp.where(lane == 97, middle, block)
        return jnp.where(lane == 98, held_loss - high - middle, block).astype(bf16)

    small = split_loss(d_block[core] + d_other[...])
    copies = []
    for k, peer in enumerate(flat):
        if k in (0, 4, 8, 12):
            core_copies[k // 4].wait()
        sent[peer[0], 0:64, :] = (
            packed[core, peer[0]].astype(f32) + other[peer[0]].astype(f32)
        ).astype(bf16)
        sent[peer[0], 64:80, :] = small
        copies += start([remote(sent.at[peer[0]], taken_w.at[wide], s3.at[k], r3.at[k], peer)])
    taken_w[wide, 0:64, :] = (packed[core, wide].astype(f32) + other[wide].astype(f32)).astype(bf16)
    taken_w[wide, 64:80, :] = small
    wait(copies)
    total = taken_w[0].astype(f32)
    for m in range(1, wide_size):
        total = total + taken_w[m].astype(f32)
    sum_z[0:64, :] = total[0:64].astype(bf16)
    sum_z[64:80, :] = split_loss(total[64:80])
    copies = start(
        [
            remote(sum_z, taken_z.at[depth], s5.at[k], r5.at[k], peer)
            for k, peer in enumerate(deep)
        ]
    )
    taken_z[depth] = sum_z[...]
    wait(copies)
    total = taken_z[0].astype(f32)
    for m in range(1, depth_size):
        total = total + taken_z[m].astype(f32)
    square[...] = jnp.broadcast_to(whole_sum(total[0:64] * total[0:64]), square.shape)
    copies = []
    for k, peer in enumerate(flat + [(wide, narrow)]):
        for other_core, device in enumerate((narrow, across)):
            if k < wide_size - 1 or other_core:
                at = 2 * k + other_core
                copies += start(
                    [remote(square, squares.at[core, wide], s8.at[at], r8.at[at], (peer[0], device))]
                )
    d_final[...] = total[64:80]
    d_copies = start([remote(d_final, d_partner, s7, r7, partner)])
    squares[core, wide] = square[...]
    other_grads[0:64, :] = total[0:64]

    wait(d_copies)
    highest = lax.Precision.HIGHEST
    first = jnp.where(core == 0, d_final[...], d_partner[...])
    second = jnp.where(core == 0, d_partner[...], d_final[...])
    for side, values in ((0, first), (1, second)):
        at = slice(32 * side, 32 * side + 32)
        d_all[0:16, at] = values[:, 0:32]
        d_all[16:32, at] = values[:, 32:64]
        d_all[32:40, at] = values[0:8, 64:96]
    d_total = d_all[...]
    grad = x
    grad[0:16, :] = other_grads[pl.ds(pl.multiple_of(depth * 16, 16), 16), :]
    grad[16:32, :] = jnp.zeros((16, 128), f32)
    grad[16:24, 0:kinds] = dot(ea[0:8, 64:128], d_total, 1, 1, highest)
    grad[24:32, 0:64] = dot(ea[0:8, 0:kinds], d_total, 1, 0, highest)
    extra = whole_sum(dot(gram[0:kinds, 0:kinds], d_total, 1, 0, highest) * d_total)
    extra += whole_sum(dot(d_total, gram[64:128, 64:128], 1, 0, highest) * d_total)
    loss_sum = jnp.sum(first[0:1, 96:99], axis=1, keepdims=True)
    line = lax.broadcasted_iota(jnp.int32, (32, 128), 0)
    lane = lax.broadcasted_iota(jnp.int32, (32, 128), 1)
    slow = (line < 8) | (line >= 24)
    fast = ((line >= 16) & (line < 24)) | ((line == 14) & (lane >= 64))
    rate = jnp.where(slow, rates[1], jnp.where(fast, rates[0], rates[3]))
    weight = state[0]
    first_part = beta_one * state[1]
    second_part = beta_two * state[2]
    wait(copies)
    total = squares[0, 0] + squares[1, 0]
    for m in range(1, wide_size):
        total = total + (squares[0, m] + squares[1, m])
    norm = jnp.sqrt(total[0:1, 0:1] + extra)
    clipped = grad[0:32, :] * jnp.minimum(1.0, clip_level / norm)
    moment = first_part + (1.0 - beta_one) * clipped
    speed = second_part + (1.0 - beta_two) * clipped * clipped
    ratio = (
        moment
        / (1.0 - beta_one**step_count)
        / (jnp.sqrt(speed / (1.0 - beta_two**step_count)) + adam_eps)
    )
    out[0:32, :] = weight - rate * (ratio + decay_rate * weight)
    out[32:64, :] = moment
    out[64:96, :] = speed
    line = lax.broadcasted_iota(jnp.int32, (8, 128), 0)
    out[96:104, :] = jnp.where(line == 0, loss_sum, jnp.where(line == 1, count, norm))


def place_kernel(stepped, *outs):
    for at in range(3):
        outs[at][...] = stepped[96 + at : 97 + at, 0:1]
    for kind in range(3):
        emb, ab, outer, tri, mix, dist, gain = outs[3 + 7 * kind : 10 + 7 * kind]
        base = 32 * kind
        outer[...] = stepped[base : base + 8, :]
        for m in range(5):
            tri[:, 128 * m : 128 * m + 128] = stepped[base + 8 + m : base + 9 + m, :]
        mix[...] = stepped[base + 13 : base + 14, :]
        dist[...] = stepped[base + 14 : base + 15, 0:64]
        gain[...] = stepped[base + 14 : base + 15, 64:66]
        emb[...] = stepped[base + 16 : base + 24, 0:vocab]
        ab[...] = stepped[base + 24 : base + 32, 0:64]


def shape(*dims, dtype=f32):
    return jax.ShapeDtypeStruct(dims, dtype)


in_vmem = pl.BlockSpec(memory_space=pltpu.VMEM)


def step_call(*args):
    def sems(*dims):
        return [pltpu.SemaphoreType.DMA(dims), pltpu.SemaphoreType.DMA(dims)]

    def one():
        return [pltpu.SemaphoreType.DMA, pltpu.SemaphoreType.DMA]

    full = VMEM((table, 128), f32)
    mine = VMEM((own, 128), f32)
    block = VMEM((16, 128), f32)
    return pl.pallas_call(
        step_kernel,
        out_shape=shape(104, 128),
        in_specs=[pl.BlockSpec(memory_space=pl.ANY)] * len(args),
        out_specs=in_vmem,
        scratch_shapes=[
            *[VMEM(arg.shape, arg.dtype) for arg in args],
            pltpu.SMEM(args[0].shape, jnp.int32), pltpu.SMEM(args[1].shape, jnp.int32),
            pltpu.SemaphoreType.DMA((26,)),
            pltpu.SemaphoreType.REGULAR,
            VMEM((3, 32, 128), f32),
            VMEM((depth_size, 16, 128), f32),
            VMEM((depth_size, 48, 128), bf16),
            VMEM((depth_size, 48, 128), bf16),
            block,
            VMEM((2, depth_size, 16, 128), bf16),
            VMEM((96, 128), bf16),
            VMEM((2, wide_size, 96, 128), bf16),
            VMEM((32 * pitch, 128), f32), VMEM((1024, 128), f32),
            VMEM((128, 128), f32),
            VMEM((16, length), f32),
            VMEM((pitch * 48, 128), f32),
            VMEM((own, 128), f32),
            full, full,
            VMEM((table, 128), bf16),
            full, full,
            VMEM((kinds * kinds, 128), f32),
            VMEM((own, bins), f32),
            mine, mine, mine, mine,
            VMEM((own, 128), bf16),
            mine, mine, mine, mine, mine, mine,
            full,
            VMEM((table, 256), bf16),
            VMEM((own, 384), bf16),
            VMEM((pitch * 48, 128), f32),
            VMEM((32 * pitch, 128), f32), VMEM((1024, 128), f32),
            VMEM((2, wide_size, 64, 128), bf16),
            VMEM((wide_size, 64, 128), bf16),
            VMEM((wide_size, 80, 128), bf16),
            VMEM((wide_size, 80, 128), bf16),
            VMEM((80, 128), bf16),
            VMEM((depth_size, 80, 128), bf16),
            VMEM((2, 16, 128), f32),
            block, block, block,
            VMEM((kinds, 64), f32),
            VMEM((1, 128), f32),
            VMEM((2, wide_size, 1, 128), f32),
            *sems(depth_size), *sems(wide_size), *one(), *sems(wide_size),
            *sems(4), *one(), *sems(wide_size), *sems(depth_size), *one(), *sems(2 * wide_size),
        ],
        compiler_params=pltpu.CompilerParams(
            collective_id=0, has_side_effects=True, vmem_limit_bytes=LIMIT
        ),
        name="pair_step",
    )(*args)


def local(tokens, segments, targets, *state):
    state = list(state)
    for at in (0, 6, 7, 13, 14, 20):
        state[at] = state[at].T
    stepped = step_call(tokens, segments, targets, *state)
    shapes = [shape(*w.shape) for w in state[0:7]]
    outs = pl.pallas_call(
        place_kernel,
        out_shape=[shape(1, 1)] * 3 + shapes * 3,
        in_specs=[in_vmem],
        out_specs=[in_vmem] * 24,
        name="place_outputs",
    )(stepped)
    outs = [value.reshape(()) for value in outs[0:3]] + list(outs[3:])
    for at in (3, 9, 10, 16, 17, 23):
        outs[at] = outs[at].T
    return tuple(outs)


def solution(mesh):
    both = ("wide", "narrow")
    whole = (P(None, both), P(both, None), P(both, None), P(both, None), P(both, None), P(both, None), P(None, both))
    return jax.shard_map(
        local,
        mesh=mesh,
        in_specs=(P(), P(), P(None, "wide", "narrow")) + whole * 3,
        out_specs=(P(), P(), P()) + whole * 3,
        check_vma=False,
    )
```

```python
import functools

import jax
import jax.numpy as jnp
from jax import lax
from jax.experimental import pallas as pl
from jax.experimental.pallas import tpu as pltpu
from jax.sharding import PartitionSpec as P

norm_eps = 1e-05
clip_level = 0.001
beta_one = 0.9
beta_two = 0.999
adam_eps = 1e-10
decay_rate = 0.01
step_count = 10.0
rates = (0.5, 0.016, 0.016, 0.044, 0.044, 0.044, 0.5)

f32 = jnp.float32
bf16 = jnp.bfloat16
MESH = pl.DeviceIdType.MESH
VMEM = pltpu.VMEM
LIMIT = 56 * 1024 * 1024

vocab = 33
kinds = 40
groups = 34
table = groups * kinds
pitch = 40
side_by_side = 4
columns_by = 4
own_rows = 12
own = own_rows * kinds
parts_all = groups + own_rows
bins = 64
wide_size = 16
depth_size = 4
length = 384


def dot(a, b, axis_a, axis_b, precision=None):
    return lax.dot_general(
        a, b, (((axis_a,), (axis_b,)), ((), ())), precision=precision, preferred_element_type=f32
    )


def rounded(values):
    return values.astype(bf16).astype(f32)


def halves(values):
    high = values.astype(bf16)
    return high, (values - high.astype(f32)).astype(bf16)


def whole_sum(values):
    return jnp.sum(jnp.sum(values, axis=0, keepdims=True), axis=1, keepdims=True)


flat_steps = [(dy, dx) for dy in (2, 1, 3, 0) for dx in (2, 1, 3, 0) if (dy, dx) != (0, 0)]
deep_steps = (2, 1, 3)


def step_kernel(*refs):
    inputs, refs = refs[:24], refs[24:]
    out, refs = refs[0], refs[1:]
    held, refs = refs[:24], refs[24:]
    (
        tok_s, seg_s, loaded, ready,
        state, tstage, stage, taken, ea, targets_in, source, gathered,
        outer_rows, other_rows, gram, tg, u, z, xhat, rstd, zn, sb, pb, tb,
        hist, many, wa, xi, ri, zr, sr, pr, x, dx, dz1, gr, gb,
        dpt, dpr, du, outer_grads, other_grads, packed, other, sent, taken_w, sum_z, taken_z,
        d_block, d_other, d_final, d_partner, d_all, square, squares,
        sz, rz, sg, rg, st, rt, sc, rc, s1, r1, s2, r2, s3, r3, s5, r5, s7, r7, s8, r8,
    ) = refs
    wide = lax.axis_index("wide")
    narrow = lax.axis_index("narrow")
    depth = narrow // 2
    core = lax.rem(narrow, 2)
    row, column = wide // 4, lax.rem(wide, 4)

    def at_step(dy, dx):
        return lax.rem(row + dy, 4) * 4 + lax.rem(column + dx, 4)

    across = depth * 2 + 1 - core
    partner = (wide, across)
    deep = [(wide, lax.rem(depth + k, depth_size) * 2 + core) for k in deep_steps]
    flat = [(at_step(dy, dx), narrow) for dy, dx in flat_steps]
    flat_from = [at_step(4 - dy, 4 - dx) for dy, dx in flat_steps]

    barrier = pltpu.get_barrier_semaphore()
    line_x = [(at_step(0, d), narrow) for d in deep_steps]
    line_y = [(at_step(d, 0), narrow) for d in deep_steps]
    for peer in line_y + line_x + deep + [partner]:
        pl.semaphore_signal(barrier, inc=1, device_id=peer, device_id_type=MESH)

    loads = [pltpu.make_async_copy(a, b, loaded.at[k]) for k, (a, b) in enumerate(zip(inputs, held))]
    loads.append(pltpu.make_async_copy(inputs[0], tok_s, loaded.at[24]))
    loads.append(pltpu.make_async_copy(inputs[1], seg_s, loaded.at[25]))
    urgent, later = loads[2:10], loads[0:2] + loads[10:]
    for load in urgent + later:
        load.start()

    def remote(source_ref, target_ref, send, receive, peer):
        return pltpu.make_async_remote_copy(
            src_ref=source_ref, dst_ref=target_ref, send_sem=send, recv_sem=receive,
            device_id=peer, device_id_type=MESH,
        )

    def start(copies):
        for copy in copies:
            copy.start()
        return copies

    def wait(copies):
        for copy in copies:
            copy.wait()

    state[...] = jnp.zeros_like(state)
    tstage[...] = jnp.zeros_like(tstage)
    stage[...] = jnp.zeros_like(stage)
    ea[...] = jnp.zeros_like(ea)
    for load in urgent:
        load.wait()
    tok_v, seg_v, tgt = held[0:3]
    def keep(kind):
        emb, ab, outer, tri, mix, dist, gain = held[3 + 7 * kind : 10 + 7 * kind]
        state[kind, 0:8, :] = outer[...]
        for m in range(5):
            state[kind, 8 + m : 9 + m, :] = tri[:, 128 * m : 128 * m + 128]
        state[kind, 13:14, :] = mix[...]
        state[kind, 14:15, 0:64] = dist[...]
        state[kind, 14:15, 64:66] = gain[...]
        state[kind, 16:24, 0:vocab] = emb[...]
        state[kind, 24:32, 0:64] = ab[...]

    keep(0)
    ea[0:8, 0:vocab] = rounded(held[3][...])
    ea[0:8, 64:128] = rounded(held[4][...])
    low = state[0, 0:16, :].astype(bf16)
    low_ea = ea[...].astype(bf16)
    for m in range(depth_size):
        tstage[m, :, 0:48] = tgt[m, 0:16, :].astype(f32)
        tstage[m, :, 64:112] = tgt[m, 8:24, :].astype(f32)
        stage[m, 0:16, :] = low
        stage[m, 16:32, :] = tstage[m].astype(bf16)
        stage[m, 32:48, :] = low_ea
    pl.semaphore_wait(barrier, 1 + len(deep) + len(line_x) + len(line_y))
    for peer in line_x:
        pl.semaphore_signal(ready, inc=1, device_id=peer, device_id_type=MESH)

    copies = start(
        [
            remote(stage.at[peer[1] // 2], taken.at[depth], sz.at[k], rz.at[k], peer)
            for k, peer in enumerate(deep)
        ]
    )
    taken[depth] = stage[depth]
    for load in later:
        load.wait()
    keep(1)
    keep(2)
    wait(copies)
    for m in range(depth_size):
        source[16 * m : 16 * m + 16, :] = taken[m, 0:16, :]
        targets_in[core, m] = taken[m, 16:32, :]
    source[64:96, :] = jnp.concatenate(
        [taken[m, 32:48, :].astype(f32)[0:8] for m in range(depth_size)], axis=0
    ).astype(bf16)
    pl.semaphore_wait(ready, len(line_x))
    wide_copies = start(
        [
            remote(source, gathered.at[core, wide], sg.at[k], rg.at[k], peer)
            for k, peer in enumerate(flat)
        ]
    )
    moved = start([remote(targets_in.at[core], targets_in.at[core], st, rt, partner)])
    gathered[core, wide] = source[...]
    core_copies = start(
        [remote(source, gathered.at[core, wide], sc.at[0], rc.at[0], partner)]
    )

    tb[table:, :] = jnp.zeros((kinds * kinds - table, 128), f32)
    gb[vocab * kinds :, :] = jnp.zeros((table - vocab * kinds, 128), f32)
    du[pitch * parts_all :, :] = jnp.zeros((pitch * (48 - parts_all), 128), f32)
    other_grads[pl.ds(7, 128, stride=8), :] = jnp.zeros((128, 128), f32)
    wait(moved)
    for m in range(depth_size):
        for side in range(2):
            piece = targets_in[side, m].astype(f32)
            piece = jnp.where(core == 0, piece[:, 0:48], piece[:, 64:112])
            at = 48 * (2 * m + side)
            tg[:, at : at + 48] = piece
    row0 = wide * 24 + core * own_rows
    tok_row = tok_v[pl.ds(depth, 1), :]
    seg_row = seg_v[pl.ds(depth, 1), :]
    hot = (lax.broadcasted_iota(jnp.int32, (kinds, length), 0) == tok_row).astype(f32).astype(bf16)
    bin_of = lax.broadcasted_iota(jnp.int32, (bins, length), 0).astype(f32)
    line = lax.broadcasted_iota(jnp.int32, (48, kinds), 0)
    kind_of = line
    for i in range(own_rows):
        kind_of = jnp.where(line == groups + i, tok_s[depth, row0 + i], kind_of)
    pick = (kind_of == lax.broadcasted_iota(jnp.int32, (48, kinds), 1)).astype(f32).astype(bf16)
    for i in range(own_rows):
        here = slice(kinds * i, kinds * i + kinds)
        wanted = jnp.where(seg_row == seg_s[depth, row0 + i], tg[pl.ds(4 * core + i, 1), :], -1.0)
        counts = dot(hot, (bin_of == wanted).astype(f32).astype(bf16), 1, 1)
        hist[here, :] = counts
        many[here, :] = jnp.broadcast_to(jnp.sum(counts, -1, keepdims=True), (kinds, 128))
    count = jnp.zeros((4, 1), f32)
    for s in range(6):
        members = jnp.sum((seg_v[...] == s).astype(f32), axis=1, keepdims=True)
        count = count + members * members
    count = jnp.sum(count, axis=0, keepdims=True)

    def unpack(side, m):
        for deep_at in range(depth_size):
            values = gathered[side, m, 16 * deep_at : 16 * deep_at + 16, :].astype(f32)
            at = pitch * (2 * m + deep_at // 2) + 8 * (2 * (deep_at % 2) + side)
            outer_rows[pl.ds(pl.multiple_of(at, 8), 8), :] = values[0:8]
            at = 8 * (8 * m + 2 * deep_at + side)
            other_rows[pl.ds(pl.multiple_of(at, 8), 8), :] = values[8:16]

    unpack(core, wide)
    for k in reversed(range(wide_size - 1)):
        wide_copies[k].wait_recv()
        slot = gathered.at[core, flat_from[k]]
        core_copies += start([remote(slot, slot, sc.at[k + 1], rc.at[k + 1], partner)])
        unpack(core, flat_from[k])
    for copy, m in zip(core_copies, [wide] + flat_from[::-1]):
        copy.wait_recv()
        unpack(1 - core, m)
    for copy in wide_copies + core_copies:
        copy.wait_send()
    shards = gathered[:, :, 64:96, :].reshape(2 * wide_size * 32, 128)
    gram[...] = dot(shards, shards, 0, 0)
    a = dot(pick, gram[0:kinds, 64:96].astype(bf16), 1, 0).astype(bf16)
    b = gram[0:kinds, 96:128].astype(bf16)
    w_outer = jnp.concatenate(
        [outer_rows[pl.ds(q, 32, stride=pitch), :] for q in range(32)], axis=1
    ).astype(bf16)
    w_own = jnp.concatenate(
        [other_rows[pl.ds(m, 128, stride=8), :] for m in (0, 1, 4)], axis=1
    ).astype(bf16)
    w_other = jnp.concatenate(
        [other_rows[pl.ds(m, 128, stride=8), :] for m in (2, 3)], axis=1
    ).astype(bf16)
    w_mix = other_rows[pl.ds(5, 128, stride=8), :].astype(bf16)
    tail_t = other_rows[pl.ds(6, 128, stride=8), :].T
    dist_t = tail_t[0:bins, :].astype(bf16)
    gain_in = tail_t[64:65, :]
    gain_mid = tail_t[65:66, :]

    u_q = rounded(dot(a, w_outer, 1, 0))
    for q in range(32):
        u[pl.ds(q, 48, stride=pitch), :] = u_q[:, 128 * q : 128 * q + 128]
    u_all = jnp.concatenate([u[pitch * t : pitch * t + 32, :] for t in range(parts_all)], axis=1).astype(bf16)
    z_cat = dot(b, u_all, 1, 0)
    pairs = jnp.concatenate([z_cat[:, 128 * t : 128 * t + 128] for t in range(groups)], axis=0)
    own_pairs = jnp.concatenate(
        [z_cat[:, 128 * t : 128 * t + 128] for t in range(groups, parts_all)], axis=0
    )
    z[...] = own_pairs

    center = pairs - jnp.mean(pairs, -1, keepdims=True)
    inverse = lax.rsqrt(jnp.mean(center * center, -1, keepdims=True) + norm_eps)
    scaled = center * inverse
    normed = (scaled * gain_in).astype(bf16)
    xhat[...] = scaled
    rstd[...] = jnp.broadcast_to(inverse, scaled.shape)
    zn[...] = normed
    projected = dot(normed, w_other, 1, 0)
    gate = jax.nn.sigmoid(projected[:, 0:128])
    value = projected[:, 128:256]
    sb[...] = gate
    pb[...] = value
    tb[0:table, :] = rounded(gate * value)

    center = own_pairs - jnp.mean(own_pairs, -1, keepdims=True)
    inverse = lax.rsqrt(jnp.mean(center * center, -1, keepdims=True) + norm_eps)
    scaled = center * inverse
    xi[...] = scaled
    ri[...] = jnp.broadcast_to(inverse, scaled.shape)
    normed = (scaled * gain_in).astype(bf16)
    zr[...] = normed
    projected = dot(normed, w_own, 1, 0)
    gate = jax.nn.sigmoid(projected[:, 0:128])
    value = projected[:, 128:256]
    sr[...] = gate
    pr[...] = value
    wa[...] = many[...] * rounded(gate * value)
    gate_out = jax.nn.sigmoid(projected[:, 256:384])

    for group in range(own_rows // columns_by):
        mine = range(columns_by * group, columns_by * group + columns_by)

        def product(v, sums, mine=mine):
            edge = tb[pl.ds(v, kinds, stride=kinds), :]
            return tuple(
                total + wa[pl.ds(kinds * i + v, 1), :] * edge for total, i in zip(sums, mine)
            )

        sums = lax.fori_loop(
            0, vocab, product, (jnp.zeros((kinds, 128), f32),) * columns_by, unroll=33
        )
        for total, i in zip(sums, mine):
            x[kinds * i : kinds * i + kinds, :] = total

    values = x[...]
    center = values - jnp.mean(values, -1, keepdims=True)
    inverse = lax.rsqrt(jnp.mean(center * center, -1, keepdims=True) + norm_eps)
    scaled = center * inverse
    mixed = (scaled * gain_mid).astype(bf16)
    branch = dot(mixed, w_mix, 1, 0)
    update = (z[...] + gate_out * branch).astype(bf16)
    logits = dot(update, dist_t, 1, 1)
    top = jnp.max(logits, -1, keepdims=True)
    powers = jnp.exp(logits - top)
    power_sum = jnp.sum(powers, -1, keepdims=True)
    counts = hist[...]
    loss = jnp.sum(many[:, 0:1] * (jnp.log(power_sum) + top), axis=0, keepdims=True) - whole_sum(
        counts * logits
    )
    grad_logits = ((many[:, 0:bins] * (powers / power_sum) - counts) / count).astype(bf16)
    grad_dist_t = dot(grad_logits, update, 0, 0)
    grad_update = dot(grad_logits, dist_t, 1, 0)
    grad_branch = (grad_update * gate_out).astype(bf16)
    dz1[...] = grad_update
    dpr[:, 256:384] = (grad_update * branch * gate_out * (1.0 - gate_out)).astype(bf16)
    grad_mix = dot(mixed, grad_branch, 0, 0)
    grad_mixed = dot(grad_branch, w_mix, 1, 1)
    grad_gain_mid = jnp.sum(grad_mixed * scaled, axis=0, keepdims=True)
    grad_hat = grad_mixed * gain_mid
    dx[...] = inverse * (
        grad_hat
        - jnp.mean(grad_hat, -1, keepdims=True)
        - scaled * jnp.mean(grad_hat * scaled, -1, keepdims=True)
    )

    for group in range(own_rows // side_by_side):
        mine = range(side_by_side * group, side_by_side * group + side_by_side)

        def edges(t, sums, mine=mine, group=group):
            at = pl.ds(pl.multiple_of(t * kinds, 8), kinds)
            edge = tb[at, :]
            right = gb[at, :] if group else jnp.zeros((kinds, 128), f32)
            news = []
            for total, i in zip(sums, mine):
                grad = dx[pl.ds(kinds * i + t, 1), :]
                news.append(total + grad * edge)
                right = right + grad * wa[kinds * i : kinds * i + kinds, :]
            gb[at, :] = right
            return tuple(news)

        sums = lax.fori_loop(
            0, vocab, edges, (jnp.zeros((kinds, 128), f32),) * side_by_side, unroll=33
        )
        for total, i in zip(sums, mine):
            here = slice(kinds * i, kinds * i + kinds)
            gr[here, :] = total * many[here, :]

    def norm_back(grad_normed, scaled, inverse):
        grad_hat = grad_normed * gain_in
        return inverse * (
            grad_hat
            - jnp.mean(grad_hat, -1, keepdims=True)
            - scaled * jnp.mean(grad_hat * scaled, -1, keepdims=True)
        )

    gate = sr[...]
    grad = gr[...] * gate
    dpr[:, 0:128] = (grad * pr[...] * (1.0 - gate)).astype(bf16)
    dpr[:, 128:256] = grad.astype(bf16)
    grad_normed = dot(dpr[...], w_own, 1, 1)
    scaled = xi[...]
    grad_gain_in = jnp.sum(grad_normed * scaled, axis=0, keepdims=True)
    grad_own = dz1[...] + norm_back(grad_normed, scaled, ri[...])
    grad_tri_own = dot(zr[...], dpr[...], 0, 0)

    gate = sb[...]
    grad = gb[...] * gate
    dpt[:, 0:128] = (grad * pb[...] * (1.0 - gate)).astype(bf16)
    dpt[:, 128:256] = grad.astype(bf16)
    grad_normed = dot(dpt[...], w_other, 1, 1)
    scaled = xhat[...]
    grad_table = norm_back(grad_normed, scaled, rstd[...])
    grad_gain_in = grad_gain_in + jnp.sum(grad_normed * scaled, axis=0, keepdims=True)
    grad_tri_other = dot(zn[...], dpt[...], 0, 0)

    for at, m in enumerate((0, 1, 4)):
        other_grads[pl.ds(m, 128, stride=8), :] = grad_tri_own[:, 128 * at : 128 * at + 128]
    for at, m in enumerate((2, 3)):
        other_grads[pl.ds(m, 128, stride=8), :] = grad_tri_other[:, 128 * at : 128 * at + 128]
    other_grads[pl.ds(5, 128, stride=8), :] = grad_mix
    other_grads[pl.ds(6, 128, stride=8), :] = jnp.concatenate(
        [grad_dist_t, grad_gain_in, grad_gain_mid, jnp.zeros((62, 128), f32)], axis=0
    ).T

    blocks = [grad_table[kinds * t : kinds * t + kinds, :] for t in range(groups)]
    blocks += [grad_own[kinds * i : kinds * i + kinds, :] for i in range(own_rows)]
    dz_all = jnp.concatenate(blocks, axis=1).astype(bf16)
    grad_u = dot(b, dz_all, 0, 0)
    for t in range(parts_all):
        du[pitch * t : pitch * t + 32, :] = grad_u[:, 128 * t : 128 * t + 128]
    grad_b = dot(dz_all, u_all, 1, 1)
    du_all = jnp.concatenate(
        [du[pl.ds(q, 48, stride=pitch), :] for q in range(32)], axis=1
    ).astype(bf16)
    grad_outer = dot(a, du_all, 0, 0)
    grad_a_high, grad_a_low = halves(dot(du_all, w_outer, 1, 1))
    grad_a = dot(pick, grad_a_high, 0, 0) + dot(pick, grad_a_low, 0, 0)

    for q in range(32):
        outer_grads[pl.ds(q, 32, stride=pitch), :] = grad_outer[:, 128 * q : 128 * q + 128]
    for side in range(2):
        for m in range(wide_size):
            for deep_at in range(depth_size):
                at = pitch * (2 * m + deep_at // 2) + 8 * (2 * (deep_at % 2) + side)
                values = [outer_grads[at : at + 8, :]]
                at = 8 * (8 * m + 2 * deep_at + side)
                values.append(other_grads[at : at + 8, :])
                packed[side, m, 16 * deep_at : 16 * deep_at + 16, :] = jnp.concatenate(values, axis=0).astype(bf16)
    d_block[...] = jnp.zeros_like(d_block)
    for side, values in ((0, grad_a), (1, grad_b)):
        d_block[side, :, 0:32] = values[0:16]
        d_block[side, :, 32:64] = values[16:32]
        d_block[side, 0:8, 64:96] = values[32:40]
    d_block[0, 0:1, 96:97] = loss

    d_copies = start([remote(d_block.at[1 - core], d_other, s2, r2, partner)])
    core_copies = []
    for k, dy in enumerate((2, 1, 3, 0)):
        at = pl.ds(lax.rem(row + dy, 4) * 4, 4)
        core_copies += start(
            [remote(packed.at[1 - core, at], other.at[at], s1.at[k], r1.at[k], partner)]
        )
    wait(d_copies)
    lane = lax.broadcasted_iota(jnp.int32, (16, 128), 1)

    def split_loss(block):
        held_loss = jnp.sum(jnp.where((lane >= 96) & (lane < 99), block, 0.0), axis=1, keepdims=True)
        high = rounded(held_loss)
        middle = rounded(held_loss - high)
        block = jnp.where(lane == 96, high, block)
        block = jnp.where(lane == 97, middle, block)
        return jnp.where(lane == 98, held_loss - high - middle, block).astype(bf16)

    small = split_loss(d_block[core] + d_other[...])
    copies = []
    for k, peer in enumerate(flat):
        if k in (0, 4, 8, 12):
            core_copies[k // 4].wait()
        sent[peer[0], 0:64, :] = (
            packed[core, peer[0]].astype(f32) + other[peer[0]].astype(f32)
        ).astype(bf16)
        sent[peer[0], 64:80, :] = small
        copies += start([remote(sent.at[peer[0]], taken_w.at[wide], s3.at[k], r3.at[k], peer)])
    taken_w[wide, 0:64, :] = (packed[core, wide].astype(f32) + other[wide].astype(f32)).astype(bf16)
    taken_w[wide, 64:80, :] = small
    wait(copies)
    total = taken_w[0].astype(f32)
    for m in range(1, wide_size):
        total = total + taken_w[m].astype(f32)
    sum_z[0:64, :] = total[0:64].astype(bf16)
    sum_z[64:80, :] = split_loss(total[64:80])
    copies = start(
        [
            remote(sum_z, taken_z.at[depth], s5.at[k], r5.at[k], peer)
            for k, peer in enumerate(deep)
        ]
    )
    taken_z[depth] = sum_z[...]
    wait(copies)
    total = taken_z[0].astype(f32)
    for m in range(1, depth_size):
        total = total + taken_z[m].astype(f32)
    square[...] = jnp.broadcast_to(whole_sum(total[0:64] * total[0:64]), square.shape)
    copies = []
    for k, peer in enumerate(flat + [(wide, narrow)]):
        for other_core, device in enumerate((narrow, across)):
            if k < wide_size - 1 or other_core:
                at = 2 * k + other_core
                copies += start(
                    [remote(square, squares.at[core, wide], s8.at[at], r8.at[at], (peer[0], device))]
                )
    d_final[...] = total[64:80]
    d_copies = start([remote(d_final, d_partner, s7, r7, partner)])
    squares[core, wide] = square[...]
    other_grads[0:64, :] = total[0:64]

    wait(d_copies)
    highest = lax.Precision.HIGHEST
    first = jnp.where(core == 0, d_final[...], d_partner[...])
    second = jnp.where(core == 0, d_partner[...], d_final[...])
    for side, values in ((0, first), (1, second)):
        at = slice(32 * side, 32 * side + 32)
        d_all[0:16, at] = values[:, 0:32]
        d_all[16:32, at] = values[:, 32:64]
        d_all[32:40, at] = values[0:8, 64:96]
    d_total = d_all[...]
    grad = x
    grad[0:16, :] = other_grads[pl.ds(pl.multiple_of(depth * 16, 16), 16), :]
    grad[16:32, :] = jnp.zeros((16, 128), f32)
    grad[16:24, 0:kinds] = dot(ea[0:8, 64:128], d_total, 1, 1, highest)
    grad[24:32, 0:64] = dot(ea[0:8, 0:kinds], d_total, 1, 0, highest)
    extra = whole_sum(dot(gram[0:kinds, 0:kinds], d_total, 1, 0, highest) * d_total)
    extra += whole_sum(dot(d_total, gram[64:128, 64:128], 1, 0, highest) * d_total)
    loss_sum = jnp.sum(first[0:1, 96:99], axis=1, keepdims=True)
    line = lax.broadcasted_iota(jnp.int32, (32, 128), 0)
    lane = lax.broadcasted_iota(jnp.int32, (32, 128), 1)
    slow = (line < 8) | (line >= 24)
    fast = ((line >= 16) & (line < 24)) | ((line == 14) & (lane >= 64))
    rate = jnp.where(slow, rates[1], jnp.where(fast, rates[0], rates[3]))
    weight = state[0]
    first_part = beta_one * state[1]
    second_part = beta_two * state[2]
    wait(copies)
    total = squares[0, 0] + squares[1, 0]
    for m in range(1, wide_size):
        total = total + (squares[0, m] + squares[1, m])
    norm = jnp.sqrt(total[0:1, 0:1] + extra)
    clipped = grad[0:32, :] * jnp.minimum(1.0, clip_level / norm)
    moment = first_part + (1.0 - beta_one) * clipped
    speed = second_part + (1.0 - beta_two) * clipped * clipped
    ratio = (
        moment
        / (1.0 - beta_one**step_count)
        / (jnp.sqrt(speed / (1.0 - beta_two**step_count)) + adam_eps)
    )
    out[0:32, :] = weight - rate * (ratio + decay_rate * weight)
    out[32:64, :] = moment
    out[64:96, :] = speed
    line = lax.broadcasted_iota(jnp.int32, (8, 128), 0)
    out[96:104, :] = jnp.where(line == 0, loss_sum, jnp.where(line == 1, count, norm))


def place_kernel(stepped, *outs):
    for at in range(3):
        outs[at][...] = stepped[96 + at : 97 + at, 0:1]
    for kind in range(3):
        emb, ab, outer, tri, mix, dist, gain = outs[3 + 7 * kind : 10 + 7 * kind]
        base = 32 * kind
        outer[...] = stepped[base : base + 8, :]
        for m in range(5):
            tri[:, 128 * m : 128 * m + 128] = stepped[base + 8 + m : base + 9 + m, :]
        mix[...] = stepped[base + 13 : base + 14, :]
        dist[...] = stepped[base + 14 : base + 15, 0:64]
        gain[...] = stepped[base + 14 : base + 15, 64:66]
        emb[...] = stepped[base + 16 : base + 24, 0:vocab]
        ab[...] = stepped[base + 24 : base + 32, 0:64]


def shape(*dims, dtype=f32):
    return jax.ShapeDtypeStruct(dims, dtype)


in_vmem = pl.BlockSpec(memory_space=pltpu.VMEM)


def step_call(*args):
    def sems(*dims):
        return [pltpu.SemaphoreType.DMA(dims), pltpu.SemaphoreType.DMA(dims)]

    def one():
        return [pltpu.SemaphoreType.DMA, pltpu.SemaphoreType.DMA]

    full = VMEM((table, 128), f32)
    mine = VMEM((own, 128), f32)
    block = VMEM((16, 128), f32)
    return pl.pallas_call(
        step_kernel,
        out_shape=shape(104, 128),
        in_specs=[pl.BlockSpec(memory_space=pl.ANY)] * len(args),
        out_specs=in_vmem,
        scratch_shapes=[
            *[VMEM(arg.shape, arg.dtype) for arg in args],
            pltpu.SMEM(args[0].shape, jnp.int32), pltpu.SMEM(args[1].shape, jnp.int32),
            pltpu.SemaphoreType.DMA((26,)),
            pltpu.SemaphoreType.REGULAR,
            VMEM((3, 32, 128), f32),
            VMEM((depth_size, 16, 128), f32),
            VMEM((depth_size, 48, 128), bf16),
            VMEM((depth_size, 48, 128), bf16),
            block,
            VMEM((2, depth_size, 16, 128), bf16),
            VMEM((96, 128), bf16),
            VMEM((2, wide_size, 96, 128), bf16),
            VMEM((32 * pitch, 128), f32), VMEM((1024, 128), f32),
            VMEM((128, 128), f32),
            VMEM((16, length), f32),
            VMEM((pitch * 48, 128), f32),
            VMEM((own, 128), f32),
            full, full,
            VMEM((table, 128), bf16),
            full, full,
            VMEM((kinds * kinds, 128), f32),
            VMEM((own, bins), f32),
            mine, mine, mine, mine,
            VMEM((own, 128), bf16),
            mine, mine, mine, mine, mine, mine,
            full,
            VMEM((table, 256), bf16),
            VMEM((own, 384), bf16),
            VMEM((pitch * 48, 128), f32),
            VMEM((32 * pitch, 128), f32), VMEM((1024, 128), f32),
            VMEM((2, wide_size, 64, 128), bf16),
            VMEM((wide_size, 64, 128), bf16),
            VMEM((wide_size, 80, 128), bf16),
            VMEM((wide_size, 80, 128), bf16),
            VMEM((80, 128), bf16),
            VMEM((depth_size, 80, 128), bf16),
            VMEM((2, 16, 128), f32),
            block, block, block,
            VMEM((kinds, 64), f32),
            VMEM((1, 128), f32),
            VMEM((2, wide_size, 1, 128), f32),
            *sems(depth_size), *sems(wide_size), *one(), *sems(wide_size),
            *sems(4), *one(), *sems(wide_size), *sems(depth_size), *one(), *sems(2 * wide_size),
        ],
        compiler_params=pltpu.CompilerParams(
            collective_id=0, has_side_effects=True, vmem_limit_bytes=LIMIT
        ),
        name="pair_step",
    )(*args)


def local(tokens, segments, targets, *state):
    state = list(state)
    for at in (0, 6, 7, 13, 14, 20):
        state[at] = state[at].T
    stepped = step_call(tokens, segments, targets, *state)
    shapes = [shape(*w.shape) for w in state[0:7]]
    outs = pl.pallas_call(
        place_kernel,
        out_shape=[shape(1, 1)] * 3 + shapes * 3,
        in_specs=[in_vmem],
        out_specs=[in_vmem] * 24,
        name="place_outputs",
    )(stepped)
    outs = [value.reshape(()) for value in outs[0:3]] + list(outs[3:])
    for at in (3, 9, 10, 16, 17, 23):
        outs[at] = outs[at].T
    return tuple(outs)


def solution(mesh):
    both = ("wide", "narrow")
    whole = (P(None, both), P(both, None), P(both, None), P(both, None), P(both, None), P(both, None), P(None, both))
    return jax.shard_map(
        local,
        mesh=mesh,
        in_specs=(P(), P(), P(None, "wide", "narrow")) + whole * 3,
        out_specs=(P(), P(), P()) + whole * 3,
        check_vma=False,
    )
```
